32 devices in a mesh: seq: 2 (over y), ctx: 4 (over x, core), fsdp: 4 (over z).
Axes of the slice: x: 2, y: 2, z: 4, core: 2. Of those that a mesh axis runs over, the one named last changes fastest.
Arguments:
- tokens: bfloat16 [8, 1024, 2048], P(('seq', 'fsdp'), 'ctx'), may hold values from -6 to 6
- block_place: int32 [8, 8], P(('seq', 'fsdp')), may hold values from 0 to 7, each once within a row
- w_qkv: bfloat16 [2048, 6144], P('fsdp'), may hold values from -0.125 to 0.125
- b_qkv: bfloat16 [6144], P('fsdp'), may hold values from -2 to 2
- w_o_t: bfloat16 [2048, 2048], P('fsdp'), may hold values from -0.5 to 0.5
- b_o: bfloat16 [2048], P('fsdp'), may hold values from -2 to 2
- w_up: bfloat16 [2048, 8192], P('fsdp'), may hold values from -0.125 to 0.125
- b_up: bfloat16 [8192], P('fsdp'), may hold values from -2 to 2
- w_down_t: bfloat16 [2048, 8192], P('fsdp'), may hold values from -0.0625 to 0.0625
- b_down: bfloat16 [2048], P('fsdp'), may hold values from -2 to 2
- norm1_gain: bfloat16 [2048], P('fsdp'), may hold values from 0.5 to 1.5
- norm1_shift: bfloat16 [2048], P('fsdp'), may hold values from -2 to 2
- norm2_gain: bfloat16 [2048], P('fsdp'), may hold values from 0.5 to 1.5
- norm2_shift: bfloat16 [2048], P('fsdp'), may hold values from -2 to 2
- cotangent: bfloat16 [8, 1024, 2048], P(('seq', 'fsdp'), 'ctx'), may hold values from -6 to 6
Outputs:
- output: bfloat16 [8, 1024, 2048], P(('seq', 'fsdp'), 'ctx')
- input_grad: bfloat16 [8, 1024, 2048], P(('seq', 'fsdp'), 'ctx')
- grad_w_qkv: float32 [2048, 6144], P('fsdp')
- grad_b_qkv: float32 [6144], P('fsdp')
- grad_w_o_t: float32 [2048, 2048], P('fsdp')
- grad_b_o: float32 [2048], P('fsdp')
- grad_w_up: float32 [2048, 8192], P('fsdp')
- grad_b_up: float32 [8192], P('fsdp')
- grad_w_down_t: float32 [2048, 8192], P('fsdp')
- grad_b_down: float32 [2048], P('fsdp')
- grad_norm1_gain: float32 [2048], P('fsdp')
- grad_norm1_shift: float32 [2048], P('fsdp')
- grad_norm2_gain: float32 [2048], P('fsdp')
- grad_norm2_shift: float32 [2048], P('fsdp')
The draws below stay inside these ranges and needn't reach their ends.
Inputs may be any that keep to these rules, and one draw needn't show every extreme that they name: Each row of block_place lists every block place of the sequence once.
All inputs are finite; a program needn't handle non-finite values.
Results may differ from the reference program's by a relative error of at most 0.015.
Values may be sent and summed in bfloat16 or wider, within the bound.
A program may use at most 704 MiB of HBM per device.

```python
import math
import jax
import jax.numpy as jnp
from jax import lax

D = 2048
HEADS = 8
HEAD = 256
ROT = 64
FF = 8192
BLK = 128
PLACES = 8
LEN = 1024
SEQS = 8


def steps_of(stream_key, dims, pieces, smallest, high):
    loudness = 1.0
    for position, blocks in pieces:
        draws = jax.random.uniform(jax.random.fold_in(jax.random.fold_in(stream_key, 6), position), (blocks,), jnp.float32, smallest / len(pieces), high / len(pieces))
        loudness = loudness * jnp.repeat(jnp.exp(draws), dims[position] // blocks).reshape((-1,) + (1,) * (len(dims) - 1 - position))
    return loudness


def gaussian(stream_key, extent, scale, limit, split=(), kind=jnp.bfloat16):
    values = jax.random.normal(stream_key, extent, jnp.float32) * scale
    if len(split) > 0:
        values = steps_of(stream_key, extent, split, -0.22, 0.18) * values
    return jnp.clip(values, min=-limit, max=limit).astype(kind)


def setup_inputs(seed: int = 0) -> dict:
    splits = jax.random.split(jax.random.key(seed), 16)
    return {
        "tokens": gaussian(splits[0], (SEQS, LEN, D), 1.0, 6.0, ((0, 8), (1, 4))),
        "block_place": jax.vmap(lambda own: jax.random.permutation(own, PLACES))(jax.random.split(splits[1], SEQS)).reshape((SEQS, PLACES)).astype(jnp.int32),
        "w_qkv": gaussian(splits[2], (D, 3 * D), D ** -0.5, 0.125, ((0, 4),)),
        "b_qkv": gaussian(splits[3], (3 * D,), 0.3, 2.0, ((0, 4),)),
        "w_o_t": gaussian(splits[4], (D, D), (D // 16) ** -0.5, 0.5, ((0, 4),)),
        "b_o": gaussian(splits[5], (D,), 0.3, 2.0, ((0, 4),)),
        "w_up": gaussian(splits[6], (D, FF), D ** -0.5, 0.125, ((0, 4),)),
        "b_up": gaussian(splits[7], (FF,), 0.3, 2.0, ((0, 4),)),
        "w_down_t": gaussian(splits[8], (D, FF), FF ** -0.5, 0.0625, ((0, 4),)),
        "b_down": gaussian(splits[9], (D,), 0.3, 2.0, ((0, 4),)),
        "norm1_gain": jnp.clip(1.0 + 0.1 * jax.random.normal(splits[10], (D,), jnp.float32), 0.5, 1.5).astype(jnp.bfloat16),
        "norm1_shift": gaussian(splits[11], (D,), 0.3, 2.0, ((0, 4),)),
        "norm2_gain": jnp.clip(1.0 + 0.1 * jax.random.normal(splits[12], (D,), jnp.float32), 0.5, 1.5).astype(jnp.bfloat16),
        "norm2_shift": gaussian(splits[13], (D,), 0.3, 2.0, ((0, 4),)),
        "cotangent": gaussian(splits[14], (SEQS, LEN, D), 1.0, 6.0, ((0, 8), (1, 4))),
    }


@jax.custom_vjp
def low(v):
    return lax.optimization_barrier(v.astype(jnp.bfloat16)).astype(jnp.float32)

@jax.custom_vjp
def low_back(v):
    return v

def low_keep(v):
    return (low(v), None)

def low_pass(kept, grad):
    return (grad,)

def back_keep(v):
    return (v, None)

def back_low(kept, grad):
    return (low(grad),)
low.defvjp(low_keep, low_pass)
low_back.defvjp(back_keep, back_low)
HIGH = lax.Precision.HIGHEST
eps = 1e-05

def norm_rows(values, gain_row, offset):
    middle = lax.optimization_barrier(jnp.mean(values, -1, keepdims=True))
    centred = values - middle
    spread = lax.optimization_barrier(jnp.mean(centred * centred, -1, keepdims=True))
    return centred * lax.rsqrt(spread + eps) * gain_row + offset

def angles(positions):
    freqs = 10000.0 ** (-(jnp.arange(ROT // 2, dtype=jnp.float32) * 2.0 / ROT))
    turned = positions.astype(jnp.float32)[:, None] * freqs[None, :]
    turned = jnp.concatenate([turned, turned], -1)
    return (jnp.cos(turned), jnp.sin(turned))

def rotate(values, cosine, sine):
    half = ROT // 2
    rotary = values[..., :ROT]
    swapped = jnp.concatenate([-rotary[..., half:], rotary[..., :half]], -1)
    moved = rotary * cosine[:, None, :] + swapped * sine[:, None, :]
    return jnp.concatenate([moved, values[..., ROT:]], -1)

def layer(inputs, w_qkv, b_qkv, w_o_t, b_o, w_up, b_up, w_down_t, b_down, gain_one, shift_one, gain_two, shift_two, positions):
    length = inputs.shape[0]
    cosine, sine = angles(positions)
    normed_one = low(norm_rows(inputs, gain_one, shift_one))
    normed_two = low(norm_rows(inputs, gain_two, shift_two))
    projected = low_back(jnp.dot(normed_one, w_qkv, precision=HIGH) + b_qkv)
    queries = low(rotate(projected[:, :D].reshape(length, HEADS, HEAD), cosine, sine))
    all_keys = low(rotate(projected[:, D:2 * D].reshape(length, HEADS, HEAD), cosine, sine))
    all_values = low(projected[:, 2 * D:].reshape(length, HEADS, HEAD))
    scaling = 1.0 / math.sqrt(HEAD)
    query_rows = math.gcd(length, 512)

    def attend(pair):
        query_part, query_pos = pair
        scores = jnp.einsum('thd,shd->hts', query_part, all_keys, precision=HIGH) * scaling
        scores = low_back(scores)
        allowed = query_pos[:, None] >= positions[None, :]
        scores = jnp.where(allowed[None], scores, -1e+30)
        weights = jax.nn.softmax(scores, -1)
        return jnp.einsum('hts,shd->thd', low(weights), all_values, precision=HIGH)
    blocks = lax.map(jax.checkpoint(attend), (queries.reshape(length // query_rows, query_rows, HEADS, HEAD), positions.reshape(length // query_rows, query_rows)))
    attended = low(low_back(blocks.reshape(length, D)))
    hidden = low_back(jnp.dot(normed_two, w_up, precision=HIGH) + b_up)
    gelu_out = low(jax.nn.gelu(hidden, approximate=False))
    return inputs + jnp.dot(attended, w_o_t.T, precision=HIGH) + b_o + jnp.dot(gelu_out, w_down_t.T, precision=HIGH) + b_down

def reference(tokens, block_place, w_qkv, b_qkv, w_o_t, b_o, w_up, b_up, w_down_t, b_down, norm1_gain, norm1_shift, norm2_gain, norm2_shift, cotangent):
    params = tuple((a.astype(jnp.float32) for a in (w_qkv, b_qkv, w_o_t, b_o, w_up, b_up, w_down_t, b_down, norm1_gain, norm1_shift, norm2_gain, norm2_shift)))

    def one_seq(totals, item):
        seq_in, places, seq_grad = item
        positions = (places[:, None] * BLK + jnp.arange(BLK, dtype=jnp.int32)[None, :]).reshape(-1).astype(jnp.int32)

        def forward(inputs, *weights):
            return layer(inputs, *weights, positions)
        result, pull = jax.vjp(forward, seq_in.astype(jnp.float32), *params)
        grads = pull(seq_grad.astype(jnp.float32))
        new_totals = tuple((t + g for t, g in zip(totals, grads[1:])))
        return (new_totals, (result.astype(jnp.bfloat16), grads[0].astype(jnp.bfloat16)))
    zeros = tuple((jnp.zeros(p.shape, jnp.float32) for p in params))
    sums, (outputs, input_grads) = lax.scan(one_seq, zeros, (tokens, block_place, cotangent))
    return (outputs, input_grads, sums[0], sums[1], sums[2], sums[3], sums[4], sums[5], sums[6], sums[7], sums[8], sums[9], sums[10], sums[11])
```

```python
import math

import jax
import jax.numpy as jnp
from jax import lax
from jax.sharding import PartitionSpec as P

HEADS = 8
HEAD = 256
ROT = 64
BLK = 128
EPS = 1e-05
PLANE = ("seq", "ctx")
LOW = jnp.bfloat16
WIDE = jnp.float32


def dot_nn(left, right):
    return lax.dot_general(left, right, (((1,), (0,)), ((), ())), preferred_element_type=WIDE)


def dot_nt(left, right):
    return lax.dot_general(left, right, (((1,), (1,)), ((), ())), preferred_element_type=WIDE)


def dot_tn(left, right):
    return lax.dot_general(left, right, (((0,), (0,)), ((), ())), preferred_element_type=WIDE)


def batch_nn(left, right):
    return lax.dot_general(left, right, (((2,), (1,)), ((0,), (0,))), preferred_element_type=WIDE)


def batch_nt(left, right):
    return lax.dot_general(left, right, (((2,), (2,)), ((0,), (0,))), preferred_element_type=WIDE)


def batch_tn(left, right):
    return lax.dot_general(left, right, (((1,), (1,)), ((0,), (0,))), preferred_element_type=WIDE)


def standardise(values):
    middle = jnp.mean(values, -1, keepdims=True)
    centred = values - middle
    spread = jnp.mean(centred * centred, -1, keepdims=True)
    scale = lax.rsqrt(spread + EPS)
    return centred * scale, scale


def angles(positions):
    freqs = 10000.0 ** (-(jnp.arange(ROT // 2, dtype=WIDE) * 2.0 / ROT))
    turned = positions.astype(WIDE)[:, None] * freqs[None, :]
    return jnp.cos(turned), jnp.sin(turned)


def turn(values, cosine, sine):
    half = ROT // 2
    one, two, rest = values[..., :half], values[..., half:ROT], values[..., ROT:]
    return jnp.concatenate([one * cosine - two * sine, two * cosine + one * sine, rest], -1)


def gelu_pair(hidden):
    bell = 0.5 * (1.0 + lax.erf(hidden * (1.0 / math.sqrt(2.0))))
    slope = bell + hidden * jnp.exp(-0.5 * hidden * hidden) * (1.0 / math.sqrt(2.0 * math.pi))
    return hidden * bell, slope


def body(tokens, block_place, w_qkv, b_qkv, w_o_t, b_o, w_up, b_up, w_down_t, b_down,
         norm1_gain, norm1_shift, norm2_gain, norm2_shift, cotangent):
    seqs, ctxs, shards = lax.axis_size("seq"), lax.axis_size("ctx"), lax.axis_size("fsdp")
    peers = seqs * ctxs
    place = lax.axis_index("seq") * ctxs + lax.axis_index("ctx")
    own, width = tokens.shape[1:]
    hidden_all = w_up.shape[1]
    length = own * ctxs
    share = max(1, peers // HEADS)
    heads = max(1, HEADS // peers)
    own_seqs = seqs // share
    group = place // share
    first_seq = (place % share) * own_seqs
    cols = heads * HEAD
    hid = hidden_all // peers

    x_own = tokens[0].astype(WIDE)
    dy_own = cotangent[0]
    both = lax.all_gather(jnp.stack([tokens[0], dy_own]), PLANE, axis=0, tiled=False)
    x_all = both[:, 0].reshape(seqs * length, width)
    dy_all = both[:, 1].reshape(seqs * length, width)
    places = lax.all_gather(block_place[0], "seq", axis=0, tiled=False)

    small = (b_qkv, b_o, b_up, b_down, norm1_gain, norm1_shift, norm2_gain, norm2_shift)
    packed = lax.all_gather(jnp.concatenate(small), "fsdp", axis=0, tiled=False)
    unpacked, start = [], 0
    for part in small:
        size = part.shape[0]
        unpacked.append(packed[:, start : start + size].reshape(-1).astype(WIDE))
        start += size
    bias_qkv, bias_o, bias_up, bias_down, gain1, shift1, gain2, shift2 = unpacked

    def head_cols(values, kinds):
        rows = values.shape[0]
        split = values.reshape(rows, kinds, HEADS * HEAD)
        return lax.dynamic_slice_in_dim(split, group * cols, cols, 2).reshape(rows, kinds * cols)

    def hid_cols(values):
        return lax.dynamic_slice_in_dim(values, place * hid, hid, 1)

    own_cols = jnp.concatenate([head_cols(w_qkv, 3), head_cols(w_o_t, 1), hid_cols(w_up), hid_cols(w_down_t)], 1)
    weights = lax.all_gather(own_cols, "fsdp", axis=0, tiled=True)
    cut = 4 * cols
    m_qkv, m_o, m_up, m_down = weights[:, : 3 * cols], weights[:, 3 * cols : cut], weights[:, cut : cut + hid], weights[:, cut + hid :]
    own_bias_qkv = head_cols(bias_qkv[None], 3)
    own_bias_up = hid_cols(bias_up[None])

    x_hat, _ = standardise(x_all.astype(WIDE))
    a1 = (x_hat * gain1 + shift1).astype(LOW)
    a2 = (x_hat * gain2 + shift2).astype(LOW)

    rows = own_seqs * length
    a1_seq = lax.dynamic_slice_in_dim(a1, first_seq * length, rows, 0)
    dy_seq = lax.dynamic_slice_in_dim(dy_all, first_seq * length, rows, 0)
    positions = (places[:, :, None] * BLK + jnp.arange(BLK, dtype=jnp.int32)).reshape(seqs, length)
    positions = lax.dynamic_slice_in_dim(positions, first_seq, own_seqs, 0)
    cosine, sine = angles(positions.reshape(-1))
    cosine, sine = cosine[:, None], sine[:, None]
    qkv = dot_nn(a1_seq, m_qkv) + own_bias_qkv

    def to_heads(values):
        return values.reshape(own_seqs, length, heads, HEAD).transpose(0, 2, 1, 3).reshape(own_seqs * heads, length, HEAD)

    def from_heads(values):
        return values.reshape(own_seqs, heads, length, HEAD).transpose(0, 2, 1, 3).reshape(rows, cols)

    def turned(values):
        return turn(values.reshape(rows, heads, HEAD), cosine, sine).reshape(rows, cols)

    def turned_back(values):
        return turn(values.reshape(rows, heads, HEAD), cosine, -sine).reshape(rows, cols)

    q = to_heads(turned(qkv[:, :cols]).astype(LOW))
    k = to_heads(turned(qkv[:, cols : 2 * cols]).astype(LOW))
    v = to_heads(qkv[:, 2 * cols :].astype(LOW))
    scaling = 1.0 / math.sqrt(HEAD)
    kept = (positions[:, :, None] >= positions[:, None, :])[:, None]
    kept = jnp.broadcast_to(kept, (own_seqs, heads, length, length)).reshape(own_seqs * heads, length, length)
    scores = jnp.where(kept, batch_nt(q, k) * scaling, -1e30)
    expo = jnp.exp(scores - jnp.max(scores, -1, keepdims=True))
    p = expo / jnp.sum(expo, -1, keepdims=True)
    p_low = p.astype(LOW)
    attn = from_heads(batch_nn(p_low, v).astype(LOW))
    d_attn = to_heads(dot_nn(dy_seq, m_o).astype(LOW))
    dp = batch_nt(d_attn, v)
    ds = jnp.where(kept, p * (dp - jnp.sum(p * dp, -1, keepdims=True)), 0.0).astype(LOW)
    dq = from_heads(batch_nn(ds, k) * scaling)
    dk = from_heads(batch_tn(ds, q) * scaling)
    dv = from_heads(batch_tn(p_low, d_attn))
    d_qkv = jnp.concatenate([turned_back(dq), turned_back(dk), dv], 1).astype(LOW)

    g, slope = gelu_pair(dot_nn(a2, m_up) + own_bias_up)
    g = g.astype(LOW)
    d_h = (dot_nn(dy_all, m_down) * slope).astype(LOW)

    def onto(values, part):
        return lax.dynamic_update_slice_in_dim(values, lax.dynamic_slice_in_dim(values, first_seq * length, rows, 0) + part, first_seq * length, 0)

    out_part = onto(dot_nt(g, m_down), dot_nt(attn, m_o))
    u_part = onto(dot_nt(d_h, m_up) * gain2, dot_nt(d_qkv, m_qkv) * gain1)
    out_sum = lax.psum_scatter(out_part.astype(LOW), PLANE, scatter_dimension=0, tiled=True).astype(WIDE)
    u_sum = lax.psum_scatter(u_part.astype(LOW), PLANE, scatter_dimension=0, tiled=True).astype(WIDE)
    output = (x_own + out_sum + bias_o + bias_down).astype(LOW)[None]
    hat_own, scale_own = standardise(x_own)
    d_x = scale_own * (u_sum - jnp.mean(u_sum, -1, keepdims=True) - hat_own * jnp.mean(u_sum * hat_own, -1, keepdims=True))
    input_grad = (dy_own.astype(WIDE) + d_x).astype(LOW)[None]

    g_qkv = dot_tn(a1_seq, d_qkv)
    g_o = dot_tn(dy_seq, attn)
    g_up = dot_tn(a2, d_h)
    g_down = dot_tn(dy_all, g)
    gb_qkv = jnp.sum(d_qkv, 0, dtype=WIDE)
    gb_up = jnp.sum(d_h, 0, dtype=WIDE)
    wide_qkv, wide_up = m_qkv.astype(WIDE), m_up.astype(WIDE)
    d_gain1 = jnp.sum(wide_qkv * (g_qkv - shift1[:, None] * gb_qkv), 1) / gain1
    d_gain2 = jnp.sum(wide_up * (g_up - shift2[:, None] * gb_up), 1) / gain2
    d_shift1 = jnp.sum(wide_qkv * gb_qkv, 1)
    d_shift2 = jnp.sum(wide_up * gb_up, 1)
    full_qkv = lax.dynamic_update_slice(jnp.zeros((3, HEADS * HEAD), WIDE), gb_qkv.reshape(3, cols), (0, group * cols)).reshape(-1)
    full_up = lax.dynamic_update_slice(jnp.zeros((hidden_all,), WIDE), gb_up, (place * hid,))
    sums = lax.psum((full_qkv, jnp.sum(dy_own, 0, dtype=WIDE), full_up, d_gain1, d_shift1, d_gain2, d_shift2), PLANE + ("fsdp",))
    mine = lax.axis_index("fsdp")

    def own_share(values):
        size = values.shape[0] // shards
        return lax.dynamic_slice_in_dim(values, mine * size, size, 0)

    sums = [own_share(s) for s in sums]
    grads = jnp.concatenate([g_qkv, g_o, g_up, g_down], 1).astype(LOW)
    reduced = lax.psum_scatter(grads, "fsdp", scatter_dimension=0, tiled=True)
    gathered = lax.all_gather(reduced, PLANE, axis=0, tiled=False)
    rows_own = reduced.shape[0]

    def spread_heads(values, kinds):
        values = values.astype(WIDE).reshape(peers // share, share, rows_own, kinds, cols).sum(1)
        return values.transpose(1, 2, 0, 3).reshape(rows_own, kinds * HEADS * HEAD)

    def spread_hid(values):
        return values.transpose(1, 0, 2).reshape(rows_own, hidden_all).astype(WIDE)

    return (
        output,
        input_grad,
        spread_heads(gathered[:, :, : 3 * cols], 3),
        sums[0],
        spread_heads(gathered[:, :, 3 * cols : cut], 1),
        sums[1],
        spread_hid(gathered[:, :, cut : cut + hid]),
        sums[2],
        spread_hid(gathered[:, :, cut + hid :]),
        sums[1],
        sums[3],
        sums[4],
        sums[5],
        sums[6],
    )


def solution(mesh):
    tok = P(("seq", "fsdp"), "ctx", None)
    mat, vec = P("fsdp", None), P("fsdp")
    params = (mat, vec, mat, vec, mat, vec, mat, vec, vec, vec, vec, vec)
    in_specs = (tok, P(("seq", "fsdp"), None)) + params + (tok,)
    return jax.shard_map(body, mesh=mesh, in_specs=in_specs, out_specs=(tok, tok) + params, check_vma=False)
```

```python
import math

import jax
import jax.numpy as jnp
from jax import lax
from jax.experimental import pallas as pl
from jax.experimental.pallas import tpu as pltpu
from jax.sharding import PartitionSpec as P

HEADS = 8
HEAD = 256
ROT = 64
BLK = 128
EPS = 1e-05
PLANE = ("seq", "ctx")
LOW = jnp.bfloat16
WIDE = jnp.float32


def dot_nn(left, right):
    return lax.dot_general(left, right, (((1,), (0,)), ((), ())), preferred_element_type=WIDE)


def dot_nt(left, right):
    return lax.dot_general(left, right, (((1,), (1,)), ((), ())), preferred_element_type=WIDE)


def dot_tn(left, right):
    return lax.dot_general(left, right, (((0,), (0,)), ((), ())), preferred_element_type=WIDE)


def batch_nn(left, right):
    return lax.dot_general(left, right, (((2,), (1,)), ((0,), (0,))), preferred_element_type=WIDE)


def batch_nt(left, right):
    return lax.dot_general(left, right, (((2,), (2,)), ((0,), (0,))), preferred_element_type=WIDE)


def batch_tn(left, right):
    return lax.dot_general(left, right, (((1,), (1,)), ((0,), (0,))), preferred_element_type=WIDE)


def standardise(values):
    middle = jnp.mean(values, -1, keepdims=True)
    centred = values - middle
    spread = jnp.mean(centred * centred, -1, keepdims=True)
    scale = lax.rsqrt(spread + EPS)
    return centred * scale, scale


def angles(positions):
    freqs = 10000.0 ** (-(jnp.arange(ROT // 2, dtype=WIDE) * 2.0 / ROT))
    turned = positions.astype(WIDE)[:, None] * freqs[None, :]
    return jnp.cos(turned), jnp.sin(turned)


def turn(values, cosine, sine):
    half = ROT // 2
    one, two, rest = values[..., :half], values[..., half:ROT], values[..., ROT:]
    return jnp.concatenate([one * cosine - two * sine, two * cosine + one * sine, rest], -1)


def gelu_pair(hidden):
    bell = 0.5 * (1.0 + lax.erf(hidden * (1.0 / math.sqrt(2.0))))
    slope = bell + hidden * jnp.exp(-0.5 * hidden * hidden) * (1.0 / math.sqrt(2.0 * math.pi))
    return hidden * bell, slope


def body(tokens, block_place, w_qkv, b_qkv, w_o_t, b_o, w_up, b_up, w_down_t, b_down,
         norm1_gain, norm1_shift, norm2_gain, norm2_shift, cotangent):
    seqs, ctxs, shards = lax.axis_size("seq"), lax.axis_size("ctx"), lax.axis_size("fsdp")
    peers = seqs * ctxs
    place = lax.axis_index("seq") * ctxs + lax.axis_index("ctx")
    own, width = tokens.shape[1:]
    hidden_all = w_up.shape[1]
    length = own * ctxs
    share = max(1, peers // HEADS)
    heads = max(1, HEADS // peers)
    own_seqs = seqs // share
    group = place // share
    first_seq = (place % share) * own_seqs
    cols = heads * HEAD
    hid = hidden_all // peers

    x_own = tokens[0].astype(WIDE)
    dy_own = cotangent[0]
    both = lax.all_gather(jnp.stack([tokens[0], dy_own]), PLANE, axis=0, tiled=False)
    x_all = both[:, 0].reshape(seqs * length, width)
    dy_all = both[:, 1].reshape(seqs * length, width)
    places = lax.all_gather(block_place[0], "seq", axis=0, tiled=False)

    small = (b_qkv, b_o, b_up, b_down, norm1_gain, norm1_shift, norm2_gain, norm2_shift)
    packed = lax.all_gather(jnp.concatenate(small), "fsdp", axis=0, tiled=False)
    unpacked, start = [], 0
    for part in small:
        size = part.shape[0]
        unpacked.append(packed[:, start : start + size].reshape(-1).astype(WIDE))
        start += size
    bias_qkv, bias_o, bias_up, bias_down, gain1, shift1, gain2, shift2 = unpacked

    def head_cols(values, kinds):
        rows = values.shape[0]
        split = values.reshape(rows, kinds, HEADS * HEAD)
        return lax.dynamic_slice_in_dim(split, group * cols, cols, 2).reshape(rows, kinds * cols)

    def hid_cols(values):
        return lax.dynamic_slice_in_dim(values, place * hid, hid, 1)

    own_cols = jnp.concatenate([head_cols(w_qkv, 3), head_cols(w_o_t, 1), hid_cols(w_up), hid_cols(w_down_t)], 1)
    weights = lax.all_gather(own_cols, "fsdp", axis=0, tiled=True)
    cut = 4 * cols
    m_qkv, m_o, m_up, m_down = weights[:, : 3 * cols], weights[:, 3 * cols : cut], weights[:, cut : cut + hid], weights[:, cut + hid :]
    own_bias_qkv = head_cols(bias_qkv[None], 3)
    own_bias_up = hid_cols(bias_up[None])

    x_hat, _ = standardise(x_all.astype(WIDE))
    a1 = (x_hat * gain1 + shift1).astype(LOW)
    a2 = (x_hat * gain2 + shift2).astype(LOW)

    rows = own_seqs * length
    a1_seq = lax.dynamic_slice_in_dim(a1, first_seq * length, rows, 0)
    dy_seq = lax.dynamic_slice_in_dim(dy_all, first_seq * length, rows, 0)
    positions = (places[:, :, None] * BLK + jnp.arange(BLK, dtype=jnp.int32)).reshape(seqs, length)
    positions = lax.dynamic_slice_in_dim(positions, first_seq, own_seqs, 0)
    cosine, sine = angles(positions.reshape(-1))
    cosine, sine = cosine[:, None], sine[:, None]
    qkv = dot_nn(a1_seq, m_qkv) + own_bias_qkv

    def to_heads(values):
        return values.reshape(own_seqs, length, heads, HEAD).transpose(0, 2, 1, 3).reshape(own_seqs * heads, length, HEAD)

    def from_heads(values):
        return values.reshape(own_seqs, heads, length, HEAD).transpose(0, 2, 1, 3).reshape(rows, cols)

    def turned(values):
        return turn(values.reshape(rows, heads, HEAD), cosine, sine).reshape(rows, cols)

    def turned_back(values):
        return turn(values.reshape(rows, heads, HEAD), cosine, -sine).reshape(rows, cols)

    q = to_heads(turned(qkv[:, :cols]).astype(LOW))
    k = to_heads(turned(qkv[:, cols : 2 * cols]).astype(LOW))
    v = to_heads(qkv[:, 2 * cols :].astype(LOW))
    scaling = 1.0 / math.sqrt(HEAD)
    kept = (positions[:, :, None] >= positions[:, None, :])[:, None]
    kept = jnp.broadcast_to(kept, (own_seqs, heads, length, length)).reshape(own_seqs * heads, length, length)
    scores = jnp.where(kept, batch_nt(q, k) * scaling, -1e30)
    expo = jnp.exp(scores - jnp.max(scores, -1, keepdims=True))
    p = expo / jnp.sum(expo, -1, keepdims=True)
    p_low = p.astype(LOW)
    attn = from_heads(batch_nn(p_low, v).astype(LOW))
    d_attn = to_heads(dot_nn(dy_seq, m_o).astype(LOW))
    dp = batch_nt(d_attn, v)
    ds = jnp.where(kept, p * (dp - jnp.sum(p * dp, -1, keepdims=True)), 0.0).astype(LOW)
    dq = from_heads(batch_nn(ds, k) * scaling)
    dk = from_heads(batch_tn(ds, q) * scaling)
    dv = from_heads(batch_tn(p_low, d_attn))
    d_qkv = jnp.concatenate([turned_back(dq), turned_back(dk), dv], 1).astype(LOW)

    g, slope = gelu_pair(dot_nn(a2, m_up) + own_bias_up)
    g = g.astype(LOW)
    d_h = (dot_nn(dy_all, m_down) * slope).astype(LOW)

    def onto(values, part):
        return lax.dynamic_update_slice_in_dim(values, lax.dynamic_slice_in_dim(values, first_seq * length, rows, 0) + part, first_seq * length, 0)

    out_part = onto(dot_nt(g, m_down), dot_nt(attn, m_o))
    u_part = onto(dot_nt(d_h, m_up) * gain2, dot_nt(d_qkv, m_qkv) * gain1)
    out_sum = lax.psum_scatter(out_part.astype(LOW), PLANE, scatter_dimension=0, tiled=True).astype(WIDE)
    u_sum = lax.psum_scatter(u_part.astype(LOW), PLANE, scatter_dimension=0, tiled=True).astype(WIDE)
    output = (x_own + out_sum + bias_o + bias_down).astype(LOW)[None]
    hat_own, scale_own = standardise(x_own)
    d_x = scale_own * (u_sum - jnp.mean(u_sum, -1, keepdims=True) - hat_own * jnp.mean(u_sum * hat_own, -1, keepdims=True))
    input_grad = (dy_own.astype(WIDE) + d_x).astype(LOW)[None]

    g_qkv = dot_tn(a1_seq, d_qkv)
    g_o = dot_tn(dy_seq, attn)
    g_up = dot_tn(a2, d_h)
    g_down = dot_tn(dy_all, g)
    gb_qkv = jnp.sum(d_qkv, 0, dtype=WIDE)
    gb_up = jnp.sum(d_h, 0, dtype=WIDE)
    wide_qkv, wide_up = m_qkv.astype(WIDE), m_up.astype(WIDE)
    d_gain1 = jnp.sum(wide_qkv * (g_qkv - shift1[:, None] * gb_qkv), 1) / gain1
    d_gain2 = jnp.sum(wide_up * (g_up - shift2[:, None] * gb_up), 1) / gain2
    d_shift1 = jnp.sum(wide_qkv * gb_qkv, 1)
    d_shift2 = jnp.sum(wide_up * gb_up, 1)
    full_qkv = lax.dynamic_update_slice(jnp.zeros((3, HEADS * HEAD), WIDE), gb_qkv.reshape(3, cols), (0, group * cols)).reshape(-1)
    full_up = lax.dynamic_update_slice(jnp.zeros((hidden_all,), WIDE), gb_up, (place * hid,))
    sums = lax.psum((full_qkv, jnp.sum(dy_own, 0, dtype=WIDE), full_up, d_gain1, d_shift1, d_gain2, d_shift2), PLANE + ("fsdp",))
    mine = lax.axis_index("fsdp")

    def own_share(values):
        size = values.shape[0] // shards
        return lax.dynamic_slice_in_dim(values, mine * size, size, 0)

    sums = [own_share(s) for s in sums]
    grads = jnp.concatenate([g_qkv, g_o, g_up, g_down], 1).astype(LOW)
    reduced = lax.psum_scatter(grads, "fsdp", scatter_dimension=0, tiled=True)
    gathered = lax.all_gather(reduced, PLANE, axis=0, tiled=False)
    rows_own = reduced.shape[0]

    def spread_heads(values, kinds):
        values = values.astype(WIDE).reshape(peers // share, share, rows_own, kinds, cols).sum(1)
        return values.transpose(1, 2, 0, 3).reshape(rows_own, kinds * HEADS * HEAD)

    def spread_hid(values):
        return values.transpose(1, 0, 2).reshape(rows_own, hidden_all).astype(WIDE)

    return (
        output,
        input_grad,
        spread_heads(gathered[:, :, : 3 * cols], 3),
        sums[0],
        spread_heads(gathered[:, :, 3 * cols : cut], 1),
        sums[1],
        spread_hid(gathered[:, :, cut : cut + hid]),
        sums[2],
        spread_hid(gathered[:, :, cut + hid :]),
        sums[1],
        sums[3],
        sums[4],
        sums[5],
        sums[6],
    )


MESH = pl.DeviceIdType.MESH
PIECES = 12
ROWS = 512
COLS = 256
WIDTH = 2048
TOK = 2048
LENGTH = 1024
HOPS = 3
AG_SLOTS = 36
RS_START = 20
RING = 6
SCALING = 1.0 / math.sqrt(HEAD)


def fits(mesh):
    return dict(mesh.shape) == {"seq": 2, "ctx": 4, "fsdp": 4}


def at(index, size):
    return pl.ds(pl.multiple_of(index * size, size), size)


def layer_kernel(x_hbm, dy_hbm, w_qkv, w_o, w_up, w_down, table, pos_row, rows_in, bias_in, cols_in,
                 red_out, out_out, u_out, small_out, gb_out,
                 w_all, act, x_buf, dy_buf, g_ring, landing, red_buf, small, gb, dk_acc, dv_acc, tab, pos, rows, bias,
                 load_sem, own_sem, ag_send, ag_recv, rs_send, rs_recv, red_sem):
    y, c, z = lax.axis_index("seq"), lax.axis_index("ctx"), lax.axis_index("fsdp")
    place = y * 4 + c
    right, left = (y, c, jnp.minimum(z + 1, 3)), (y, c, jnp.maximum(z - 1, 0))

    barrier = pltpu.get_barrier_semaphore()

    @pl.when(z < 3)
    def _():
        pl.semaphore_signal(barrier, inc=1, device_id=right, device_id_type=MESH)

    @pl.when(z > 0)
    def _():
        pl.semaphore_signal(barrier, inc=1, device_id=left, device_id_type=MESH)

    def own_piece(i):
        if i < 3:
            source = w_qkv.at[:, at(i * 8 + place, COLS)]
        elif i == 3:
            source = w_o.at[:, at(place, COLS)]
        else:
            source = (w_up if i % 2 == 0 else w_down).at[:, at(place * 4 + (i - 4) // 2, COLS)]
        return pltpu.make_async_copy(source, w_all.at[i, at(z, ROWS)], own_sem.at[i])

    for i in range(PIECES):
        own_piece(i).start()
    loads = [
        pltpu.make_async_copy(x_hbm, x_buf, load_sem.at[0]),
        pltpu.make_async_copy(dy_hbm, dy_buf, load_sem.at[1]),
        pltpu.make_async_copy(table, tab, load_sem.at[2]),
        pltpu.make_async_copy(pos_row, pos, load_sem.at[3]),
        pltpu.make_async_copy(rows_in, rows, load_sem.at[4]),
        pltpu.make_async_copy(bias_in, bias, load_sem.at[5]),
        pltpu.make_async_copy(cols_in, small, load_sem.at[6]),
    ]
    for load in loads:
        load.start()
    for i in range(PIECES):
        own_piece(i).wait()
    pl.semaphore_wait(barrier, jnp.where((z > 0) & (z < 3), 2, 1))

    def ag_copy(way, piece, hop, shard):
        block = w_all.at[piece, at(shard, ROWS)]
        return pltpu.make_async_remote_copy(
            src_ref=block, dst_ref=block, send_sem=ag_send.at[way, piece, hop], recv_sem=ag_recv.at[way, piece, hop],
            device_id=right if way == 0 else left, device_id_type=MESH)

    def ag_service(slot):
        before = slot - 2

        def parts(s):
            return (s // 6) * 2 + s % 2, (s // 2) % 3

        old, old_hop = parts(jnp.maximum(before, 0))
        live = (before >= 0) & (before < AG_SLOTS)

        @pl.when(live & (z >= 1) & (z - 1 - old_hop >= 0))
        def _():
            ag_copy(0, old, old_hop, z - 1 - old_hop).wait_recv()

        @pl.when(live & (z <= 2) & (z + 1 + old_hop <= 3))
        def _():
            ag_copy(1, old, old_hop, z + 1 + old_hop).wait_recv()

        piece, hop = parts(jnp.minimum(slot, AG_SLOTS - 1))

        @pl.when((slot < AG_SLOTS) & (z <= 2) & (z - hop >= 0))
        def _():
            ag_copy(0, piece, hop, z - hop).start()

        @pl.when((slot < AG_SLOTS) & (z >= 1) & (z + hop <= 3))
        def _():
            ag_copy(1, piece, hop, z + hop).start()

        @pl.when(live & (z <= 2) & (z - old_hop >= 0))
        def _():
            ag_copy(0, old, old_hop, z - old_hop).wait_send()

        @pl.when(live & (z >= 1) & (z + old_hop <= 3))
        def _():
            ag_copy(1, old, old_hop, z + old_hop).wait_send()

    def rs_piece(n):
        return jnp.where(n < 4, 3 - n, n)

    def rs_copy(way, n, hop, shard):
        return pltpu.make_async_remote_copy(
            src_ref=g_ring.at[n % RING, at(shard, ROWS)], dst_ref=landing.at[way, n % 4, hop],
            send_sem=rs_send.at[way, n, hop], recv_sem=rs_recv.at[way, n, hop],
            device_id=right if way == 0 else left, device_id_type=MESH)

    def rs_add(way, n, hop, shard):
        rs_copy(way, n, hop, shard).wait_recv()
        block = g_ring.at[n % RING, at(shard, ROWS)]
        block[...] = (block[...].astype(WIDE) + landing[way, n % 4, hop].astype(WIDE)).astype(LOW)

    def red_copy(n):
        return pltpu.make_async_copy(red_buf.at[n % 4], red_out.at[rs_piece(n)], red_sem.at[n])

    def rs_service(slot):
        before = slot - 2

        def parts(s):
            return (s // 6) * 2 + s % 2, (s // 2) % 3

        old, old_hop = parts(jnp.clip(before, 0, AG_SLOTS - 1))
        live = (before >= 0) & (before < AG_SLOTS)

        @pl.when(live & (z >= 1) & (z - 1 <= old_hop))
        def _():
            rs_add(0, old, old_hop, z + 2 - old_hop)

        @pl.when(live & (z <= 2) & (2 - z <= old_hop))
        def _():
            rs_add(1, old, old_hop, z - 2 + old_hop)

        @pl.when(live & (z <= 2) & (z <= old_hop))
        def _():
            rs_copy(0, old, old_hop, z + 3 - old_hop).wait_send()

        @pl.when(live & (z >= 1) & (3 - z <= old_hop))
        def _():
            rs_copy(1, old, old_hop, z - 3 + old_hop).wait_send()

        piece, hop = parts(jnp.clip(slot, 0, AG_SLOTS - 1))
        sending = (slot >= 0) & (slot < AG_SLOTS)

        @pl.when(sending & (z <= 2) & (z <= hop))
        def _():
            rs_copy(0, piece, hop, z + 3 - hop).start()

        @pl.when(sending & (z >= 1) & (3 - z <= hop))
        def _():
            rs_copy(1, piece, hop, z - 3 + hop).start()

        @pl.when(live & (old_hop == 2))
        def _():
            @pl.when(old >= 4)
            def _():
                red_copy(old - 4).wait()

            red_buf[old % 4] = g_ring[old % RING, at(z, ROWS)]
            red_copy(old).start()

    def service(slot):
        if isinstance(slot, int):
            if slot < AG_SLOTS + 2:
                ag_service(jnp.int32(slot))
            if slot >= RS_START:
                rs_service(jnp.int32(slot - RS_START))
        else:
            ag_service(slot)
            rs_service(slot - RS_START)

    def loop(count, body, first=None):
        def step(i, carry):
            if first is not None:
                service(first + i)
            body(i)
            return carry

        lax.fori_loop(0, count, step, 0)

    def norm_tile(which):
        def run(i):
            def part(n, carry):
                block = at(i * 4 + n, 64)
                centred, scale = standardise_rows(x_buf[block, :].astype(WIDE))
                x_buf[block, :] = (centred * scale * rows[2 * which : 2 * which + 1, :] + rows[2 * which + 1 : 2 * which + 2, :]).astype(LOW)
                return carry

            lax.fori_loop(0, 4, part, 0)
        return run

    loads[0].wait()
    for load in loads[2:]:
        load.wait()
    loop(8, norm_tile(0), 0)

    lane = lax.broadcasted_iota(jnp.int32, (1, 128), 1)

    def turned(values, block, sign):
        entry = tab[block, :]
        cosine = jnp.where(lane < 32, entry, jnp.where(lane < 64, pltpu.roll(entry, 32, 1), 1.0))
        sine = jnp.where(lane < 32, -pltpu.roll(entry, 96, 1), jnp.where(lane < 64, entry, 0.0))
        low = values[:, :128]
        partner = jnp.where(lane < 32, pltpu.roll(low, 96, 1), pltpu.roll(low, 32, 1))
        return jnp.concatenate([low * cosine + partner * (sine * sign), values[:, 128:]], 1)

    def project(kind):
        def run(i):
            block = at(i, 512)
            made = dot_nn(x_buf[block, :], w_all[kind]) + bias[kind : kind + 1, :]
            if kind < 2:
                made = turned(made, block, 1.0)
            act[9 + kind, block, :] = made.astype(LOW)
        return run

    loop(4, project(0), 8)
    loop(4, project(1))
    loop(4, project(2), 12)
    loads[1].wait()

    def attend(i):
        seq = i // 4
        block, keys = at(i, 256), at(seq, LENGTH)

        @pl.when(i % 4 == 0)
        def _():
            dk_acc[...] = jnp.zeros_like(dk_acc)
            dv_acc[...] = jnp.zeros_like(dv_acc)

        q, k, v = act[9, block, :], act[10, keys, :], act[11, keys, :]
        kept = tab[block, 64:65] >= pos[pl.ds(seq, 1), :]
        scores = jnp.where(kept, dot_nt(q, k) * SCALING, -1e30)
        expo = jnp.exp(scores - jnp.max(scores, -1, keepdims=True))
        p = expo * (1.0 / jnp.sum(expo, -1, keepdims=True))
        p_low = p.astype(LOW)
        act[3, block, :] = dot_nn(p_low, v).astype(LOW)
        d_attn = dot_nn(dy_buf[block, :], w_all[3]).astype(LOW)
        dp = dot_nt(d_attn, v)
        ds = jnp.where(kept, p * (dp - jnp.sum(p * dp, -1, keepdims=True)), 0.0).astype(LOW)
        act[0, block, :] = turned(dot_nn(ds, k) * SCALING, block, -1.0).astype(LOW)
        dk_acc[...] += dot_tn(ds, q)
        dv_acc[...] += dot_tn(p_low, d_attn)

        @pl.when(i % 4 == 3)
        def _():
            act[1, keys, :] = turned(dk_acc[...] * SCALING, keys, -1.0).astype(LOW)
            act[2, keys, :] = dv_acc[...].astype(LOW)

    def attend_two(i):
        attend(2 * i)
        attend(2 * i + 1)

    loop(4, attend_two, 16)

    def gradient(piece, n, source):
        def run():
            if piece != 3 and (piece < 3 or piece % 2 == 0):
                gb[piece : piece + 1, :] = jnp.sum(act[piece].astype(WIDE), 0, keepdims=True)

            def part(s, carry):
                block = at(s, ROWS)
                made = dot_tn(source[:, block], act[piece])
                g_ring[n % RING, block, :] = made.astype(LOW)
                if piece < 3 or (piece != 3 and piece % 2 == 0):
                    mine = 0 if piece < 3 else 1
                    weight = w_all[piece, block, :].astype(WIDE)
                    sums = gb[piece : piece + 1, :]
                    gain = jnp.sum(weight * (made - small[block, mine : mine + 1] * sums), 1, keepdims=True)
                    shift = jnp.sum(weight * sums, 1, keepdims=True)
                    here = 8 + 2 * mine
                    old = small[block, :]
                    small[block, :] = old + jnp.where(lane == here, gain, 0.0) + jnp.where(lane == here + 1, shift, 0.0)
                return carry

            lax.fori_loop(0, 4, part, 0)
        return run

    gradient(3, 0, dy_buf)()
    gradient(2, 1, x_buf)()
    service(20)
    gradient(1, 2, x_buf)()
    service(21)
    gradient(0, 3, x_buf)()
    service(22)
    again = pltpu.make_async_copy(x_hbm, x_buf, load_sem.at[0])
    again.start()
    again.wait()
    service(23)
    loop(4, norm_tile(1), 24)
    loop(4, lambda i: norm_tile(1)(i + 4))

    def feed(part):
        up, down = 4 + 2 * part, 5 + 2 * part

        def run(i):
            block = at(i, 512)
            hidden = dot_nn(x_buf[block, :], w_all[up]) + bias[3 + part : 4 + part, :]
            d_gelu = dot_nn(dy_buf[block, :], w_all[down])
            made, slope = gelu_pair(hidden)
            act[down, block, :] = made.astype(LOW)
            act[up, block, :] = (d_gelu * slope).astype(LOW)
        return run

    slot = 28
    for part in range(4):
        if part == 3:
            loop(RS_START + 20 + 2 - slot, lambda i: None, slot)
            slot = RS_START + 20 + 2
        loop(2, feed(part), slot)
        loop(2, lambda i, part=part: feed(part)(i + 2))
        slot += 2
        gradient(4 + 2 * part, 4 + 2 * part, x_buf)()
        service(slot)
        gradient(5 + 2 * part, 5 + 2 * part, dy_buf)()
        service(slot + 1)
        slot += 2

    def finish(i):
        block, columns = at(i // 4, 512), at(i % 4, 512)

        def total(pieces):
            return sum(dot_nt(act[piece, block, :], w_all[piece, columns, :]) for piece in pieces)

        x_buf[block, columns] = total((3, 5, 7, 9, 11)).astype(LOW)
        first = total((0, 1, 2)) * rows[0:1, columns]
        dy_buf[block, columns] = (first + total((4, 6, 8, 10)) * rows[2:3, columns]).astype(LOW)

    last = RS_START + AG_SLOTS + 2
    loop(16, finish)
    loop(last - slot, lambda i: None, slot)
    ends = [
        pltpu.make_async_copy(x_buf, out_out, load_sem.at[0]),
        pltpu.make_async_copy(dy_buf, u_out, load_sem.at[1]),
        pltpu.make_async_copy(small, small_out, load_sem.at[2]),
        pltpu.make_async_copy(gb, gb_out, load_sem.at[3]),
    ]
    for end in ends:
        end.start()
    for end in ends:
        end.wait()
    for n in range(8, 12):
        red_copy(n).wait()


def standardise_rows(values):
    middle = jnp.mean(values, -1, keepdims=True)
    centred = values - middle
    spread = jnp.mean(centred * centred, -1, keepdims=True)
    return centred, lax.rsqrt(spread + EPS)


def layer_call(*operands):
    anywhere = pl.BlockSpec(memory_space=pltpu.HBM)
    shape = jax.ShapeDtypeStruct
    dma = pltpu.SemaphoreType.DMA
    return pl.pallas_call(
        layer_kernel,
        out_shape=(
            shape((PIECES, ROWS, COLS), LOW),
            shape((TOK, WIDTH), LOW),
            shape((TOK, WIDTH), LOW),
            shape((WIDTH, 128), WIDE),
            shape((16, COLS), WIDE),
        ),
        in_specs=[anywhere] * len(operands),
        out_specs=[anywhere] * 5,
        scratch_shapes=[
            pltpu.VMEM((PIECES, WIDTH, COLS), LOW),
            pltpu.VMEM((PIECES, TOK, COLS), LOW),
            pltpu.VMEM((TOK, WIDTH), LOW),
            pltpu.VMEM((TOK, WIDTH), LOW),
            pltpu.VMEM((RING, WIDTH, COLS), LOW),
            pltpu.VMEM((2, 4, HOPS, ROWS, COLS), LOW),
            pltpu.VMEM((4, ROWS, COLS), LOW),
            pltpu.VMEM((WIDTH, 128), WIDE),
            pltpu.VMEM((16, COLS), WIDE),
            pltpu.VMEM((LENGTH, COLS), WIDE),
            pltpu.VMEM((LENGTH, COLS), WIDE),
            pltpu.VMEM((TOK, 128), WIDE),
            pltpu.VMEM((8, LENGTH), WIDE),
            pltpu.VMEM((8, WIDTH), WIDE),
            pltpu.VMEM((8, COLS), WIDE),
            dma((7,)),
            dma((PIECES,)),
            dma((2, PIECES, HOPS)),
            dma((2, PIECES, HOPS)),
            dma((2, PIECES, HOPS)),
            dma((2, PIECES, HOPS)),
            dma((PIECES,)),
        ],
        compiler_params=pltpu.CompilerParams(collective_id=0, has_side_effects=True, vmem_limit_bytes=64000 * 1024),
    )(*operands)


def fused_body(tokens, block_place, w_qkv, b_qkv, w_o_t, b_o, w_up, b_up, w_down_t, b_down,
               norm1_gain, norm1_shift, norm2_gain, norm2_shift, cotangent):
    place = lax.axis_index("seq") * 4 + lax.axis_index("ctx")
    both = lax.all_gather(jnp.stack([tokens[0], cotangent[0]]), PLANE, axis=0, tiled=False)
    x_all, dy_all = both[:, 0].reshape(TOK, WIDTH), both[:, 1].reshape(TOK, WIDTH)
    places = lax.all_gather(block_place[0], "seq", axis=0, tiled=False)
    small = (b_qkv, b_o, b_up, b_down, norm1_gain, norm1_shift, norm2_gain, norm2_shift)
    packed = lax.all_gather(jnp.concatenate(small), "fsdp", axis=0, tiled=False)
    unpacked, start = [], 0
    for part in small:
        size = part.shape[0]
        unpacked.append(packed[:, start : start + size].reshape(-1).astype(WIDE))
        start += size
    bias_qkv, bias_o, bias_up, bias_down, gain1, shift1, gain2, shift2 = unpacked

    positions = (places[:, :, None] * BLK + jnp.arange(BLK, dtype=jnp.int32)).reshape(2, LENGTH)
    cosine, sine = angles(positions.reshape(-1))
    flat = positions.astype(WIDE).reshape(TOK, 1)
    table = jnp.concatenate([cosine, sine, jnp.broadcast_to(flat, (TOK, 64))], 1)
    pos_row = jnp.concatenate([positions.astype(WIDE), jnp.zeros((6, LENGTH), WIDE)])
    rows = jnp.concatenate([jnp.stack([gain1, shift1, gain2, shift2]), jnp.zeros((4, WIDTH), WIDE)])
    own_qkv = lax.dynamic_slice(bias_qkv.reshape(3, WIDTH), (0, place * COLS), (3, COLS))
    own_up = lax.dynamic_slice(bias_up, (place * 1024,), (1024,)).reshape(4, COLS)
    bias = jnp.concatenate([own_qkv, own_up, jnp.zeros((1, COLS), WIDE)])
    cols = jnp.concatenate([shift1[:, None], shift2[:, None], jnp.zeros((WIDTH, 126), WIDE)], 1)

    red, out_part, u_part, norms, gb = layer_call(
        x_all, dy_all, w_qkv, w_o_t, w_up, w_down_t, table, pos_row, rows, bias, cols)

    x_own, dy_own = tokens[0].astype(WIDE), cotangent[0].astype(WIDE)
    out_sum = lax.psum_scatter(out_part, PLANE, scatter_dimension=0, tiled=True).astype(WIDE)
    u_sum = lax.psum_scatter(u_part, PLANE, scatter_dimension=0, tiled=True).astype(WIDE)
    output = (x_own + out_sum + bias_o + bias_down).astype(LOW)[None]
    hat_own, scale_own = standardise(x_own)
    d_x = scale_own * (u_sum - jnp.mean(u_sum, -1, keepdims=True) - hat_own * jnp.mean(u_sum * hat_own, -1, keepdims=True))
    input_grad = (dy_own + d_x).astype(LOW)[None]

    gathered = lax.all_gather(red, PLANE, axis=0, tiled=False)
    g_qkv = gathered[:, :3].transpose(2, 1, 0, 3).reshape(ROWS, 3 * WIDTH).astype(WIDE)
    g_o = gathered[:, 3].transpose(1, 0, 2).reshape(ROWS, WIDTH).astype(WIDE)
    g_up = gathered[:, 4::2].transpose(2, 0, 1, 3).reshape(ROWS, 4 * WIDTH).astype(WIDE)
    g_down = gathered[:, 5::2].transpose(2, 0, 1, 3).reshape(ROWS, 4 * WIDTH).astype(WIDE)

    full_qkv = lax.dynamic_update_slice(jnp.zeros((3, WIDTH), WIDE), gb[:3], (0, place * COLS)).reshape(-1)
    full_up = lax.dynamic_update_slice(jnp.zeros((4 * WIDTH,), WIDE), gb[4:12:2].reshape(-1), (place * 1024,))
    sums = lax.psum((full_qkv, jnp.sum(dy_own, 0), full_up, norms[:, 8] / gain1, norms[:, 9], norms[:, 10] / gain2, norms[:, 11]), PLANE + ("fsdp",))
    mine = lax.axis_index("fsdp")
    sums = [lax.dynamic_slice_in_dim(s, mine * (s.shape[0] // 4), s.shape[0] // 4, 0) for s in sums]
    return (output, input_grad, g_qkv, sums[0], g_o, sums[1], g_up, sums[2], g_down, sums[1], sums[3], sums[4], sums[5], sums[6])


def solution(mesh):
    tok = P(("seq", "fsdp"), "ctx", None)
    mat, vec = P("fsdp", None), P("fsdp")
    params = (mat, vec, mat, vec, mat, vec, mat, vec, vec, vec, vec, vec)
    in_specs = (tok, P(("seq", "fsdp"), None)) + params + (tok,)
    return jax.shard_map(fused_body if fits(mesh) else body, mesh=mesh, in_specs=in_specs, out_specs=(tok, tok) + params, check_vma=False)
```

```python
import math

import jax
import jax.numpy as jnp
from jax import lax
from jax.experimental import pallas as pl
from jax.experimental.pallas import tpu as pltpu
from jax.sharding import PartitionSpec as P

HEADS = 8
HEAD = 256
ROT = 64
BLK = 128
EPS = 1e-05
PLANE = ("seq", "ctx")
LOW = jnp.bfloat16
WIDE = jnp.float32


def dot_nn(left, right):
    return lax.dot_general(left, right, (((1,), (0,)), ((), ())), preferred_element_type=WIDE)


def dot_nt(left, right):
    return lax.dot_general(left, right, (((1,), (1,)), ((), ())), preferred_element_type=WIDE)


def dot_tn(left, right):
    return lax.dot_general(left, right, (((0,), (0,)), ((), ())), preferred_element_type=WIDE)


def batch_nn(left, right):
    return lax.dot_general(left, right, (((2,), (1,)), ((0,), (0,))), preferred_element_type=WIDE)


def batch_nt(left, right):
    return lax.dot_general(left, right, (((2,), (2,)), ((0,), (0,))), preferred_element_type=WIDE)


def batch_tn(left, right):
    return lax.dot_general(left, right, (((1,), (1,)), ((0,), (0,))), preferred_element_type=WIDE)


def standardise(values):
    middle = jnp.mean(values, -1, keepdims=True)
    centred = values - middle
    spread = jnp.mean(centred * centred, -1, keepdims=True)
    scale = lax.rsqrt(spread + EPS)
    return centred * scale, scale


def angles(positions):
    freqs = 10000.0 ** (-(jnp.arange(ROT // 2, dtype=WIDE) * 2.0 / ROT))
    turned = positions.astype(WIDE)[:, None] * freqs[None, :]
    return jnp.cos(turned), jnp.sin(turned)


def turn(values, cosine, sine):
    half = ROT // 2
    one, two, rest = values[..., :half], values[..., half:ROT], values[..., ROT:]
    return jnp.concatenate([one * cosine - two * sine, two * cosine + one * sine, rest], -1)


def gelu_pair(hidden):
    bell = 0.5 * (1.0 + lax.erf(hidden * (1.0 / math.sqrt(2.0))))
    slope = bell + hidden * jnp.exp(-0.5 * hidden * hidden) * (1.0 / math.sqrt(2.0 * math.pi))
    return hidden * bell, slope


def body(tokens, block_place, w_qkv, b_qkv, w_o_t, b_o, w_up, b_up, w_down_t, b_down,
         norm1_gain, norm1_shift, norm2_gain, norm2_shift, cotangent):
    seqs, ctxs, shards = lax.axis_size("seq"), lax.axis_size("ctx"), lax.axis_size("fsdp")
    peers = seqs * ctxs
    place = lax.axis_index("seq") * ctxs + lax.axis_index("ctx")
    own, width = tokens.shape[1:]
    hidden_all = w_up.shape[1]
    length = own * ctxs
    share = max(1, peers // HEADS)
    heads = max(1, HEADS // peers)
    own_seqs = seqs // share
    group = place // share
    first_seq = (place % share) * own_seqs
    cols = heads * HEAD
    hid = hidden_all // peers

    x_own = tokens[0].astype(WIDE)
    dy_own = cotangent[0]
    both = lax.all_gather(jnp.stack([tokens[0], dy_own]), PLANE, axis=0, tiled=False)
    x_all = both[:, 0].reshape(seqs * length, width)
    dy_all = both[:, 1].reshape(seqs * length, width)
    places = lax.all_gather(block_place[0], "seq", axis=0, tiled=False)

    small = (b_qkv, b_o, b_up, b_down, norm1_gain, norm1_shift, norm2_gain, norm2_shift)
    packed = lax.all_gather(jnp.concatenate(small), "fsdp", axis=0, tiled=False)
    unpacked, start = [], 0
    for part in small:
        size = part.shape[0]
        unpacked.append(packed[:, start : start + size].reshape(-1).astype(WIDE))
        start += size
    bias_qkv, bias_o, bias_up, bias_down, gain1, shift1, gain2, shift2 = unpacked

    def head_cols(values, kinds):
        rows = values.shape[0]
        split = values.reshape(rows, kinds, HEADS * HEAD)
        return lax.dynamic_slice_in_dim(split, group * cols, cols, 2).reshape(rows, kinds * cols)

    def hid_cols(values):
        return lax.dynamic_slice_in_dim(values, place * hid, hid, 1)

    own_cols = jnp.concatenate([head_cols(w_qkv, 3), head_cols(w_o_t, 1), hid_cols(w_up), hid_cols(w_down_t)], 1)
    weights = lax.all_gather(own_cols, "fsdp", axis=0, tiled=True)
    cut = 4 * cols
    m_qkv, m_o, m_up, m_down = weights[:, : 3 * cols], weights[:, 3 * cols : cut], weights[:, cut : cut + hid], weights[:, cut + hid :]
    own_bias_qkv = head_cols(bias_qkv[None], 3)
    own_bias_up = hid_cols(bias_up[None])

    x_hat, _ = standardise(x_all.astype(WIDE))
    a1 = (x_hat * gain1 + shift1).astype(LOW)
    a2 = (x_hat * gain2 + shift2).astype(LOW)

    rows = own_seqs * length
    a1_seq = lax.dynamic_slice_in_dim(a1, first_seq * length, rows, 0)
    dy_seq = lax.dynamic_slice_in_dim(dy_all, first_seq * length, rows, 0)
    positions = (places[:, :, None] * BLK + jnp.arange(BLK, dtype=jnp.int32)).reshape(seqs, length)
    positions = lax.dynamic_slice_in_dim(positions, first_seq, own_seqs, 0)
    cosine, sine = angles(positions.reshape(-1))
    cosine, sine = cosine[:, None], sine[:, None]
    qkv = dot_nn(a1_seq, m_qkv) + own_bias_qkv

    def to_heads(values):
        return values.reshape(own_seqs, length, heads, HEAD).transpose(0, 2, 1, 3).reshape(own_seqs * heads, length, HEAD)

    def from_heads(values):
        return values.reshape(own_seqs, heads, length, HEAD).transpose(0, 2, 1, 3).reshape(rows, cols)

    def turned(values):
        return turn(values.reshape(rows, heads, HEAD), cosine, sine).reshape(rows, cols)

    def turned_back(values):
        return turn(values.reshape(rows, heads, HEAD), cosine, -sine).reshape(rows, cols)

    q = to_heads(turned(qkv[:, :cols]).astype(LOW))
    k = to_heads(turned(qkv[:, cols : 2 * cols]).astype(LOW))
    v = to_heads(qkv[:, 2 * cols :].astype(LOW))
    scaling = 1.0 / math.sqrt(HEAD)
    kept = (positions[:, :, None] >= positions[:, None, :])[:, None]
    kept = jnp.broadcast_to(kept, (own_seqs, heads, length, length)).reshape(own_seqs * heads, length, length)
    scores = jnp.where(kept, batch_nt(q, k) * scaling, -1e30)
    expo = jnp.exp(scores - jnp.max(scores, -1, keepdims=True))
    p = expo / jnp.sum(expo, -1, keepdims=True)
    p_low = p.astype(LOW)
    attn = from_heads(batch_nn(p_low, v).astype(LOW))
    d_attn = to_heads(dot_nn(dy_seq, m_o).astype(LOW))
    dp = batch_nt(d_attn, v)
    ds = jnp.where(kept, p * (dp - jnp.sum(p * dp, -1, keepdims=True)), 0.0).astype(LOW)
    dq = from_heads(batch_nn(ds, k) * scaling)
    dk = from_heads(batch_tn(ds, q) * scaling)
    dv = from_heads(batch_tn(p_low, d_attn))
    d_qkv = jnp.concatenate([turned_back(dq), turned_back(dk), dv], 1).astype(LOW)

    g, slope = gelu_pair(dot_nn(a2, m_up) + own_bias_up)
    g = g.astype(LOW)
    d_h = (dot_nn(dy_all, m_down) * slope).astype(LOW)

    def onto(values, part):
        return lax.dynamic_update_slice_in_dim(values, lax.dynamic_slice_in_dim(values, first_seq * length, rows, 0) + part, first_seq * length, 0)

    out_part = onto(dot_nt(g, m_down), dot_nt(attn, m_o))
    u_part = onto(dot_nt(d_h, m_up) * gain2, dot_nt(d_qkv, m_qkv) * gain1)
    out_sum = lax.psum_scatter(out_part.astype(LOW), PLANE, scatter_dimension=0, tiled=True).astype(WIDE)
    u_sum = lax.psum_scatter(u_part.astype(LOW), PLANE, scatter_dimension=0, tiled=True).astype(WIDE)
    output = (x_own + out_sum + bias_o + bias_down).astype(LOW)[None]
    hat_own, scale_own = standardise(x_own)
    d_x = scale_own * (u_sum - jnp.mean(u_sum, -1, keepdims=True) - hat_own * jnp.mean(u_sum * hat_own, -1, keepdims=True))
    input_grad = (dy_own.astype(WIDE) + d_x).astype(LOW)[None]

    g_qkv = dot_tn(a1_seq, d_qkv)
    g_o = dot_tn(dy_seq, attn)
    g_up = dot_tn(a2, d_h)
    g_down = dot_tn(dy_all, g)
    gb_qkv = jnp.sum(d_qkv, 0, dtype=WIDE)
    gb_up = jnp.sum(d_h, 0, dtype=WIDE)
    wide_qkv, wide_up = m_qkv.astype(WIDE), m_up.astype(WIDE)
    d_gain1 = jnp.sum(wide_qkv * (g_qkv - shift1[:, None] * gb_qkv), 1) / gain1
    d_gain2 = jnp.sum(wide_up * (g_up - shift2[:, None] * gb_up), 1) / gain2
    d_shift1 = jnp.sum(wide_qkv * gb_qkv, 1)
    d_shift2 = jnp.sum(wide_up * gb_up, 1)
    full_qkv = lax.dynamic_update_slice(jnp.zeros((3, HEADS * HEAD), WIDE), gb_qkv.reshape(3, cols), (0, group * cols)).reshape(-1)
    full_up = lax.dynamic_update_slice(jnp.zeros((hidden_all,), WIDE), gb_up, (place * hid,))
    sums = lax.psum((full_qkv, jnp.sum(dy_own, 0, dtype=WIDE), full_up, d_gain1, d_shift1, d_gain2, d_shift2), PLANE + ("fsdp",))
    mine = lax.axis_index("fsdp")

    def own_share(values):
        size = values.shape[0] // shards
        return lax.dynamic_slice_in_dim(values, mine * size, size, 0)

    sums = [own_share(s) for s in sums]
    grads = jnp.concatenate([g_qkv, g_o, g_up, g_down], 1).astype(LOW)
    reduced = lax.psum_scatter(grads, "fsdp", scatter_dimension=0, tiled=True)
    gathered = lax.all_gather(reduced, PLANE, axis=0, tiled=False)
    rows_own = reduced.shape[0]

    def spread_heads(values, kinds):
        values = values.astype(WIDE).reshape(peers // share, share, rows_own, kinds, cols).sum(1)
        return values.transpose(1, 2, 0, 3).reshape(rows_own, kinds * HEADS * HEAD)

    def spread_hid(values):
        return values.transpose(1, 0, 2).reshape(rows_own, hidden_all).astype(WIDE)

    return (
        output,
        input_grad,
        spread_heads(gathered[:, :, : 3 * cols], 3),
        sums[0],
        spread_heads(gathered[:, :, 3 * cols : cut], 1),
        sums[1],
        spread_hid(gathered[:, :, cut : cut + hid]),
        sums[2],
        spread_hid(gathered[:, :, cut + hid :]),
        sums[1],
        sums[3],
        sums[4],
        sums[5],
        sums[6],
    )


MESH = pl.DeviceIdType.MESH
PIECES = 12
ROWS = 512
COLS = 256
WIDTH = 2048
TOK = 2048
OWN = 256
LENGTH = 1024
HOPS = 3
SLOTS = 36
RS_START = 18
RING = 6
LAST = RS_START + SLOTS + 7
SCALING = 1.0 / math.sqrt(HEAD)


def fits(mesh):
    return dict(mesh.shape) == {"seq": 2, "ctx": 4, "fsdp": 4}


def at(index, size):
    return pl.ds(pl.multiple_of(index * size, size), size)


def remote(source, target, sent, came, device):
    return pltpu.make_async_remote_copy(
        src_ref=source, dst_ref=target, send_sem=sent, recv_sem=came, device_id=device, device_id_type=MESH)


def layer_kernel(tokens, cotangent, w_qkv, w_o, w_up, w_down, vec_own, place_own, turns,
                 out, input_grad, small_out, gout, x_land, core_land, first_land, second_land,
                 w_all, act, x_buf, dy_buf, g_ring, landing, small, gb, tab, pos, rows, bias,
                 stage, vecs, vec32, places, pack, pack_z, pack_p, final,
                 load_sem, own_sem, ag_send, ag_recv, rs_send, rs_recv, red_sem, ga_send, ga_recv,
                 vec_send, vec_recv, pk_send, pk_recv, pp_send, pp_recv, core_send, core_recv, one_send, one_recv,
                 two_send, two_recv):
    y, c, z = lax.axis_index("seq"), lax.axis_index("ctx"), lax.axis_index("fsdp")
    core = lax.rem(c, 2)
    chip = c // 2
    place = y * 4 + c
    right, left = (y, c, jnp.minimum(z + 1, 3)), (y, c, jnp.maximum(z - 1, 0))
    c_x, c_core = lax.rem(c + 2, 4), c + 1 - 2 * core
    dev_x, dev_y, dev_c = (y, c_x, z), (1 - y, c, z), (y, c_core, z)
    place_x, place_y, place_d = y * 4 + c_x, (1 - y) * 4 + c, (1 - y) * 4 + c_x
    c_core_x = lax.rem(c_core + 2, 4)
    place_c, place_cx, place_cy, place_cd = y * 4 + c_core, y * 4 + c_core_x, (1 - y) * 4 + c_core, (1 - y) * 4 + c_core_x
    above = [(y, c, lax.rem(z + d, 4)) for d in (1, 2, 3)]
    beside = []
    for d in range(1, 8):
        other = lax.rem(place + d, 8)
        beside.append((other // 4, lax.rem(other, 4), z))
    lane = lax.broadcasted_iota(jnp.int32, (1, 128), 1)

    barrier = pltpu.get_barrier_semaphore()
    for device in above + beside:
        pl.semaphore_signal(barrier, inc=1, device_id=device, device_id_type=MESH)

    def own_piece(i):
        if i < 3:
            source = w_qkv.at[:, at(i * 8 + place, COLS)]
        elif i == 3:
            source = w_o.at[:, at(place, COLS)]
        else:
            source = (w_up if i % 2 == 0 else w_down).at[:, at(place * 4 + (i - 4) // 2, COLS)]
        return pltpu.make_async_copy(source, w_all.at[i, at(z, ROWS)], own_sem.at[i])

    loads = [
        pltpu.make_async_copy(tokens.at[0], x_land.at[place], load_sem.at[0]),
        pltpu.make_async_copy(cotangent.at[0], dy_buf.at[at(place, OWN)], load_sem.at[1]),
        pltpu.make_async_copy(vec_own, vecs.at[z], load_sem.at[2]),
        pltpu.make_async_copy(place_own, places.at[y], load_sem.at[3]),
        pltpu.make_async_copy(turns, small.at[pl.ds(0, LENGTH)], load_sem.at[4]),
    ]
    for i in range(PIECES):
        own_piece(i).start()
    for load in loads:
        load.start()
    pl.semaphore_wait(barrier, 10)

    def gather(tag, source, target):
        def copy(k):
            sent, came = ga_send.at[tag, k], ga_recv.at[tag, k]
            if k == 0:
                return remote(source(0), target(place, 0), sent, came, dev_x)
            if k == 1:
                return remote(source(1), target(place, 1), sent, came, dev_x)
            if k == 2:
                return remote(source(1), target(place, 1), sent, came, dev_y)
            if k == 3:
                return remote(source(0), target(place, 0), sent, came, dev_y)
            if k == 4:
                return remote(source(None), target(place, None), sent, came, dev_c)
            if k == 5:
                return remote(target(place_x, 0), target(place_x, 0), sent, came, dev_y)
            if k == 6:
                return remote(target(place_y, 1), target(place_y, 1), sent, came, dev_x)
            which = (place_x, place_y, place_d)[k - 7]
            return remote(target(which, None), target(which, None), sent, came, dev_c)

        def arrived(k):
            spot = (
                (place_x, 0), (place_x, 1), (place_y, 1), (place_y, 0), (place_c, None),
                (place_d, 0), (place_d, 1), (place_cx, None), (place_cy, None), (place_cd, None),
            )[k]
            here = target(*spot)
            remote(here, here, ga_send.at[tag, k], ga_recv.at[tag, k], dev_c).wait_recv()

        def start():
            for k in (0, 2, 1, 3, 4):
                copy(k).start()

        def middle():
            arrived(0)
            copy(5).start()
            arrived(2)
            copy(6).start()

        def forward():
            arrived(1)
            copy(7).start()
            arrived(3)
            copy(8).start()

        def far():
            arrived(5)
            arrived(6)
            copy(9).start()

        def end():
            for k in (4, 7, 8, 9):
                arrived(k)
            for k in range(10):
                copy(k).wait_send()

        return start, middle, forward, far, end

    def half_of(ref, half, size):
        return ref if half is None else ref.at[pl.ds(half * size, size)]

    x_gather = gather(0, lambda half: half_of(tokens.at[0], half, 128), lambda who, half: half_of(x_land.at[who], half, 128))
    dy_gather = gather(
        1, lambda half: half_of(cotangent.at[0], half, 128),
        lambda who, half: dy_buf.at[at(who, OWN)] if half is None else dy_buf.at[at(who * 2 + half, 128)])
    x_gather[0]()

    def vec_copy(d):
        return remote(vec_own, vecs.at[z], vec_send.at[d], vec_recv.at[d], above[d])

    def place_copy():
        return remote(place_own, places.at[y], vec_send.at[3], vec_recv.at[3], dev_y)

    for d in range(3):
        vec_copy(d).start()
    place_copy().start()
    for i in range(PIECES):
        own_piece(i).wait()

    def parts(s):
        return (s // 6) * 2 + s % 2, (s // 2) % 3

    def ag_copy(way, piece, hop, shard):
        block = w_all.at[piece, at(shard, ROWS)]
        return remote(block, block, ag_send.at[way, piece, hop], ag_recv.at[way, piece, hop], right if way == 0 else left)

    def ag_service(slot):
        before = slot - 2
        old, old_hop = parts(jnp.maximum(before, 0))
        live = (before >= 0) & (before < SLOTS)

        @pl.when(live & (z >= 1) & (z - 1 - old_hop >= 0))
        def _():
            ag_copy(0, old, old_hop, z - 1 - old_hop).wait_recv()

        @pl.when(live & (z <= 2) & (z + 1 + old_hop <= 3))
        def _():
            ag_copy(1, old, old_hop, z + 1 + old_hop).wait_recv()

        piece, hop = parts(jnp.minimum(slot, SLOTS - 1))

        @pl.when((slot < SLOTS) & (z <= 2) & (z - hop >= 0))
        def _():
            ag_copy(0, piece, hop, z - hop).start()

        @pl.when((slot < SLOTS) & (z >= 1) & (z + hop <= 3))
        def _():
            ag_copy(1, piece, hop, z + hop).start()

        @pl.when(live & (z <= 2) & (z - old_hop >= 0))
        def _():
            ag_copy(0, old, old_hop, z - old_hop).wait_send()

        @pl.when(live & (z >= 1) & (z + old_hop <= 3))
        def _():
            ag_copy(1, old, old_hop, z + old_hop).wait_send()

    def rs_piece(n):
        return jnp.where(n < 4, 3 - n, 4 + (n - 4) // 2 + 4 * (n % 2))

    def landing_slot(n, hop):
        return jnp.where(hop < 2, (n % 2) * 2 + hop, 4 + n % 4)

    def rs_copy(way, n, hop, shard):
        return remote(
            g_ring.at[n % RING, at(shard, ROWS)], landing.at[way, landing_slot(n, hop)],
            rs_send.at[way, n, hop], rs_recv.at[way, n, hop], right if way == 0 else left)

    def rs_add(way, n, hop, shard):
        rs_copy(way, n, hop, shard).wait_recv()
        block = g_ring.at[n % RING, at(shard, ROWS)]
        block[...] = (block[...].astype(WIDE) + landing[way, landing_slot(n, hop)].astype(WIDE)).astype(LOW)

    def red_copy(n):
        return pltpu.make_async_copy(g_ring.at[n % RING, at(z, ROWS)], gout.at[rs_piece(n), place], red_sem.at[n])

    def red_gather(n):
        piece = rs_piece(n)
        return gather(
            2 + n, lambda half: half_of(gout.at[piece, place], half, 256),
            lambda who, half: half_of(gout.at[piece, who], half, 256))

    def rs_service(slot):
        before = slot - 2
        old, old_hop = parts(jnp.clip(before, 0, SLOTS - 1))
        live = (before >= 0) & (before < SLOTS)

        @pl.when(live & (z >= 1) & (z - 1 <= old_hop))
        def _():
            rs_add(0, old, old_hop, z + 2 - old_hop)

        @pl.when(live & (z <= 2) & (2 - z <= old_hop))
        def _():
            rs_add(1, old, old_hop, z - 2 + old_hop)

        piece, hop = parts(jnp.clip(slot, 0, SLOTS - 1))
        sending = (slot >= 0) & (slot < SLOTS)

        @pl.when(sending & (z <= 2) & (z <= hop))
        def _():
            rs_copy(0, piece, hop, z + 3 - hop).start()

        @pl.when(sending & (z >= 1) & (3 - z <= hop))
        def _():
            rs_copy(1, piece, hop, z - 3 + hop).start()

        @pl.when(live & (z <= 2) & (z <= old_hop))
        def _():
            rs_copy(0, old, old_hop, z + 3 - old_hop).wait_send()

        @pl.when(live & (z >= 1) & (3 - z <= old_hop))
        def _():
            rs_copy(1, old, old_hop, z - 3 + old_hop).wait_send()

        @pl.when(live & (old_hop == 2))
        def _():
            red_copy(old).start()
            red_copy(old).wait()
            red_gather(old)[0]()

        for step, delay in ((1, 1), (2, 2), (3, 3), (4, 5)):
            begun = slot - delay
            n = jnp.clip((begun // 6) * 2 - 2 + begun % 6, 0, PIECES - 1)

            @pl.when((begun >= 6) & (begun < SLOTS + 6) & (begun % 6 < 2))
            def _(step=step, n=n):
                red_gather(n)[step]()

    def service(slot):
        if isinstance(slot, int):
            if slot < SLOTS + 2:
                ag_service(jnp.int32(slot))
            if slot >= RS_START:
                rs_service(jnp.int32(slot - RS_START))
        else:
            ag_service(slot)
            rs_service(slot - RS_START)

    def services(first, last, early=False):
        def step(slot, carry):
            ag_service(slot)
            if not early:
                rs_service(slot - RS_START)
            return carry

        lax.fori_loop(first, last, step, 0)

    def loop(count, body, first=None, ag=True, rs=True):
        def step(i, carry):
            if first is not None:
                if ag:
                    ag_service(first + i)
                if rs:
                    rs_service(first + i - RS_START)
            body(i)
            return carry

        lax.fori_loop(0, count, step, 0)

    services(0, 2, True)
    for load in loads[2:]:
        load.wait()
    for d in range(3):
        here = vecs.at[lax.rem(z + 3 - d, 4)]
        remote(here, here, vec_send.at[d], vec_recv.at[d], above[d]).wait_recv()
    other = places.at[1 - y]
    remote(other, other, vec_send.at[3], vec_recv.at[3], dev_y).wait_recv()
    for shard in range(4):
        vec32[pl.ds(shard * 16, 16), :] = vecs[shard].astype(WIDE)
        for k in range(4):
            rows[k : k + 1, pl.ds(shard * ROWS, ROWS)] = vec32[shard * 16 + 9 + k : shard * 16 + 10 + k, :]
        rows[4:5, pl.ds(shard * ROWS, ROWS)] = vec32[shard * 16 + 3 : shard * 16 + 4, :] + vec32[shard * 16 + 8 : shard * 16 + 9, :]
        rows[5:8, pl.ds(shard * ROWS, ROWS)] = jnp.zeros((3, ROWS), WIDE)
    for kind in range(3):
        flat = kind * WIDTH + place * COLS
        bias[kind : kind + 1, :] = vec32[pl.ds((flat // 1536) * 16 + (flat % 1536) // 512, 1), at((flat % 512) // 256, COLS)]
    for part in range(4):
        flat = place * 1024 + part * COLS
        bias[3 + part : 4 + part, :] = vec32[pl.ds((flat // 2048) * 16 + 4 + (flat % 2048) // 512, 1), at((flat % 512) // 256, COLS)]
    def set_place(i, carry):
        seq, block = i // 8, i % 8
        value = jnp.sum(jnp.where(lane == block, places[seq, 0:1, :], 0.0), 1, keepdims=True)
        made = jnp.zeros((BLK, 128), WIDE)
        for b in range(8):
            made = jnp.where(value == float(b), small[pl.ds(b * BLK, BLK), :], made)
        tab[at(i, BLK), :] = made
        pos[seq, :, at(block, BLK)] = jnp.broadcast_to(value * float(BLK) + lane.astype(WIDE), (8, BLK))
        return carry

    services(2, 3, True)
    lax.fori_loop(0, 16, set_place, 0)
    for shard in range(4):
        tall = jnp.concatenate([rows[:, pl.ds(shard * ROWS, ROWS)], jnp.zeros((120, ROWS), WIDE)], 0)
        small[pl.ds(shard * ROWS, ROWS), :] = jnp.transpose(tall)
    x_gather[1]()
    services(3, 5, True)
    x_gather[2]()
    dy_gather[0]()
    services(5, 7, True)
    x_gather[3]()
    services(7, 8, True)
    x_gather[4]()
    loads[0].wait()

    def norm_tile(which):
        def run(i):
            def part(n, carry):
                block = at(i * 4 + n, 64)
                centred, scale = standardise_rows(x_buf[block, :].astype(WIDE))
                x_buf[block, :] = (centred * scale * rows[2 * which : 2 * which + 1, :] + rows[2 * which + 1 : 2 * which + 2, :]).astype(LOW)
                return carry

            lax.fori_loop(0, 4, part, 0)
        return run

    def load_x():
        copies = [pltpu.make_async_copy(x_land.at[p], x_buf.at[pl.ds(p * OWN, OWN)], own_sem.at[p]) for p in range(8)]
        for copy in copies:
            copy.start()
        for copy in copies:
            copy.wait()

    def norm(which, first, rs):
        load_x()

        def body(i):
            for n in range(4):
                norm_tile(which)(4 * i + n)

        loop(2, body, first, rs=rs)

    norm(0, 8, False)
    dy_gather[1]()

    def turned(values, block, sign):
        entry = tab[block, :]
        cosine = jnp.where(lane < 32, entry, jnp.where(lane < 64, pltpu.roll(entry, 32, 1), 1.0))
        sine = jnp.where(lane < 32, -pltpu.roll(entry, 96, 1), jnp.where(lane < 64, entry, 0.0))
        low = values[:, :128]
        partner = jnp.where(lane < 32, pltpu.roll(low, 96, 1), pltpu.roll(low, 32, 1))
        return jnp.concatenate([low * cosine + partner * (sine * sign), values[:, 128:]], 1)

    def project(kind):
        def run(i):
            block = at(i, 512)
            made = dot_nn(x_buf[block, :], w_all[kind]) + bias[kind : kind + 1, :]
            if kind < 2:
                made = turned(made, block, 1.0)
            act[9 + kind, block, :] = made.astype(LOW)
        return run

    services(10, 11, True)
    loop(4, project(0))
    dy_gather[2]()
    services(11, 12, True)
    loop(4, project(1))
    services(12, 14, True)
    loop(4, project(2))
    dy_gather[3]()
    dy_gather[4]()
    loads[1].wait()

    def attend(i):
        seq = i // 4
        block, keys = at(i, 256), at(seq, LENGTH)

        q, k, v = act[9, block, :], act[10, keys, :], act[11, keys, :]
        kept = tab[block, 64:65] >= pos[seq, 0:1, :]
        scores = jnp.where(kept, dot_nt(q, k) * SCALING, -1e30)
        expo = jnp.exp(scores - jnp.max(scores, -1, keepdims=True))
        p = expo * (1.0 / jnp.sum(expo, -1, keepdims=True))
        p_low = p.astype(LOW)
        act[3, block, :] = dot_nn(p_low, v).astype(LOW)
        d_attn = dot_nn(dy_buf[block, :], w_all[3]).astype(LOW)
        dp = dot_nt(d_attn, v)
        ds = jnp.where(kept, p * (dp - jnp.sum(p * dp, -1, keepdims=True)), 0.0).astype(LOW)
        act[0, block, :] = turned(dot_nn(ds, k) * SCALING, block, -1.0).astype(LOW)
        act[8, block, :] = d_attn
        for n in range(4):
            g_ring[n, at(i % 4, 256), :] = ds[:, n * COLS : (n + 1) * COLS]
            g_ring[n, at(4 + i % 4, 256), :] = p_low[:, n * COLS : (n + 1) * COLS]

        @pl.when(i % 4 == 3)
        def _():
            def keyed(n, carry):
                mine = at(seq * 4 + n, COLS)
                d_keys = dot_tn(g_ring[n, 0:LENGTH, :], act[9, keys, :]) * SCALING
                act[1, mine, :] = turned(d_keys, mine, -1.0).astype(LOW)
                act[2, mine, :] = dot_tn(g_ring[n, LENGTH:, :], act[8, keys, :]).astype(LOW)
                return carry

            lax.fori_loop(0, 4, keyed, 0)

    def attend_two(i):
        def inner(n, carry):
            attend(2 * i + n)
            return carry

        lax.fori_loop(0, 2, inner, 0)

    loop(4, attend_two, 14, rs=False)

    def gradient(piece, n, source):
        summed = piece < 3 or (piece != 3 and piece % 2 == 0)
        if summed:
            gb[piece : piece + 1, :] = jnp.zeros((1, COLS), WIDE)

            def count(i, carry):
                gb[piece : piece + 1, :] += jnp.sum(act[piece, at(i, 256), :].astype(WIDE), 0, keepdims=True)
                return carry

            lax.fori_loop(0, 8, count, 0)

        def part(s, carry):
            block = at(s, ROWS)
            made = dot_tn(source[:, block], act[piece])
            g_ring[n % RING, block, :] = made.astype(LOW)
            if summed:
                mine = 0 if piece < 3 else 1
                weight = w_all[piece, block, :].astype(WIDE)
                sums = gb[piece : piece + 1, :]
                gain = jnp.sum(weight * (made - small[block, 2 * mine + 1 : 2 * mine + 2] * sums), 1, keepdims=True)
                shift = jnp.sum(weight * sums, 1, keepdims=True)
                here = 8 + 2 * mine
                old = small[block, :]
                small[block, :] = old + jnp.where(lane == here, gain, 0.0) + jnp.where(lane == here + 1, shift, 0.0)
            return carry

        lax.fori_loop(0, 4, part, 0)

    rows[5:6, :] = jnp.sum(dy_buf[at(place, OWN), :].astype(WIDE), 0, keepdims=True)
    gradient(3, 0, dy_buf)
    service(18)
    gradient(2, 1, x_buf)
    service(19)
    gradient(1, 2, x_buf)
    service(20)
    gradient(0, 3, x_buf)
    service(21)
    norm(1, 22, True)

    def feed(part):
        up, down = 4 + 2 * part, 5 + 2 * part

        def run(i):
            for n in range(2):
                block = at(2 * i + n, 512)
                hidden = dot_nn(x_buf[block, :], w_all[up]) + bias[3 + part : 4 + part, :]
                d_gelu = dot_nn(dy_buf[block, :], w_all[down])
                made, slope = gelu_pair(hidden)
                act[down, block, :] = made.astype(LOW)
                act[up, block, :] = (d_gelu * slope).astype(LOW)
        return run

    slot = 24
    for part in range(4):
        if part == 3:
            services(slot, SLOTS + 2)
            slot = SLOTS + 2
        loop(2, feed(part), slot)
        slot += 2
        gradient(4 + 2 * part, 4 + 2 * part, x_buf)
        service(slot)
        gradient(5 + 2 * part, 5 + 2 * part, dy_buf)
        service(slot + 1)
        slot += 2

    for shard in range(4):
        here = pl.ds(shard * ROWS, ROWS)
        flat = jnp.transpose(small[here, :])
        pack[shard, 0:1, :] = flat[8:9] / rows[0:1, here]
        pack[shard, 1:2, :] = flat[9:10]
        pack[shard, 2:3, :] = flat[10:11] / rows[2:3, here]
        pack[shard, 3:4, :] = flat[11:12]
        pack[shard, 4:5, :] = rows[5:6, here]
        pack[shard, 5:8, :] = jnp.zeros((3, ROWS), WIDE)
        pack[shard, 8:16, :] = jnp.zeros((8, ROWS), WIDE)
        for kind in range(3):
            pack[shard, 8 + kind : 9 + kind, :COLS] = gb[kind : kind + 1, :]
        for part in range(4):
            pack[shard, 11 + part : 12 + part, :COLS] = gb[4 + 2 * part : 5 + 2 * part, :]
    pack_z[z] = pack[z]

    def pack_copy(d):
        return remote(pack.at[lax.rem(z + d + 1, 4)], pack_z.at[z], pk_send.at[d], pk_recv.at[d], above[d])

    def peer_copy(d):
        return remote(pack_p.at[place], pack_p.at[place], pp_send.at[d], pp_recv.at[d], beside[d])

    for d in range(3):
        pack_copy(d).start()

    def sum_z():
        for d in range(3):
            here = pack_z.at[lax.rem(z + 3 - d, 4)]
            remote(here, here, pk_send.at[d], pk_recv.at[d], above[d]).wait_recv()
        pack_p[place] = pack_z[0] + pack_z[1] + pack_z[2] + pack_z[3]
        for d in range(7):
            peer_copy(d).start()

    def sum_plane():
        for d in range(7):
            here = pack_p.at[lax.rem(place + 7 - d, 8)]
            remote(here, here, pp_send.at[d], pp_recv.at[d], beside[d]).wait_recv()
        total = pack_p[0, 0:8, :]
        for p in range(1, 8):
            total = total + pack_p[p, 0:8, :]
        final[:, 0:ROWS] = total
        final[:, ROWS:] = jnp.zeros((8, 2 * COLS), WIDE)
        for r in range(6):
            flat = 6 * z + r
            final[r : r + 1, ROWS : ROWS + COLS] = pack_p[flat % 8, pl.ds(8 + flat // 8, 1), 0:COLS]
        for r in range(8):
            final[r : r + 1, ROWS + COLS :] = pack_p[2 * z + r // 4, 11 + r % 4 : 12 + r % 4, 0:COLS]

    tiles = {"d": (1 - y) * 2 + 1 - chip, "x": y * 2 + 1 - chip, "y": (1 - y) * 2 + chip, "own": y * 2 + chip}
    order = ("d", "x", "y", "own")
    both = (x_buf, dy_buf)

    def finish(tile):
        def run(i):
            block, columns = at(tile, 512), at(i, 512)

            def total(pieces):
                return sum(dot_nt(act[piece, block, :], w_all[piece, columns, :]) for piece in pieces)

            x_buf[block, columns] = total((3, 5, 7, 9, 11)).astype(LOW)
            first = total((0, 1, 2)) * rows[0:1, columns]
            dy_buf[block, columns] = (first + total((4, 6, 8, 10)) * rows[2:3, columns]).astype(LOW)
        return run

    def block_of(name, whose):
        return at(tiles[name] * 2 + whose, OWN)

    def half_rows(name, half):
        return at(tiles[name] * 4 + core * 2 + half, 128)

    def core_copy(name, a):
        i = order.index(name)
        return remote(both[a].at[block_of(name, 1 - core)], core_land.at[i, a], core_send.at[i, a], core_recv.at[i, a], dev_c)

    def first_copy(i, a):
        name, half, device = (("d", 0, dev_x), ("d", 1, dev_y), ("x", 0, dev_x), ("y", 1, dev_y))[i]
        return remote(both[a].at[half_rows(name, half)], first_land.at[i, a], one_send.at[i, a], one_recv.at[i, a], device)

    def second_copy(i, a):
        name, half, device = (("y", 0, dev_y), ("x", 1, dev_x))[i]
        return remote(both[a].at[half_rows(name, half)], second_land.at[i, a], two_send.at[i, a], two_recv.at[i, a], device)

    def fetch(source, a):
        return pltpu.make_async_copy(source, stage.at[a], load_sem.at[a])

    def add_in(copies, sources, spots):
        for a in range(2):
            copies[a].wait_recv()
        for half, spot in enumerate(spots):
            for a in range(2):
                fetch(sources[a].at[pl.ds(half * 128, 128)], a).start()
            for a in range(2):
                fetch(sources[a].at[pl.ds(half * 128, 128)], a).wait()
                both[a][spot, :] = (both[a][spot, :].astype(WIDE) + stage[a].astype(WIDE)).astype(LOW)

    def core_start(name):
        for a in range(2):
            core_copy(name, a).start()

    def core_add(name):
        i = order.index(name)
        add_in([core_copy(name, a) for a in range(2)], [core_land.at[i, a] for a in range(2)], [half_rows(name, 0), half_rows(name, 1)])

    def first_start(i):
        for a in range(2):
            first_copy(i, a).start()

    def first_add(i):
        name, half = (("y", 0), ("x", 1), ("own", 0), ("own", 1))[i]
        add_in([first_copy(i, a) for a in range(2)], [first_land.at[i, a] for a in range(2)], [half_rows(name, half)])

    def second_start(i):
        for a in range(2):
            second_copy(i, a).start()

    def second_add(i):
        add_in([second_copy(i, a) for a in range(2)], [second_land.at[i, a] for a in range(2)], [half_rows("own", i)])

    def finish_tile(name, first):
        def body(i):
            finish(tiles[name])(2 * i)
            finish(tiles[name])(2 * i + 1)

        loop(2, body, first, ag=False)
        core_start(name)

    finish_tile("d", 42)
    finish_tile("x", 44)
    core_add("d")
    first_start(0)
    first_start(1)
    sum_z()
    finish_tile("y", 46)
    core_add("x")
    first_start(2)
    finish_tile("own", 48)
    core_add("y")
    first_start(3)
    service(50)
    service(51)
    first_add(0)
    second_start(0)
    first_add(1)
    second_start(1)
    service(52)
    core_add("own")
    sum_plane()
    service(53)
    first_add(2)
    service(54)
    first_add(3)
    service(55)
    second_add(0)
    service(56)
    second_add(1)
    service(57)

    for half in range(2):
        given = [tokens.at[0, pl.ds(half * 128, 128)], cotangent.at[0, pl.ds(half * 128, 128)]]
        for a in range(2):
            fetch(given[a], a).start()
        for a in range(2):
            fetch(given[a], a).wait()

        def emit(i, carry, half=half):
            here, mine = at(i, 64), at(place * 4 + half * 2 + i, 64)
            inputs = stage[0, here, :].astype(WIDE)
            x_buf[mine, :] = (inputs + x_buf[mine, :].astype(WIDE) + rows[4:5, :]).astype(LOW)
            centred, scale = standardise_rows(inputs)
            hat = centred * scale
            u = dy_buf[mine, :].astype(WIDE)
            inner = jnp.mean(u * hat, -1, keepdims=True)
            d_x = scale * (u - jnp.mean(u, -1, keepdims=True) - hat * inner)
            dy_buf[mine, :] = (stage[1, here, :].astype(WIDE) + d_x).astype(LOW)
            return carry

        lax.fori_loop(0, 2, emit, 0)
    ends = [
        pltpu.make_async_copy(x_buf.at[at(place, OWN)], out, load_sem.at[0]),
        pltpu.make_async_copy(dy_buf.at[at(place, OWN)], input_grad, load_sem.at[1]),
        pltpu.make_async_copy(final, small_out, load_sem.at[2]),
    ]
    for end in ends:
        end.start()
    services(58, LAST)
    for end in ends:
        end.wait()
    for d in range(3):
        vec_copy(d).wait_send()
        pack_copy(d).wait_send()
    place_copy().wait_send()
    for d in range(7):
        peer_copy(d).wait_send()
    for a in range(2):
        for name in order:
            core_copy(name, a).wait_send()
        for i in range(4):
            first_copy(i, a).wait_send()
        for i in range(2):
            second_copy(i, a).wait_send()


def standardise_rows(values):
    middle = jnp.mean(values, -1, keepdims=True)
    centred = values - middle
    spread = jnp.mean(centred * centred, -1, keepdims=True)
    return centred, lax.rsqrt(spread + EPS)


def layer_call(*operands):
    anywhere = pl.BlockSpec(memory_space=pltpu.HBM)
    shape = jax.ShapeDtypeStruct
    dma = pltpu.SemaphoreType.DMA
    out_shape = (
        shape((OWN, WIDTH), LOW),
        shape((OWN, WIDTH), LOW),
        shape((8, 1024), WIDE),
        shape((PIECES, 8, ROWS, COLS), LOW),
        shape((8, OWN, WIDTH), LOW),
        shape((4, 2, OWN, WIDTH), LOW),
        shape((4, 2, 128, WIDTH), LOW),
        shape((2, 2, 128, WIDTH), LOW),
    )
    return pl.pallas_call(
        layer_kernel,
        out_shape=out_shape,
        in_specs=[anywhere] * len(operands),
        out_specs=[anywhere] * len(out_shape),
        scratch_shapes=[
            pltpu.VMEM((PIECES, WIDTH, COLS), LOW),
            pltpu.VMEM((PIECES, TOK, COLS), LOW),
            pltpu.VMEM((TOK, WIDTH), LOW),
            pltpu.VMEM((TOK, WIDTH), LOW),
            pltpu.VMEM((RING, WIDTH, COLS), LOW),
            pltpu.VMEM((2, 8, ROWS, COLS), LOW),
            pltpu.VMEM((WIDTH, 128), WIDE),
            pltpu.VMEM((16, COLS), WIDE),
            pltpu.VMEM((TOK, 128), WIDE),
            pltpu.VMEM((2, 8, LENGTH), WIDE),
            pltpu.VMEM((8, WIDTH), WIDE),
            pltpu.VMEM((8, COLS), WIDE),
            pltpu.VMEM((2, 128, WIDTH), LOW),
            pltpu.VMEM((4, 16, ROWS), LOW),
            pltpu.VMEM((64, ROWS), WIDE),
            pltpu.VMEM((2, 8, 128), WIDE),
            pltpu.VMEM((4, 16, ROWS), WIDE),
            pltpu.VMEM((4, 16, ROWS), WIDE),
            pltpu.VMEM((8, 16, ROWS), WIDE),
            pltpu.VMEM((8, 1024), WIDE),
            dma((5,)),
            dma((PIECES,)),
            dma((2, PIECES, HOPS)),
            dma((2, PIECES, HOPS)),
            dma((2, PIECES, HOPS)),
            dma((2, PIECES, HOPS)),
            dma((PIECES,)),
            dma((2 + PIECES, 10)),
            dma((2 + PIECES, 10)),
            dma((4,)),
            dma((4,)),
            dma((3,)),
            dma((3,)),
            dma((7,)),
            dma((7,)),
            dma((4, 2)),
            dma((4, 2)),
            dma((4, 2)),
            dma((4, 2)),
            dma((2, 2)),
            dma((2, 2)),
        ],
        compiler_params=pltpu.CompilerParams(collective_id=0, has_side_effects=True, vmem_limit_bytes=61 * 1024 * 1024),
    )(*operands)


def widen_kernel(first, second, g_qkv, g_o, g_up, g_down):
    step = pl.program_id(0)

    @pl.when(step < 3)
    def _():
        for p in range(8):
            g_qkv[:, p * COLS : (p + 1) * COLS] = first[0, p].astype(WIDE)

    @pl.when(step == 3)
    def _():
        for p in range(8):
            g_o[:, p * COLS : (p + 1) * COLS] = first[0, p].astype(WIDE)

    @pl.when((step >= 4) & (step < 12))
    def _():
        for part in range(4):
            g_up[:, part * COLS : (part + 1) * COLS] = second[part, 0].astype(WIDE)

    @pl.when(step >= 12)
    def _():
        for part in range(4):
            g_down[:, part * COLS : (part + 1) * COLS] = second[part, 0].astype(WIDE)


def widen(gathered):
    shape = jax.ShapeDtypeStruct
    return pl.pallas_call(
        widen_kernel,
        grid=(20,),
        in_specs=[
            pl.BlockSpec((1, 8, ROWS, COLS), lambda i: (jnp.minimum(i, 3), 0, 0, 0)),
            pl.BlockSpec((4, 1, ROWS, COLS), lambda i: (jnp.where(i < 12, 1, 2), jnp.where(i < 4, 0, (i - 4) % 8), 0, 0)),
        ],
        out_specs=[
            pl.BlockSpec((ROWS, WIDTH), lambda i: (0, jnp.minimum(i, 2))),
            pl.BlockSpec((ROWS, WIDTH), lambda i: (0, 0)),
            pl.BlockSpec((ROWS, 1024), lambda i: (0, jnp.clip(i - 4, 0, 7))),
            pl.BlockSpec((ROWS, 1024), lambda i: (0, jnp.clip(i - 12, 0, 7))),
        ],
        out_shape=(shape((ROWS, 3 * WIDTH), WIDE), shape((ROWS, WIDTH), WIDE), shape((ROWS, 4 * WIDTH), WIDE), shape((ROWS, 4 * WIDTH), WIDE)),
        compiler_params=pltpu.CompilerParams(vmem_limit_bytes=48 * 1024 * 1024),
    )(gathered, gathered)


def fused_body(tokens, block_place, w_qkv, b_qkv, w_o_t, b_o, w_up, b_up, w_down_t, b_down,
               norm1_gain, norm1_shift, norm2_gain, norm2_shift, cotangent):
    vec = jnp.concatenate([b_qkv, b_o, b_up, b_down, norm1_gain, norm1_shift, norm2_gain, norm2_shift, jnp.zeros((3 * ROWS,), LOW)])
    place_own = jnp.broadcast_to(jnp.pad(block_place.astype(WIDE), ((0, 0), (0, 120))), (8, 128))
    cosine, sine = angles(jnp.arange(LENGTH, dtype=jnp.int32))
    where = jnp.broadcast_to(jnp.arange(LENGTH, dtype=WIDE)[:, None], (LENGTH, 64))
    turns = jnp.concatenate([cosine, sine, where], 1)
    results = layer_call(tokens, cotangent, w_qkv, w_o_t, w_up, w_down_t, vec.reshape(16, ROWS), place_own, turns)
    output, input_grad, sums, gathered = results[:4]
    g_qkv, g_o, g_up, g_down = widen(gathered)
    grad_bias = sums[4, :ROWS]
    return (
        output[None],
        input_grad[None],
        g_qkv,
        sums[:6, ROWS : ROWS + COLS].reshape(-1),
        g_o,
        grad_bias,
        g_up,
        sums[:, ROWS + COLS :].reshape(-1),
        g_down,
        grad_bias,
        sums[0, :ROWS],
        sums[1, :ROWS],
        sums[2, :ROWS],
        sums[3, :ROWS],
    )


def solution(mesh):
    tok = P(("seq", "fsdp"), "ctx", None)
    mat, vec = P("fsdp", None), P("fsdp")
    params = (mat, vec, mat, vec, mat, vec, mat, vec, vec, vec, vec, vec)
    in_specs = (tok, P(("seq", "fsdp"), None)) + params + (tok,)
    return jax.shard_map(fused_body if fits(mesh) else body, mesh=mesh, in_specs=in_specs, out_specs=(tok, tok) + params, check_vma=False)
```

```python
import math

import jax
import jax.numpy as jnp
import numpy as np
from jax import lax
from jax.experimental import pallas as pl
from jax.experimental.pallas import tpu as pltpu
from jax.sharding import PartitionSpec as P

HEADS = 8
HEAD = 256
ROT = 64
BLK = 128
EPS = 1e-05
PLANE = ("seq", "ctx")
LOW = jnp.bfloat16
WIDE = jnp.float32


def dot_nn(left, right):
    return lax.dot_general(left, right, (((1,), (0,)), ((), ())), preferred_element_type=WIDE)


def dot_nt(left, right):
    return lax.dot_general(left, right, (((1,), (1,)), ((), ())), preferred_element_type=WIDE)


def dot_tn(left, right):
    return lax.dot_general(left, right, (((0,), (0,)), ((), ())), preferred_element_type=WIDE)


def batch_nn(left, right):
    return lax.dot_general(left, right, (((2,), (1,)), ((0,), (0,))), preferred_element_type=WIDE)


def batch_nt(left, right):
    return lax.dot_general(left, right, (((2,), (2,)), ((0,), (0,))), preferred_element_type=WIDE)


def batch_tn(left, right):
    return lax.dot_general(left, right, (((1,), (1,)), ((0,), (0,))), preferred_element_type=WIDE)


def standardise(values):
    middle = jnp.mean(values, -1, keepdims=True)
    centred = values - middle
    spread = jnp.mean(centred * centred, -1, keepdims=True)
    scale = lax.rsqrt(spread + EPS)
    return centred * scale, scale


def angles(positions):
    freqs = 10000.0 ** (-(jnp.arange(ROT // 2, dtype=WIDE) * 2.0 / ROT))
    turned = positions.astype(WIDE)[:, None] * freqs[None, :]
    return jnp.cos(turned), jnp.sin(turned)


def turn(values, cosine, sine):
    half = ROT // 2
    one, two, rest = values[..., :half], values[..., half:ROT], values[..., ROT:]
    return jnp.concatenate([one * cosine - two * sine, two * cosine + one * sine, rest], -1)


def gelu_pair(hidden):
    bell = 0.5 * (1.0 + lax.erf(hidden * (1.0 / math.sqrt(2.0))))
    slope = bell + hidden * jnp.exp(-0.5 * hidden * hidden) * (1.0 / math.sqrt(2.0 * math.pi))
    return hidden * bell, slope


def body(tokens, block_place, w_qkv, b_qkv, w_o_t, b_o, w_up, b_up, w_down_t, b_down,
         norm1_gain, norm1_shift, norm2_gain, norm2_shift, cotangent):
    seqs, ctxs, shards = lax.axis_size("seq"), lax.axis_size("ctx"), lax.axis_size("fsdp")
    peers = seqs * ctxs
    place = lax.axis_index("seq") * ctxs + lax.axis_index("ctx")
    own, width = tokens.shape[1:]
    hidden_all = w_up.shape[1]
    length = own * ctxs
    share = max(1, peers // HEADS)
    heads = max(1, HEADS // peers)
    own_seqs = seqs // share
    group = place // share
    first_seq = (place % share) * own_seqs
    cols = heads * HEAD
    hid = hidden_all // peers

    x_own = tokens[0].astype(WIDE)
    dy_own = cotangent[0]
    both = lax.all_gather(jnp.stack([tokens[0], dy_own]), PLANE, axis=0, tiled=False)
    x_all = both[:, 0].reshape(seqs * length, width)
    dy_all = both[:, 1].reshape(seqs * length, width)
    places = lax.all_gather(block_place[0], "seq", axis=0, tiled=False)

    small = (b_qkv, b_o, b_up, b_down, norm1_gain, norm1_shift, norm2_gain, norm2_shift)
    packed = lax.all_gather(jnp.concatenate(small), "fsdp", axis=0, tiled=False)
    unpacked, start = [], 0
    for part in small:
        size = part.shape[0]
        unpacked.append(packed[:, start : start + size].reshape(-1).astype(WIDE))
        start += size
    bias_qkv, bias_o, bias_up, bias_down, gain1, shift1, gain2, shift2 = unpacked

    def head_cols(values, kinds):
        rows = values.shape[0]
        split = values.reshape(rows, kinds, HEADS * HEAD)
        return lax.dynamic_slice_in_dim(split, group * cols, cols, 2).reshape(rows, kinds * cols)

    def hid_cols(values):
        return lax.dynamic_slice_in_dim(values, place * hid, hid, 1)

    own_cols = jnp.concatenate([head_cols(w_qkv, 3), head_cols(w_o_t, 1), hid_cols(w_up), hid_cols(w_down_t)], 1)
    weights = lax.all_gather(own_cols, "fsdp", axis=0, tiled=True)
    cut = 4 * cols
    m_qkv, m_o, m_up, m_down = weights[:, : 3 * cols], weights[:, 3 * cols : cut], weights[:, cut : cut + hid], weights[:, cut + hid :]
    own_bias_qkv = head_cols(bias_qkv[None], 3)
    own_bias_up = hid_cols(bias_up[None])

    x_hat, _ = standardise(x_all.astype(WIDE))
    a1 = (x_hat * gain1 + shift1).astype(LOW)
    a2 = (x_hat * gain2 + shift2).astype(LOW)

    rows = own_seqs * length
    a1_seq = lax.dynamic_slice_in_dim(a1, first_seq * length, rows, 0)
    dy_seq = lax.dynamic_slice_in_dim(dy_all, first_seq * length, rows, 0)
    positions = (places[:, :, None] * BLK + jnp.arange(BLK, dtype=jnp.int32)).reshape(seqs, length)
    positions = lax.dynamic_slice_in_dim(positions, first_seq, own_seqs, 0)
    cosine, sine = angles(positions.reshape(-1))
    cosine, sine = cosine[:, None], sine[:, None]
    qkv = dot_nn(a1_seq, m_qkv) + own_bias_qkv

    def to_heads(values):
        return values.reshape(own_seqs, length, heads, HEAD).transpose(0, 2, 1, 3).reshape(own_seqs * heads, length, HEAD)

    def from_heads(values):
        return values.reshape(own_seqs, heads, length, HEAD).transpose(0, 2, 1, 3).reshape(rows, cols)

    def turned(values):
        return turn(values.reshape(rows, heads, HEAD), cosine, sine).reshape(rows, cols)

    def turned_back(values):
        return turn(values.reshape(rows, heads, HEAD), cosine, -sine).reshape(rows, cols)

    q = to_heads(turned(qkv[:, :cols]).astype(LOW))
    k = to_heads(turned(qkv[:, cols : 2 * cols]).astype(LOW))
    v = to_heads(qkv[:, 2 * cols :].astype(LOW))
    scaling = 1.0 / math.sqrt(HEAD)
    kept = (positions[:, :, None] >= positions[:, None, :])[:, None]
    kept = jnp.broadcast_to(kept, (own_seqs, heads, length, length)).reshape(own_seqs * heads, length, length)
    scores = jnp.where(kept, batch_nt(q, k) * scaling, -1e30)
    expo = jnp.exp(scores - jnp.max(scores, -1, keepdims=True))
    p = expo / jnp.sum(expo, -1, keepdims=True)
    p_low = p.astype(LOW)
    attn = from_heads(batch_nn(p_low, v).astype(LOW))
    d_attn = to_heads(dot_nn(dy_seq, m_o).astype(LOW))
    dp = batch_nt(d_attn, v)
    ds = jnp.where(kept, p * (dp - jnp.sum(p * dp, -1, keepdims=True)), 0.0).astype(LOW)
    dq = from_heads(batch_nn(ds, k) * scaling)
    dk = from_heads(batch_tn(ds, q) * scaling)
    dv = from_heads(batch_tn(p_low, d_attn))
    d_qkv = jnp.concatenate([turned_back(dq), turned_back(dk), dv], 1).astype(LOW)

    g, slope = gelu_pair(dot_nn(a2, m_up) + own_bias_up)
    g = g.astype(LOW)
    d_h = (dot_nn(dy_all, m_down) * slope).astype(LOW)

    def onto(values, part):
        return lax.dynamic_update_slice_in_dim(values, lax.dynamic_slice_in_dim(values, first_seq * length, rows, 0) + part, first_seq * length, 0)

    out_part = onto(dot_nt(g, m_down), dot_nt(attn, m_o))
    u_part = onto(dot_nt(d_h, m_up) * gain2, dot_nt(d_qkv, m_qkv) * gain1)
    out_sum = lax.psum_scatter(out_part.astype(LOW), PLANE, scatter_dimension=0, tiled=True).astype(WIDE)
    u_sum = lax.psum_scatter(u_part.astype(LOW), PLANE, scatter_dimension=0, tiled=True).astype(WIDE)
    output = (x_own + out_sum + bias_o + bias_down).astype(LOW)[None]
    hat_own, scale_own = standardise(x_own)
    d_x = scale_own * (u_sum - jnp.mean(u_sum, -1, keepdims=True) - hat_own * jnp.mean(u_sum * hat_own, -1, keepdims=True))
    input_grad = (dy_own.astype(WIDE) + d_x).astype(LOW)[None]

    g_qkv = dot_tn(a1_seq, d_qkv)
    g_o = dot_tn(dy_seq, attn)
    g_up = dot_tn(a2, d_h)
    g_down = dot_tn(dy_all, g)
    gb_qkv = jnp.sum(d_qkv, 0, dtype=WIDE)
    gb_up = jnp.sum(d_h, 0, dtype=WIDE)
    wide_qkv, wide_up = m_qkv.astype(WIDE), m_up.astype(WIDE)
    d_gain1 = jnp.sum(wide_qkv * (g_qkv - shift1[:, None] * gb_qkv), 1) / gain1
    d_gain2 = jnp.sum(wide_up * (g_up - shift2[:, None] * gb_up), 1) / gain2
    d_shift1 = jnp.sum(wide_qkv * gb_qkv, 1)
    d_shift2 = jnp.sum(wide_up * gb_up, 1)
    full_qkv = lax.dynamic_update_slice(jnp.zeros((3, HEADS * HEAD), WIDE), gb_qkv.reshape(3, cols), (0, group * cols)).reshape(-1)
    full_up = lax.dynamic_update_slice(jnp.zeros((hidden_all,), WIDE), gb_up, (place * hid,))
    sums = lax.psum((full_qkv, jnp.sum(dy_own, 0, dtype=WIDE), full_up, d_gain1, d_shift1, d_gain2, d_shift2), PLANE + ("fsdp",))
    mine = lax.axis_index("fsdp")

    def own_share(values):
        size = values.shape[0] // shards
        return lax.dynamic_slice_in_dim(values, mine * size, size, 0)

    sums = [own_share(s) for s in sums]
    grads = jnp.concatenate([g_qkv, g_o, g_up, g_down], 1).astype(LOW)
    reduced = lax.psum_scatter(grads, "fsdp", scatter_dimension=0, tiled=True)
    gathered = lax.all_gather(reduced, PLANE, axis=0, tiled=False)
    rows_own = reduced.shape[0]

    def spread_heads(values, kinds):
        values = values.astype(WIDE).reshape(peers // share, share, rows_own, kinds, cols).sum(1)
        return values.transpose(1, 2, 0, 3).reshape(rows_own, kinds * HEADS * HEAD)

    def spread_hid(values):
        return values.transpose(1, 0, 2).reshape(rows_own, hidden_all).astype(WIDE)

    return (
        output,
        input_grad,
        spread_heads(gathered[:, :, : 3 * cols], 3),
        sums[0],
        spread_heads(gathered[:, :, 3 * cols : cut], 1),
        sums[1],
        spread_hid(gathered[:, :, cut : cut + hid]),
        sums[2],
        spread_hid(gathered[:, :, cut + hid :]),
        sums[1],
        sums[3],
        sums[4],
        sums[5],
        sums[6],
    )


MESH = pl.DeviceIdType.MESH
PIECES = 12
ROWS = 512
COLS = 256
WIDTH = 2048
TOK = 2048
OWN = 256
LENGTH = 1024
HOPS = 3
SLOTS = 36
RS_START = 18
RING = 6
LAST = RS_START + SLOTS + 7
SCALING = 1.0 / math.sqrt(HEAD)


def fits(mesh):
    return dict(mesh.shape) == {"seq": 2, "ctx": 4, "fsdp": 4}


def at(index, size):
    return pl.ds(pl.multiple_of(index * size, size), size)


def remote(source, target, sent, came, device):
    return pltpu.make_async_remote_copy(
        src_ref=source, dst_ref=target, send_sem=sent, recv_sem=came, device_id=device, device_id_type=MESH)


def layer_kernel(tokens, cotangent, w_qkv, w_o, w_up, w_down, vec_own, turns,
                 out, input_grad, small_out, gout, x_land, core_land, first_land, second_land,
                 w_all, act, x_buf, dy_buf, g_ring, landing, small, gb, tab, pos, rows, bias,
                 stage, vecs, places, pack, pack_z, pack_p, final,
                 load_sem, own_sem, ag_send, ag_recv, rs_send, rs_recv, red_sem, ga_send, ga_recv,
                 vec_send, vec_recv, pk_send, pk_recv, pp_send, pp_recv, core_send, core_recv, one_send, one_recv,
                 two_send, two_recv):
    y, c, z = lax.axis_index("seq"), lax.axis_index("ctx"), lax.axis_index("fsdp")
    core = lax.rem(c, 2)
    chip = c // 2
    place = y * 4 + c
    right, left = (y, c, jnp.minimum(z + 1, 3)), (y, c, jnp.maximum(z - 1, 0))
    c_x, c_core = lax.rem(c + 2, 4), c + 1 - 2 * core
    dev_x, dev_y, dev_c = (y, c_x, z), (1 - y, c, z), (y, c_core, z)
    place_x, place_y, place_d = y * 4 + c_x, (1 - y) * 4 + c, (1 - y) * 4 + c_x
    c_core_x = lax.rem(c_core + 2, 4)
    place_c, place_cx, place_cy, place_cd = y * 4 + c_core, y * 4 + c_core_x, (1 - y) * 4 + c_core, (1 - y) * 4 + c_core_x
    above = [(y, c, lax.rem(z + d, 4)) for d in (1, 2, 3)]
    beside = []
    for d in range(1, 8):
        other = lax.rem(place + d, 8)
        beside.append((other // 4, lax.rem(other, 4), z))
    lane = lax.broadcasted_iota(jnp.int32, (1, 128), 1)

    barrier = pltpu.get_barrier_semaphore()
    for device in above + beside:
        pl.semaphore_signal(barrier, inc=1, device_id=device, device_id_type=MESH)

    def own_piece(i):
        if i < 3:
            source = w_qkv.at[:, at(i * 8 + place, COLS)]
        elif i == 3:
            source = w_o.at[:, at(place, COLS)]
        else:
            source = (w_up if i % 2 == 0 else w_down).at[:, at(place * 4 + (i - 4) // 2, COLS)]
        return pltpu.make_async_copy(source, w_all.at[i, at(z, ROWS)], own_sem.at[i])

    loads = [
        pltpu.make_async_copy(tokens.at[0], x_land.at[place], load_sem.at[0]),
        pltpu.make_async_copy(cotangent.at[0], dy_buf.at[at(place, OWN)], load_sem.at[1]),
        pltpu.make_async_copy(vec_own, vecs.at[z], load_sem.at[2]),
        pltpu.make_async_copy(vec_own.at[pl.ds(8, 8)], places.at[y], load_sem.at[3]),
        pltpu.make_async_copy(turns, small.at[pl.ds(0, LENGTH)], load_sem.at[4]),
    ]
    for i in range(PIECES):
        own_piece(i).start()
    for load in loads:
        load.start()
    pl.semaphore_wait(barrier, 10)

    def gather(tag, source, target):
        def copy(k):
            sent, came = ga_send.at[tag, k], ga_recv.at[tag, k]
            if k == 0:
                return remote(source(0), target(place, 0), sent, came, dev_x)
            if k == 1:
                return remote(source(1), target(place, 1), sent, came, dev_x)
            if k == 2:
                return remote(source(1), target(place, 1), sent, came, dev_y)
            if k == 3:
                return remote(source(0), target(place, 0), sent, came, dev_y)
            if k == 4:
                return remote(source(None), target(place, None), sent, came, dev_c)
            if k == 5:
                return remote(target(place_x, 0), target(place_x, 0), sent, came, dev_y)
            if k == 6:
                return remote(target(place_y, 1), target(place_y, 1), sent, came, dev_x)
            which = (place_x, place_y, place_d)[k - 7]
            return remote(target(which, None), target(which, None), sent, came, dev_c)

        def arrived(k):
            spot = (
                (place_x, 0), (place_x, 1), (place_y, 1), (place_y, 0), (place_c, None),
                (place_d, 0), (place_d, 1), (place_cx, None), (place_cy, None), (place_cd, None),
            )[k]
            here = target(*spot)
            remote(here, here, ga_send.at[tag, k], ga_recv.at[tag, k], dev_c).wait_recv()

        def start():
            for k in (0, 2, 1, 3, 4):
                copy(k).start()

        def middle():
            arrived(0)
            copy(5).start()
            arrived(2)
            copy(6).start()

        def forward():
            arrived(1)
            copy(7).start()
            arrived(3)
            copy(8).start()

        def far():
            arrived(5)
            arrived(6)
            copy(9).start()

        def end():
            for k in (4, 7, 8, 9):
                arrived(k)
            for k in range(10):
                copy(k).wait_send()

        return start, middle, forward, far, end

    def half_of(ref, half, size):
        return ref if half is None else ref.at[pl.ds(half * size, size)]

    x_gather = gather(0, lambda half: half_of(tokens.at[0], half, 128), lambda who, half: half_of(x_land.at[who], half, 128))
    dy_gather = gather(
        1, lambda half: half_of(cotangent.at[0], half, 128),
        lambda who, half: dy_buf.at[at(who, OWN)] if half is None else dy_buf.at[at(who * 2 + half, 128)])
    x_gather[0]()

    def vec_copy(d):
        return remote(vec_own, vecs.at[z], vec_send.at[d], vec_recv.at[d], above[d])

    def place_copy():
        return remote(vec_own.at[pl.ds(8, 8)], places.at[y], vec_send.at[3], vec_recv.at[3], dev_y)

    for d in range(3):
        vec_copy(d).start()
    place_copy().start()
    for i in range(PIECES):
        own_piece(i).wait()

    def parts(s):
        return (s // 6) * 2 + s % 2, (s // 2) % 3

    def ag_copy(way, piece, hop, shard):
        block = w_all.at[piece, at(shard, ROWS)]
        return remote(block, block, ag_send.at[way, piece, hop], ag_recv.at[way, piece, hop], right if way == 0 else left)

    def ag_service(slot):
        before = slot - 2
        old, old_hop = parts(jnp.maximum(before, 0))
        live = (before >= 0) & (before < SLOTS)

        @pl.when(live & (z >= 1) & (z - 1 - old_hop >= 0))
        def _():
            ag_copy(0, old, old_hop, z - 1 - old_hop).wait_recv()

        @pl.when(live & (z <= 2) & (z + 1 + old_hop <= 3))
        def _():
            ag_copy(1, old, old_hop, z + 1 + old_hop).wait_recv()

        piece, hop = parts(jnp.minimum(slot, SLOTS - 1))
        later = (hop == 0) & (piece >= PIECES // 2)
        ahead = (slot < SLOTS // 2) & (hop == 2)

        @pl.when((slot < SLOTS) & (z <= 2) & (z - hop >= 0) & ~(later & (z <= 1)))
        def _():
            ag_copy(0, piece, hop, z - hop).start()

        @pl.when((slot < SLOTS) & (z >= 1) & (z + hop <= 3) & ~(later & (z >= 2)))
        def _():
            ag_copy(1, piece, hop, z + hop).start()

        @pl.when(ahead & (z <= 1))
        def _():
            ag_copy(0, piece + PIECES // 2, 0, z).start()

        @pl.when(ahead & (z >= 2))
        def _():
            ag_copy(1, piece + PIECES // 2, 0, z).start()

        @pl.when(live & (z <= 2) & (z - old_hop >= 0))
        def _():
            ag_copy(0, old, old_hop, z - old_hop).wait_send()

        @pl.when(live & (z >= 1) & (z + old_hop <= 3))
        def _():
            ag_copy(1, old, old_hop, z + old_hop).wait_send()

    def rs_piece(n):
        return jnp.where(n < 4, 3 - n, 4 + (n - 4) // 2 + 4 * (n % 2))

    def landing_slot(n, hop):
        return jnp.where(hop < 2, (n % 2) * 2 + hop, 4 + n % 4)

    def rs_copy(way, n, hop, shard):
        return remote(
            g_ring.at[n % RING, at(shard, ROWS)], landing.at[way, landing_slot(n, hop)],
            rs_send.at[way, n, hop], rs_recv.at[way, n, hop], right if way == 0 else left)

    def rs_add(way, n, hop, shard):
        rs_copy(way, n, hop, shard).wait_recv()
        block = g_ring.at[n % RING, at(shard, ROWS)]
        block[...] = (block[...].astype(WIDE) + landing[way, landing_slot(n, hop)].astype(WIDE)).astype(LOW)

    def red_copy(n):
        return pltpu.make_async_copy(g_ring.at[n % RING, at(z, ROWS)], gout.at[rs_piece(n), place], red_sem.at[n])

    def red_gather(n):
        piece = rs_piece(n)
        return gather(
            2 + n, lambda half: half_of(gout.at[piece, place], half, 256),
            lambda who, half: half_of(gout.at[piece, who], half, 256))

    def rs_service(slot):
        before = slot - 2
        old, old_hop = parts(jnp.clip(before, 0, SLOTS - 1))
        live = (before >= 0) & (before < SLOTS)

        @pl.when(live & (z >= 1) & (z - 1 <= old_hop))
        def _():
            rs_add(0, old, old_hop, z + 2 - old_hop)

        @pl.when(live & (z <= 2) & (2 - z <= old_hop))
        def _():
            rs_add(1, old, old_hop, z - 2 + old_hop)

        piece, hop = parts(jnp.clip(slot, 0, SLOTS - 1))
        sending = (slot >= 0) & (slot < SLOTS)

        @pl.when(sending & (z <= 2) & (z <= hop))
        def _():
            rs_copy(0, piece, hop, z + 3 - hop).start()

        @pl.when(sending & (z >= 1) & (3 - z <= hop))
        def _():
            rs_copy(1, piece, hop, z - 3 + hop).start()

        @pl.when(live & (z <= 2) & (z <= old_hop))
        def _():
            rs_copy(0, old, old_hop, z + 3 - old_hop).wait_send()

        @pl.when(live & (z >= 1) & (3 - z <= old_hop))
        def _():
            rs_copy(1, old, old_hop, z - 3 + old_hop).wait_send()

        @pl.when(live & (old_hop == 2))
        def _():
            red_copy(old).start()
            red_copy(old).wait()
            red_gather(old)[0]()

        for step, delay in ((1, 1), (2, 2), (3, 3), (4, 5)):
            begun = slot - delay
            n = jnp.clip((begun // 6) * 2 - 2 + begun % 6, 0, PIECES - 1)

            @pl.when((begun >= 6) & (begun < SLOTS + 6) & (begun % 6 < 2))
            def _(step=step, n=n):
                red_gather(n)[step]()

    def service(slot):
        if isinstance(slot, int):
            if slot < SLOTS + 2:
                ag_service(jnp.int32(slot))
            if slot >= RS_START:
                rs_service(jnp.int32(slot - RS_START))
        else:
            ag_service(slot)
            rs_service(slot - RS_START)

    def services(first, last, early=False):
        def step(slot, carry):
            ag_service(slot)
            if not early:
                rs_service(slot - RS_START)
            return carry

        lax.fori_loop(first, last, step, 0)

    def loop(count, body, first=None, ag=True, rs=True):
        def step(i, carry):
            if first is not None:
                if ag:
                    ag_service(first + i)
                if rs:
                    rs_service(first + i - RS_START)
            body(i)
            return carry

        lax.fori_loop(0, count, step, 0)

    services(0, 2, True)
    for load in loads[2:]:
        load.wait()
    for d in range(3):
        here = vecs.at[lax.rem(z + 3 - d, 4)]
        remote(here, here, vec_send.at[d], vec_recv.at[d], above[d]).wait_recv()
    other = places.at[1 - y]
    remote(other, other, vec_send.at[3], vec_recv.at[3], dev_y).wait_recv()
    for shard in range(4):
        here = pl.ds(shard * ROWS, ROWS)
        for k in range(4):
            rows[k : k + 1, here] = vecs[shard, 9 + k : 10 + k, :]
        rows[4:5, here] = vecs[shard, 3:4, :] + vecs[shard, 8:9, :]
        rows[5:8, here] = jnp.zeros((3, ROWS), WIDE)
    for kind in range(3):
        flat = kind * WIDTH + place * COLS
        bias[kind : kind + 1, :] = vecs[flat // 1536, pl.ds((flat % 1536) // 512, 1), at((flat % 512) // 256, COLS)]
    for part in range(4):
        flat = place * 1024 + part * COLS
        bias[3 + part : 4 + part, :] = vecs[flat // 2048, pl.ds(4 + (flat % 2048) // 512, 1), at((flat % 512) // 256, COLS)]

    def set_place(i, carry):
        seq, block = i // 8, i % 8
        value = jnp.sum(jnp.where(lane == block, places[seq, 5:6, 0:128], 0.0), 1, keepdims=True)
        made = jnp.zeros((BLK, 128), WIDE)
        for b in range(8):
            made = jnp.where(value == float(b), small[pl.ds(b * BLK, BLK), :], made)
        tab[at(i, BLK), :] = made
        pos[seq, :, at(block, BLK)] = jnp.broadcast_to(value * float(BLK) + lane.astype(WIDE), (8, BLK))
        return carry

    services(2, 3, True)
    lax.fori_loop(0, 16, set_place, 0)
    for shard in range(4):
        tall = jnp.concatenate([rows[:, pl.ds(shard * ROWS, ROWS)], jnp.zeros((120, ROWS), WIDE)], 0)
        small[pl.ds(shard * ROWS, ROWS), :] = jnp.transpose(tall)
    x_gather[1]()
    services(3, 5, True)
    x_gather[2]()
    dy_gather[0]()
    services(5, 7, True)
    x_gather[3]()
    services(7, 8, True)
    x_gather[4]()
    loads[0].wait()

    def norm_tile(which):
        def run(i):
            def part(n, carry):
                block = at(i * 4 + n, 64)
                centred, scale = standardise_rows(x_buf[block, :].astype(WIDE))
                x_buf[block, :] = (centred * scale * rows[2 * which : 2 * which + 1, :] + rows[2 * which + 1 : 2 * which + 2, :]).astype(LOW)
                return carry

            lax.fori_loop(0, 4, part, 0)
        return run

    def load_x():
        copies = [pltpu.make_async_copy(x_land.at[p], x_buf.at[pl.ds(p * OWN, OWN)], own_sem.at[p]) for p in range(8)]
        for copy in copies:
            copy.start()
        for copy in copies:
            copy.wait()

    def norm(which, first, rs):
        load_x()

        def body(i):
            for n in range(4):
                norm_tile(which)(4 * i + n)

        loop(2, body, first, rs=rs)

    norm(0, 8, False)
    dy_gather[1]()

    def turned(values, block, sign):
        entry = tab[block, :]
        cosine = jnp.where(lane < 32, entry, jnp.where(lane < 64, pltpu.roll(entry, 32, 1), 1.0))
        sine = jnp.where(lane < 32, -pltpu.roll(entry, 96, 1), jnp.where(lane < 64, entry, 0.0))
        low = values[:, :128]
        partner = jnp.where(lane < 32, pltpu.roll(low, 96, 1), pltpu.roll(low, 32, 1))
        return jnp.concatenate([low * cosine + partner * (sine * sign), values[:, 128:]], 1)

    def project(kind):
        def run(i):
            block = at(i, 512)
            made = dot_nn(x_buf[block, :], w_all[kind]) + bias[kind : kind + 1, :]
            if kind < 2:
                made = turned(made, block, 1.0)
            act[9 + kind, block, :] = made.astype(LOW)
        return run

    services(10, 11, True)
    loop(4, project(0))
    dy_gather[2]()
    services(11, 12, True)
    loop(4, project(1))
    services(12, 14, True)
    loop(4, project(2))
    dy_gather[3]()
    dy_gather[4]()
    loads[1].wait()

    def attend(i):
        seq = i // 4
        block, keys = at(i, 256), at(seq, LENGTH)

        q, k, v = act[9, block, :], act[10, keys, :], act[11, keys, :]
        kept = tab[block, 64:65] >= pos[seq, 0:1, :]
        scores = jnp.where(kept, dot_nt(q, k) * SCALING, -1e30)
        expo = jnp.exp(scores - jnp.max(scores, -1, keepdims=True))
        p = expo * (1.0 / jnp.sum(expo, -1, keepdims=True))
        p_low = p.astype(LOW)
        act[3, block, :] = dot_nn(p_low, v).astype(LOW)
        d_attn = dot_nn(dy_buf[block, :], w_all[3]).astype(LOW)
        dp = dot_nt(d_attn, v)
        ds = jnp.where(kept, p * (dp - jnp.sum(p * dp, -1, keepdims=True)), 0.0).astype(LOW)
        act[0, block, :] = turned(dot_nn(ds, k) * SCALING, block, -1.0).astype(LOW)
        act[8, block, :] = d_attn
        for n in range(4):
            g_ring[n, at(i % 4, 256), :] = ds[:, n * COLS : (n + 1) * COLS]
            g_ring[n, at(4 + i % 4, 256), :] = p_low[:, n * COLS : (n + 1) * COLS]

        @pl.when(i % 4 == 3)
        def _():
            def keyed(n, carry):
                mine = at(seq * 4 + n, COLS)
                d_keys = dot_tn(g_ring[n, 0:LENGTH, :], act[9, keys, :]) * SCALING
                act[1, mine, :] = turned(d_keys, mine, -1.0).astype(LOW)
                act[2, mine, :] = dot_tn(g_ring[n, LENGTH:, :], act[8, keys, :]).astype(LOW)
                return carry

            lax.fori_loop(0, 4, keyed, 0)

    def attend_two(i):
        def inner(n, carry):
            attend(2 * i + n)
            return carry

        lax.fori_loop(0, 2, inner, 0)

    loop(4, attend_two, 14, rs=False)

    def gradient(piece, n, source):
        summed = piece < 3 or (piece != 3 and piece % 2 == 0)
        if summed:
            gb[piece : piece + 1, :] = jnp.zeros((1, COLS), WIDE)

            def count(i, carry):
                gb[piece : piece + 1, :] += jnp.sum(act[piece, at(i, 256), :].astype(WIDE), 0, keepdims=True)
                return carry

            lax.fori_loop(0, 8, count, 0)

        def part(s, carry):
            block = at(s, ROWS)
            made = dot_tn(source[:, block], act[piece])
            g_ring[n % RING, block, :] = made.astype(LOW)
            if summed:
                mine = 0 if piece < 3 else 1
                weight = w_all[piece, block, :].astype(WIDE)
                sums = gb[piece : piece + 1, :]
                gain = jnp.sum(weight * (made - small[block, 2 * mine + 1 : 2 * mine + 2] * sums), 1, keepdims=True)
                shift = jnp.sum(weight * sums, 1, keepdims=True)
                here = 8 + 2 * mine
                old = small[block, :]
                small[block, :] = old + jnp.where(lane == here, gain, 0.0) + jnp.where(lane == here + 1, shift, 0.0)
            return carry

        lax.fori_loop(0, 4, part, 0)

    rows[5:6, :] = jnp.sum(dy_buf[at(place, OWN), :].astype(WIDE), 0, keepdims=True)
    gradient(3, 0, dy_buf)
    service(18)
    gradient(2, 1, x_buf)
    service(19)
    gradient(1, 2, x_buf)
    service(20)
    gradient(0, 3, x_buf)
    service(21)
    norm(1, 22, True)

    def feed(part):
        up, down = 4 + 2 * part, 5 + 2 * part

        def run(i):
            for n in range(2):
                block = at(2 * i + n, 512)
                hidden = dot_nn(x_buf[block, :], w_all[up]) + bias[3 + part : 4 + part, :]
                d_gelu = dot_nn(dy_buf[block, :], w_all[down])
                made, slope = gelu_pair(hidden)
                act[down, block, :] = made.astype(LOW)
                act[up, block, :] = (d_gelu * slope).astype(LOW)
        return run

    slot = 24
    for part in range(3):
        loop(2, feed(part), slot)
        slot += 2
        gradient(4 + 2 * part, 4 + 2 * part, x_buf)
        service(slot)
        gradient(5 + 2 * part, 5 + 2 * part, dy_buf)
        service(slot + 1)
        slot += 2
    services(36, 38)
    loop(2, feed(3), 38)
    gradient(10, 10, x_buf)
    service(40)

    def make_pack():
        for shard in range(4):
            here = pl.ds(shard * ROWS, ROWS)
            flat = jnp.transpose(small[here, :])
            pack[shard, 0:1, :] = flat[8:9] / rows[0:1, here]
            pack[shard, 1:2, :] = flat[9:10]
            pack[shard, 2:3, :] = flat[10:11] / rows[2:3, here]
            pack[shard, 3:4, :] = flat[11:12]
            pack[shard, 4:5, :] = rows[5:6, here]
            pack[shard, 5:8, :] = jnp.zeros((3, ROWS), WIDE)
            pack[shard, 8:16, :] = jnp.zeros((8, ROWS), WIDE)
            for kind in range(3):
                pack[shard, 8 + kind : 9 + kind, :COLS] = gb[kind : kind + 1, :]
            for part in range(4):
                pack[shard, 11 + part : 12 + part, :COLS] = gb[4 + 2 * part : 5 + 2 * part, :]
        pack_z[z] = pack[z]

    def pack_copy(d):
        return remote(pack.at[lax.rem(z + d + 1, 4)], pack_z.at[z], pk_send.at[d], pk_recv.at[d], above[d])

    def peer_copy(d):
        return remote(pack_p.at[place], pack_p.at[place], pp_send.at[d], pp_recv.at[d], beside[d])

    def sum_start():
        for d in range(3):
            pack_copy(d).start()

    def sum_z():
        for d in range(3):
            here = pack_z.at[lax.rem(z + 3 - d, 4)]
            remote(here, here, pk_send.at[d], pk_recv.at[d], above[d]).wait_recv()
        pack_p[place] = pack_z[0] + pack_z[1] + pack_z[2] + pack_z[3]
        for d in range(7):
            peer_copy(d).start()

    def sum_plane():
        for d in range(7):
            here = pack_p.at[lax.rem(place + 7 - d, 8)]
            remote(here, here, pp_send.at[d], pp_recv.at[d], beside[d]).wait_recv()
        total = pack_p[0, 0:8, :]
        for p in range(1, 8):
            total = total + pack_p[p, 0:8, :]
        final[:, 0:ROWS] = total
        final[:, ROWS:] = jnp.zeros((8, 2 * COLS), WIDE)
        for r in range(6):
            flat = 6 * z + r
            final[r : r + 1, ROWS : ROWS + COLS] = pack_p[flat % 8, pl.ds(8 + flat // 8, 1), 0:COLS]
        for r in range(8):
            final[r : r + 1, ROWS + COLS :] = pack_p[2 * z + r // 4, 11 + r % 4 : 12 + r % 4, 0:COLS]

    tiles = {"d": (1 - y) * 2 + 1 - chip, "x": y * 2 + 1 - chip, "y": (1 - y) * 2 + chip, "own": y * 2 + chip}
    order = ("d", "x", "y", "own")
    both = (x_buf, dy_buf)

    def finish(name, whose, a):
        block = block_of(name, whose)

        def run(i, carry):
            columns = at(i, 512)

            def total(pieces):
                return sum(dot_nt(act[piece, block, :], w_all[piece, columns, :]) for piece in pieces)

            if a == 0:
                x_buf[block, columns] = total((3, 5, 7, 9, 11)).astype(LOW)
            else:
                first = total((0, 1, 2)) * rows[0:1, columns]
                dy_buf[block, columns] = (first + total((4, 6, 8, 10)) * rows[2:3, columns]).astype(LOW)
            return carry

        lax.fori_loop(0, 4, run, 0)

    def block_of(name, whose):
        return at(tiles[name] * 2 + whose, OWN)

    def half_rows(name, half):
        return at(tiles[name] * 4 + core * 2 + half, 128)

    def core_copy(name, a):
        i = order.index(name)
        return remote(both[a].at[block_of(name, 1 - core)], core_land.at[i, a], core_send.at[i, a], core_recv.at[i, a], dev_c)

    def first_copy(i, a):
        name, half, device = (("d", 0, dev_x), ("d", 1, dev_y), ("x", 0, dev_x), ("y", 1, dev_y))[i]
        return remote(both[a].at[half_rows(name, half)], first_land.at[i, a], one_send.at[i, a], one_recv.at[i, a], device)

    def second_copy(i, a):
        name, half, device = (("y", 0, dev_y), ("x", 1, dev_x))[i]
        return remote(both[a].at[half_rows(name, half)], second_land.at[i, a], two_send.at[i, a], two_recv.at[i, a], device)

    def fetch(source, a):
        return pltpu.make_async_copy(source, stage.at[a], load_sem.at[a])

    def add_in(copy, source, spots, a):
        copy.wait_recv()
        for half, spot in enumerate(spots):
            fetch(source.at[pl.ds(half * 128, 128)], a).start()
            fetch(source.at[pl.ds(half * 128, 128)], a).wait()
            both[a][spot, :] = (both[a][spot, :].astype(WIDE) + stage[a].astype(WIDE)).astype(LOW)

    def core_add(name, a):
        i = order.index(name)
        add_in(core_copy(name, a), core_land.at[i, a], [half_rows(name, 0), half_rows(name, 1)], a)

    def first_add(i, a):
        name, half = (("y", 0), ("x", 1), ("own", 0), ("own", 1))[i]
        add_in(first_copy(i, a), first_land.at[i, a], [half_rows(name, half)], a)

    def second_add(i, a):
        add_in(second_copy(i, a), second_land.at[i, a], [half_rows("own", i)], a)

    def pass_on(a):
        for i in range(2):
            first_add(i, a)
            second_copy(i, a).start()

    def spread(a, slots):
        for i, name in enumerate(order):
            finish(name, 1 - core, a)
            core_copy(name, a).start()
            if i == 1:
                core_add("d", a)
                first_copy(0, a).start()
                first_copy(1, a).start()
            elif i > 1:
                core_add(order[i - 1], a)
                first_copy(i, a).start()
            finish(name, core, a)
            if slots[i] is not None:
                service(slots[i])

    spread(0, (41, None, 42, None))
    gradient(11, 11, dy_buf)
    service(43)
    make_pack()
    sum_start()
    core_add("own", 0)
    spread(1, (44, 45, 46, 47))
    core_add("own", 1)
    pass_on(0)
    sum_z()
    services(48, 50)
    first_add(2, 0)
    first_add(3, 0)
    service(50)
    pass_on(1)
    services(51, 53)
    sum_plane()
    second_add(0, 0)
    second_add(1, 0)
    first_add(2, 1)
    first_add(3, 1)
    services(53, 56)
    second_add(0, 1)
    second_add(1, 1)

    for half in range(2):
        given = [tokens.at[0, pl.ds(half * 128, 128)], cotangent.at[0, pl.ds(half * 128, 128)]]
        for a in range(2):
            fetch(given[a], a).start()
        for a in range(2):
            fetch(given[a], a).wait()

        def emit(i, carry, half=half):
            here, mine = at(i, 64), at(place * 4 + half * 2 + i, 64)
            inputs = stage[0, here, :].astype(WIDE)
            x_buf[mine, :] = (inputs + x_buf[mine, :].astype(WIDE) + rows[4:5, :]).astype(LOW)
            centred, scale = standardise_rows(inputs)
            hat = centred * scale
            u = dy_buf[mine, :].astype(WIDE)
            inner = jnp.mean(u * hat, -1, keepdims=True)
            d_x = scale * (u - jnp.mean(u, -1, keepdims=True) - hat * inner)
            dy_buf[mine, :] = (stage[1, here, :].astype(WIDE) + d_x).astype(LOW)
            return carry

        lax.fori_loop(0, 2, emit, 0)
    ends = [
        pltpu.make_async_copy(x_buf.at[at(place, OWN)], out, load_sem.at[0]),
        pltpu.make_async_copy(dy_buf.at[at(place, OWN)], input_grad, load_sem.at[1]),
        pltpu.make_async_copy(final, small_out, load_sem.at[2]),
    ]
    for end in ends:
        end.start()
    services(56, LAST)
    for end in ends:
        end.wait()
    for d in range(3):
        vec_copy(d).wait_send()
        pack_copy(d).wait_send()
    place_copy().wait_send()
    for d in range(7):
        peer_copy(d).wait_send()
    for a in range(2):
        for name in order:
            core_copy(name, a).wait_send()
        for i in range(4):
            first_copy(i, a).wait_send()
        for i in range(2):
            second_copy(i, a).wait_send()


def standardise_rows(values):
    middle = jnp.mean(values, -1, keepdims=True)
    centred = values - middle
    spread = jnp.mean(centred * centred, -1, keepdims=True)
    return centred, lax.rsqrt(spread + EPS)


def layer_call(*operands):
    anywhere = pl.BlockSpec(memory_space=pltpu.HBM)
    shape = jax.ShapeDtypeStruct
    dma = pltpu.SemaphoreType.DMA
    out_shape = (
        shape((OWN, WIDTH), LOW),
        shape((OWN, WIDTH), LOW),
        shape((8, 1024), WIDE),
        shape((PIECES, 8, ROWS, COLS), LOW),
        shape((8, OWN, WIDTH), LOW),
        shape((4, 2, OWN, WIDTH), LOW),
        shape((4, 2, 128, WIDTH), LOW),
        shape((2, 2, 128, WIDTH), LOW),
    )
    return pl.pallas_call(
        layer_kernel,
        out_shape=out_shape,
        in_specs=[anywhere] * len(operands),
        out_specs=[anywhere] * len(out_shape),
        scratch_shapes=[
            pltpu.VMEM((PIECES, WIDTH, COLS), LOW),
            pltpu.VMEM((PIECES, TOK, COLS), LOW),
            pltpu.VMEM((TOK, WIDTH), LOW),
            pltpu.VMEM((TOK, WIDTH), LOW),
            pltpu.VMEM((RING, WIDTH, COLS), LOW),
            pltpu.VMEM((2, 8, ROWS, COLS), LOW),
            pltpu.VMEM((WIDTH, 128), WIDE),
            pltpu.VMEM((16, COLS), WIDE),
            pltpu.VMEM((TOK, 128), WIDE),
            pltpu.VMEM((2, 8, LENGTH), WIDE),
            pltpu.VMEM((8, WIDTH), WIDE),
            pltpu.VMEM((8, COLS), WIDE),
            pltpu.VMEM((2, 128, WIDTH), LOW),
            pltpu.VMEM((4, 16, ROWS), WIDE),
            pltpu.VMEM((2, 8, ROWS), WIDE),
            pltpu.VMEM((4, 16, ROWS), WIDE),
            pltpu.VMEM((4, 16, ROWS), WIDE),
            pltpu.VMEM((8, 16, ROWS), WIDE),
            pltpu.VMEM((8, 1024), WIDE),
            dma((5,)),
            dma((PIECES,)),
            dma((2, PIECES, HOPS)),
            dma((2, PIECES, HOPS)),
            dma((2, PIECES, HOPS)),
            dma((2, PIECES, HOPS)),
            dma((PIECES,)),
            dma((2 + PIECES, 10)),
            dma((2 + PIECES, 10)),
            dma((4,)),
            dma((4,)),
            dma((3,)),
            dma((3,)),
            dma((7,)),
            dma((7,)),
            dma((4, 2)),
            dma((4, 2)),
            dma((4, 2)),
            dma((4, 2)),
            dma((2, 2)),
            dma((2, 2)),
        ],
        compiler_params=pltpu.CompilerParams(collective_id=0, has_side_effects=True, vmem_limit_bytes=61 * 1024 * 1024),
    )(*operands)


DEPTH = 8


def widen_kernel(gathered, g_qkv, g_o, g_up, g_down, low, wide, low_sem, wide_sem):
    def load(i):
        return pltpu.make_async_copy(gathered.at[i // 8, i % 8], low.at[i % DEPTH], low_sem.at[i % DEPTH])

    def store(i, act):
        piece, p = i // 8, i % 8

        def copy(target):
            act(pltpu.make_async_copy(wide.at[i % DEPTH], target, wide_sem.at[i % DEPTH]))

        @pl.when(piece < 3)
        def _():
            copy(g_qkv.at[:, at(jnp.minimum(i, 23), COLS)])

        @pl.when(piece == 3)
        def _():
            copy(g_o.at[:, at(p, COLS)])

        @pl.when((piece >= 4) & (piece < 8))
        def _():
            copy(g_up.at[:, at(p * 4 + jnp.clip(piece - 4, 0, 3), COLS)])

        @pl.when(piece >= 8)
        def _():
            copy(g_down.at[:, at(p * 4 + jnp.clip(piece - 8, 0, 3), COLS)])

    def first(i, carry):
        load(i).start()
        return carry

    def step(i, carry):
        load(i).wait()

        @pl.when(i >= DEPTH)
        def _():
            store(i - DEPTH, lambda copy: copy.wait())

        wide[i % DEPTH] = low[i % DEPTH].astype(WIDE)
        store(i, lambda copy: copy.start())

        @pl.when(i + DEPTH < 96)
        def _():
            load(i + DEPTH).start()

        return carry

    def last(i, carry):
        store(i, lambda copy: copy.wait())
        return carry

    lax.fori_loop(0, DEPTH, first, 0)
    lax.fori_loop(0, 96, step, 0)
    lax.fori_loop(96 - DEPTH, 96, last, 0)


def widen(gathered):
    shape = jax.ShapeDtypeStruct
    anywhere = pl.BlockSpec(memory_space=pltpu.HBM)
    return pl.pallas_call(
        widen_kernel,
        in_specs=[anywhere],
        out_specs=[anywhere] * 4,
        out_shape=(shape((ROWS, 3 * WIDTH), WIDE), shape((ROWS, WIDTH), WIDE), shape((ROWS, 4 * WIDTH), WIDE), shape((ROWS, 4 * WIDTH), WIDE)),
        scratch_shapes=[
            pltpu.VMEM((DEPTH, ROWS, COLS), LOW),
            pltpu.VMEM((DEPTH, ROWS, COLS), WIDE),
            pltpu.SemaphoreType.DMA((DEPTH,)),
            pltpu.SemaphoreType.DMA((DEPTH,)),
        ],
        compiler_params=pltpu.CompilerParams(vmem_limit_bytes=24 * 1024 * 1024),
    )(gathered)


def turn_table():
    where = np.arange(LENGTH, dtype=np.float32)[:, None]
    freqs = np.float32(10000.0) ** (-(np.arange(ROT // 2, dtype=np.float32) * np.float32(2.0 / ROT)))
    turned = (where * freqs[None, :]).astype(np.float32)
    return np.concatenate([np.cos(turned), np.sin(turned), np.broadcast_to(where, (LENGTH, 64))], 1).astype(np.float32)


def fused_body(tokens, block_place, w_qkv, b_qkv, w_o_t, b_o, w_up, b_up, w_down_t, b_down,
               norm1_gain, norm1_shift, norm2_gain, norm2_shift, cotangent):
    given = (b_qkv, b_o, b_up, b_down, norm1_gain, norm1_shift, norm2_gain, norm2_shift)
    spots = jnp.pad(block_place.astype(WIDE), ((0, 0), (0, ROWS - 8)))
    vec = jnp.concatenate([part.astype(WIDE).reshape(-1, ROWS) for part in given] + [spots, jnp.zeros((2, ROWS), WIDE)])
    turns = jnp.asarray(turn_table())
    results = layer_call(tokens, cotangent, w_qkv, w_o_t, w_up, w_down_t, vec, turns)
    output, input_grad, sums, gathered = results[:4]
    g_qkv, g_o, g_up, g_down = widen(gathered)
    grad_bias = sums[4, :ROWS]
    return (
        output[None],
        input_grad[None],
        g_qkv,
        sums[:6, ROWS : ROWS + COLS].reshape(-1),
        g_o,
        grad_bias,
        g_up,
        sums[:, ROWS + COLS :].reshape(-1),
        g_down,
        grad_bias,
        sums[0, :ROWS],
        sums[1, :ROWS],
        sums[2, :ROWS],
        sums[3, :ROWS],
    )


def solution(mesh):
    tok = P(("seq", "fsdp"), "ctx", None)
    mat, vec = P("fsdp", None), P("fsdp")
    params = (mat, vec, mat, vec, mat, vec, mat, vec, vec, vec, vec, vec)
    in_specs = (tok, P(("seq", "fsdp"), None)) + params + (tok,)
    return jax.shard_map(fused_body if fits(mesh) else body, mesh=mesh, in_specs=in_specs, out_specs=(tok, tok) + params, check_vma=False)
```

```python
import math

import jax
import jax.numpy as jnp
import numpy as np
from jax import lax
from jax.experimental import pallas as pl
from jax.experimental.pallas import tpu as pltpu
from jax.sharding import PartitionSpec as P

HEADS = 8
HEAD = 256
ROT = 64
BLK = 128
EPS = 1e-05
PLANE = ("seq", "ctx")
LOW = jnp.bfloat16
WIDE = jnp.float32


def dot_nn(left, right):
    return lax.dot_general(left, right, (((1,), (0,)), ((), ())), preferred_element_type=WIDE)


def dot_nt(left, right):
    return lax.dot_general(left, right, (((1,), (1,)), ((), ())), preferred_element_type=WIDE)


def dot_tn(left, right):
    return lax.dot_general(left, right, (((0,), (0,)), ((), ())), preferred_element_type=WIDE)


def batch_nn(left, right):
    return lax.dot_general(left, right, (((2,), (1,)), ((0,), (0,))), preferred_element_type=WIDE)


def batch_nt(left, right):
    return lax.dot_general(left, right, (((2,), (2,)), ((0,), (0,))), preferred_element_type=WIDE)


def batch_tn(left, right):
    return lax.dot_general(left, right, (((1,), (1,)), ((0,), (0,))), preferred_element_type=WIDE)


def standardise(values):
    middle = jnp.mean(values, -1, keepdims=True)
    centred = values - middle
    spread = jnp.mean(centred * centred, -1, keepdims=True)
    scale = lax.rsqrt(spread + EPS)
    return centred * scale, scale


def angles(positions):
    freqs = 10000.0 ** (-(jnp.arange(ROT // 2, dtype=WIDE) * 2.0 / ROT))
    turned = positions.astype(WIDE)[:, None] * freqs[None, :]
    return jnp.cos(turned), jnp.sin(turned)


def turn(values, cosine, sine):
    half = ROT // 2
    one, two, rest = values[..., :half], values[..., half:ROT], values[..., ROT:]
    return jnp.concatenate([one * cosine - two * sine, two * cosine + one * sine, rest], -1)


def gelu_pair(hidden):
    bell = 0.5 * (1.0 + lax.erf(hidden * (1.0 / math.sqrt(2.0))))
    slope = bell + hidden * jnp.exp(-0.5 * hidden * hidden) * (1.0 / math.sqrt(2.0 * math.pi))
    return hidden * bell, slope


def body(tokens, block_place, w_qkv, b_qkv, w_o_t, b_o, w_up, b_up, w_down_t, b_down,
         norm1_gain, norm1_shift, norm2_gain, norm2_shift, cotangent):
    seqs, ctxs, shards = lax.axis_size("seq"), lax.axis_size("ctx"), lax.axis_size("fsdp")
    peers = seqs * ctxs
    place = lax.axis_index("seq") * ctxs + lax.axis_index("ctx")
    own, width = tokens.shape[1:]
    hidden_all = w_up.shape[1]
    length = own * ctxs
    share = max(1, peers // HEADS)
    heads = max(1, HEADS // peers)
    own_seqs = seqs // share
    group = place // share
    first_seq = (place % share) * own_seqs
    cols = heads * HEAD
    hid = hidden_all // peers

    x_own = tokens[0].astype(WIDE)
    dy_own = cotangent[0]
    both = lax.all_gather(jnp.stack([tokens[0], dy_own]), PLANE, axis=0, tiled=False)
    x_all = both[:, 0].reshape(seqs * length, width)
    dy_all = both[:, 1].reshape(seqs * length, width)
    places = lax.all_gather(block_place[0], "seq", axis=0, tiled=False)

    small = (b_qkv, b_o, b_up, b_down, norm1_gain, norm1_shift, norm2_gain, norm2_shift)
    packed = lax.all_gather(jnp.concatenate(small), "fsdp", axis=0, tiled=False)
    unpacked, start = [], 0
    for part in small:
        size = part.shape[0]
        unpacked.append(packed[:, start : start + size].reshape(-1).astype(WIDE))
        start += size
    bias_qkv, bias_o, bias_up, bias_down, gain1, shift1, gain2, shift2 = unpacked

    def head_cols(values, kinds):
        rows = values.shape[0]
        split = values.reshape(rows, kinds, HEADS * HEAD)
        return lax.dynamic_slice_in_dim(split, group * cols, cols, 2).reshape(rows, kinds * cols)

    def hid_cols(values):
        return lax.dynamic_slice_in_dim(values, place * hid, hid, 1)

    own_cols = jnp.concatenate([head_cols(w_qkv, 3), head_cols(w_o_t, 1), hid_cols(w_up), hid_cols(w_down_t)], 1)
    weights = lax.all_gather(own_cols, "fsdp", axis=0, tiled=True)
    cut = 4 * cols
    m_qkv, m_o, m_up, m_down = weights[:, : 3 * cols], weights[:, 3 * cols : cut], weights[:, cut : cut + hid], weights[:, cut + hid :]
    own_bias_qkv = head_cols(bias_qkv[None], 3)
    own_bias_up = hid_cols(bias_up[None])

    x_hat, _ = standardise(x_all.astype(WIDE))
    a1 = (x_hat * gain1 + shift1).astype(LOW)
    a2 = (x_hat * gain2 + shift2).astype(LOW)

    rows = own_seqs * length
    a1_seq = lax.dynamic_slice_in_dim(a1, first_seq * length, rows, 0)
    dy_seq = lax.dynamic_slice_in_dim(dy_all, first_seq * length, rows, 0)
    positions = (places[:, :, None] * BLK + jnp.arange(BLK, dtype=jnp.int32)).reshape(seqs, length)
    positions = lax.dynamic_slice_in_dim(positions, first_seq, own_seqs, 0)
    cosine, sine = angles(positions.reshape(-1))
    cosine, sine = cosine[:, None], sine[:, None]
    qkv = dot_nn(a1_seq, m_qkv) + own_bias_qkv

    def to_heads(values):
        return values.reshape(own_seqs, length, heads, HEAD).transpose(0, 2, 1, 3).reshape(own_seqs * heads, length, HEAD)

    def from_heads(values):
        return values.reshape(own_seqs, heads, length, HEAD).transpose(0, 2, 1, 3).reshape(rows, cols)

    def turned(values):
        return turn(values.reshape(rows, heads, HEAD), cosine, sine).reshape(rows, cols)

    def turned_back(values):
        return turn(values.reshape(rows, heads, HEAD), cosine, -sine).reshape(rows, cols)

    q = to_heads(turned(qkv[:, :cols]).astype(LOW))
    k = to_heads(turned(qkv[:, cols : 2 * cols]).astype(LOW))
    v = to_heads(qkv[:, 2 * cols :].astype(LOW))
    scaling = 1.0 / math.sqrt(HEAD)
    kept = (positions[:, :, None] >= positions[:, None, :])[:, None]
    kept = jnp.broadcast_to(kept, (own_seqs, heads, length, length)).reshape(own_seqs * heads, length, length)
    scores = jnp.where(kept, batch_nt(q, k) * scaling, -1e30)
    expo = jnp.exp(scores - jnp.max(scores, -1, keepdims=True))
    p = expo / jnp.sum(expo, -1, keepdims=True)
    p_low = p.astype(LOW)
    attn = from_heads(batch_nn(p_low, v).astype(LOW))
    d_attn = to_heads(dot_nn(dy_seq, m_o).astype(LOW))
    dp = batch_nt(d_attn, v)
    ds = jnp.where(kept, p * (dp - jnp.sum(p * dp, -1, keepdims=True)), 0.0).astype(LOW)
    dq = from_heads(batch_nn(ds, k) * scaling)
    dk = from_heads(batch_tn(ds, q) * scaling)
    dv = from_heads(batch_tn(p_low, d_attn))
    d_qkv = jnp.concatenate([turned_back(dq), turned_back(dk), dv], 1).astype(LOW)

    g, slope = gelu_pair(dot_nn(a2, m_up) + own_bias_up)
    g = g.astype(LOW)
    d_h = (dot_nn(dy_all, m_down) * slope).astype(LOW)

    def onto(values, part):
        return lax.dynamic_update_slice_in_dim(values, lax.dynamic_slice_in_dim(values, first_seq * length, rows, 0) + part, first_seq * length, 0)

    out_part = onto(dot_nt(g, m_down), dot_nt(attn, m_o))
    u_part = onto(dot_nt(d_h, m_up) * gain2, dot_nt(d_qkv, m_qkv) * gain1)
    out_sum = lax.psum_scatter(out_part.astype(LOW), PLANE, scatter_dimension=0, tiled=True).astype(WIDE)
    u_sum = lax.psum_scatter(u_part.astype(LOW), PLANE, scatter_dimension=0, tiled=True).astype(WIDE)
    output = (x_own + out_sum + bias_o + bias_down).astype(LOW)[None]
    hat_own, scale_own = standardise(x_own)
    d_x = scale_own * (u_sum - jnp.mean(u_sum, -1, keepdims=True) - hat_own * jnp.mean(u_sum * hat_own, -1, keepdims=True))
    input_grad = (dy_own.astype(WIDE) + d_x).astype(LOW)[None]

    g_qkv = dot_tn(a1_seq, d_qkv)
    g_o = dot_tn(dy_seq, attn)
    g_up = dot_tn(a2, d_h)
    g_down = dot_tn(dy_all, g)
    gb_qkv = jnp.sum(d_qkv, 0, dtype=WIDE)
    gb_up = jnp.sum(d_h, 0, dtype=WIDE)
    wide_qkv, wide_up = m_qkv.astype(WIDE), m_up.astype(WIDE)
    d_gain1 = jnp.sum(wide_qkv * (g_qkv - shift1[:, None] * gb_qkv), 1) / gain1
    d_gain2 = jnp.sum(wide_up * (g_up - shift2[:, None] * gb_up), 1) / gain2
    d_shift1 = jnp.sum(wide_qkv * gb_qkv, 1)
    d_shift2 = jnp.sum(wide_up * gb_up, 1)
    full_qkv = lax.dynamic_update_slice(jnp.zeros((3, HEADS * HEAD), WIDE), gb_qkv.reshape(3, cols), (0, group * cols)).reshape(-1)
    full_up = lax.dynamic_update_slice(jnp.zeros((hidden_all,), WIDE), gb_up, (place * hid,))
    sums = lax.psum((full_qkv, jnp.sum(dy_own, 0, dtype=WIDE), full_up, d_gain1, d_shift1, d_gain2, d_shift2), PLANE + ("fsdp",))
    mine = lax.axis_index("fsdp")

    def own_share(values):
        size = values.shape[0] // shards
        return lax.dynamic_slice_in_dim(values, mine * size, size, 0)

    sums = [own_share(s) for s in sums]
    grads = jnp.concatenate([g_qkv, g_o, g_up, g_down], 1).astype(LOW)
    reduced = lax.psum_scatter(grads, "fsdp", scatter_dimension=0, tiled=True)
    gathered = lax.all_gather(reduced, PLANE, axis=0, tiled=False)
    rows_own = reduced.shape[0]

    def spread_heads(values, kinds):
        values = values.astype(WIDE).reshape(peers // share, share, rows_own, kinds, cols).sum(1)
        return values.transpose(1, 2, 0, 3).reshape(rows_own, kinds * HEADS * HEAD)

    def spread_hid(values):
        return values.transpose(1, 0, 2).reshape(rows_own, hidden_all).astype(WIDE)

    return (
        output,
        input_grad,
        spread_heads(gathered[:, :, : 3 * cols], 3),
        sums[0],
        spread_heads(gathered[:, :, 3 * cols : cut], 1),
        sums[1],
        spread_hid(gathered[:, :, cut : cut + hid]),
        sums[2],
        spread_hid(gathered[:, :, cut + hid :]),
        sums[1],
        sums[3],
        sums[4],
        sums[5],
        sums[6],
    )


MESH = pl.DeviceIdType.MESH
PIECES = 12
ROWS = 512
COLS = 256
WIDTH = 2048
TOK = 2048
OWN = 256
LENGTH = 1024
HOPS = 3
SLOTS = 36
RS_START = 17
RING = 6
HOLD = 4
LAST = RS_START + SLOTS + 7
SCALING = 1.0 / math.sqrt(HEAD)


def fits(mesh):
    return dict(mesh.shape) == {"seq": 2, "ctx": 4, "fsdp": 4}


def at(index, size):
    return pl.ds(pl.multiple_of(index * size, size), size)


def remote(source, target, sent, came, device):
    return pltpu.make_async_remote_copy(
        src_ref=source, dst_ref=target, send_sem=sent, recv_sem=came, device_id=device, device_id_type=MESH)


def layer_kernel(tokens, cotangent, w_qkv, w_o, w_up, w_down, vec_own, turns,
                 out, input_grad, small_out, gout, x_land, core_land, first_land, second_land,
                 w_all, act, x_buf, dy_buf, g_ring, landing, small, gb, tab, pos, rows, bias,
                 stage, vecs, places, pack, pack_z, pack_p, final,
                 load_sem, own_sem, ag_send, ag_recv, rs_send, rs_recv, red_sem, ga_send, ga_recv,
                 vec_send, vec_recv, pk_send, pk_recv, pp_send, pp_recv, core_send, core_recv, one_send, one_recv,
                 two_send, two_recv):
    y, c, z = lax.axis_index("seq"), lax.axis_index("ctx"), lax.axis_index("fsdp")
    core = lax.rem(c, 2)
    chip = c // 2
    place = y * 4 + c
    right, left = (y, c, jnp.minimum(z + 1, 3)), (y, c, jnp.maximum(z - 1, 0))
    c_x, c_core = lax.rem(c + 2, 4), c + 1 - 2 * core
    dev_x, dev_y, dev_c = (y, c_x, z), (1 - y, c, z), (y, c_core, z)
    place_x, place_y, place_d = y * 4 + c_x, (1 - y) * 4 + c, (1 - y) * 4 + c_x
    c_core_x = lax.rem(c_core + 2, 4)
    place_c, place_cx, place_cy, place_cd = y * 4 + c_core, y * 4 + c_core_x, (1 - y) * 4 + c_core, (1 - y) * 4 + c_core_x
    above = [(y, c, lax.rem(z + d, 4)) for d in (1, 2, 3)]
    beside = []
    for d in range(1, 8):
        other = lax.rem(place + d, 8)
        beside.append((other // 4, lax.rem(other, 4), z))
    lane = lax.broadcasted_iota(jnp.int32, (1, 128), 1)

    barrier = pltpu.get_barrier_semaphore()
    for device in above + beside:
        pl.semaphore_signal(barrier, inc=1, device_id=device, device_id_type=MESH)

    def own_piece(i):
        if i < 3:
            source = w_qkv.at[:, at(i * 8 + place, COLS)]
        elif i == 3:
            source = w_o.at[:, at(place, COLS)]
        else:
            source = (w_up if i % 2 == 0 else w_down).at[:, at(place * 4 + (i - 4) // 2, COLS)]
        return pltpu.make_async_copy(source, w_all.at[i, at(z, ROWS)], own_sem.at[i])

    loads = [
        pltpu.make_async_copy(cotangent.at[0], dy_buf.at[at(place, OWN)], load_sem.at[1]),
        pltpu.make_async_copy(vec_own, vecs.at[z], load_sem.at[2]),
        pltpu.make_async_copy(vec_own.at[pl.ds(8, 8)], places.at[y], load_sem.at[3]),
        pltpu.make_async_copy(turns, small.at[pl.ds(0, LENGTH)], load_sem.at[4]),
    ]
    for i in range(PIECES):
        own_piece(i).start()
    for load in loads:
        load.start()
    pl.semaphore_wait(barrier, 10)

    def gather(tag, source, target):
        def copy(k):
            sent, came = ga_send.at[tag, k], ga_recv.at[tag, k]
            if k == 0:
                return remote(source(0), target(place, 0), sent, came, dev_x)
            if k == 1:
                return remote(source(1), target(place, 1), sent, came, dev_x)
            if k == 2:
                return remote(source(1), target(place, 1), sent, came, dev_y)
            if k == 3:
                return remote(source(0), target(place, 0), sent, came, dev_y)
            if k == 4:
                return remote(source(None), target(place, None), sent, came, dev_c)
            if k == 5:
                return remote(target(place_x, 0), target(place_x, 0), sent, came, dev_y)
            if k == 6:
                return remote(target(place_y, 1), target(place_y, 1), sent, came, dev_x)
            which = (place_x, place_y, place_d)[k - 7]
            return remote(target(which, None), target(which, None), sent, came, dev_c)

        def arrived(k):
            spot = (
                (place_x, 0), (place_x, 1), (place_y, 1), (place_y, 0), (place_c, None),
                (place_d, 0), (place_d, 1), (place_cx, None), (place_cy, None), (place_cd, None),
            )[k]
            here = target(*spot)
            remote(here, here, ga_send.at[tag, k], ga_recv.at[tag, k], dev_c).wait_recv()

        def start():
            for k in (0, 2, 1, 3, 4):
                copy(k).start()

        def middle():
            arrived(0)
            copy(5).start()
            arrived(2)
            copy(6).start()

        def forward():
            arrived(1)
            copy(7).start()
            arrived(3)
            copy(8).start()

        def far():
            arrived(5)
            arrived(6)
            copy(9).start()

        def end():
            for k in (4, 7, 8, 9):
                arrived(k)
            for k in range(10):
                copy(k).wait_send()

        return start, middle, forward, far, end

    def half_of(ref, half, size):
        return ref if half is None else ref.at[pl.ds(half * size, size)]

    x_gather = gather(0, lambda half: half_of(tokens.at[0], half, 128), lambda who, half: half_of(x_land.at[who], half, 128))
    dy_gather = gather(
        1, lambda half: half_of(cotangent.at[0], half, 128),
        lambda who, half: dy_buf.at[at(who, OWN)] if half is None else dy_buf.at[at(who * 2 + half, 128)])
    x_gather[0]()

    def vec_copy(d):
        return remote(vec_own, vecs.at[z], vec_send.at[d], vec_recv.at[d], above[d])

    def place_copy():
        return remote(vec_own.at[pl.ds(8, 8)], places.at[y], vec_send.at[3], vec_recv.at[3], dev_y)

    for d in range(3):
        vec_copy(d).start()
    place_copy().start()
    for i in range(PIECES):
        own_piece(i).wait()

    def parts(s):
        return (s // 6) * 2 + s % 2, (s // 2) % 3

    def ag_copy(way, piece, hop, shard):
        block = w_all.at[piece, at(shard, ROWS)]
        return remote(block, block, ag_send.at[way, piece, hop], ag_recv.at[way, piece, hop], right if way == 0 else left)

    def ag_service(slot):
        before = slot - 2
        old, old_hop = parts(jnp.maximum(before, 0))
        live = (before >= 0) & (before < SLOTS)

        @pl.when(live & (z >= 1) & (z - 1 - old_hop >= 0))
        def _():
            ag_copy(0, old, old_hop, z - 1 - old_hop).wait_recv()

        @pl.when(live & (z <= 2) & (z + 1 + old_hop <= 3))
        def _():
            ag_copy(1, old, old_hop, z + 1 + old_hop).wait_recv()

        piece, hop = parts(jnp.minimum(slot, SLOTS - 1))
        later = (hop == 0) & (piece >= PIECES // 2)
        ahead = (slot < SLOTS // 2) & (hop == 2)

        @pl.when((slot < SLOTS) & (z <= 2) & (z - hop >= 0) & ~(later & (z <= 1)))
        def _():
            ag_copy(0, piece, hop, z - hop).start()

        @pl.when((slot < SLOTS) & (z >= 1) & (z + hop <= 3) & ~(later & (z >= 2)))
        def _():
            ag_copy(1, piece, hop, z + hop).start()

        @pl.when(ahead & (z <= 1))
        def _():
            ag_copy(0, piece + PIECES // 2, 0, z).start()

        @pl.when(ahead & (z >= 2))
        def _():
            ag_copy(1, piece + PIECES // 2, 0, z).start()

        @pl.when(live & (z <= 2) & (z - old_hop >= 0))
        def _():
            ag_copy(0, old, old_hop, z - old_hop).wait_send()

        @pl.when(live & (z >= 1) & (z + old_hop <= 3))
        def _():
            ag_copy(1, old, old_hop, z + old_hop).wait_send()

    def rs_piece(n):
        return jnp.where(n < 4, 3 - n, 4 + (n - 4) // 2 + 4 * (n % 2))

    def landing_slot(n, hop):
        return jnp.where(hop < 2, (n % 2) * 2 + hop, 4 + n % 4)

    def rs_copy(way, n, hop, shard):
        return remote(
            g_ring.at[n % RING, at(shard, ROWS)], landing.at[way, landing_slot(n, hop)],
            rs_send.at[way, n, hop], rs_recv.at[way, n, hop], right if way == 0 else left)

    def rs_add(way, n, hop, shard):
        rs_copy(way, n, hop, shard).wait_recv()
        block = g_ring.at[n % RING, at(shard, ROWS)]
        block[...] = (block[...].astype(WIDE) + landing[way, landing_slot(n, hop)].astype(WIDE)).astype(LOW)

    def held_copy(way, n):
        return remote(
            g_ring.at[n % RING, pl.ds((1 - way) * 3 * ROWS, ROWS)], landing.at[1 - way, n],
            rs_send.at[way, n, 2], rs_recv.at[way, n, 2], right if way == 0 else left)

    def held_add(way, n):
        held_copy(way, n).wait_recv()
        block = g_ring.at[n % RING, pl.ds((1 - way) * 3 * ROWS, ROWS)]
        block[...] = (block[...].astype(WIDE) + landing[1 - way, n].astype(WIDE)).astype(LOW)

    def red_copy(n):
        return pltpu.make_async_copy(g_ring.at[n % RING, at(z, ROWS)], gout.at[rs_piece(n), place], red_sem.at[n])

    def red_gather(n):
        piece = rs_piece(n)
        return gather(
            2 + n, lambda half: half_of(gout.at[piece, place], half, 256),
            lambda who, half: half_of(gout.at[piece, who], half, 256))

    def rs_service(slot):
        before = slot - 2
        old, old_hop = parts(jnp.clip(before, 0, SLOTS - 1))
        live = (before >= 0) & (before < SLOTS)
        ends = (z == 0) | (z == 3)
        old_held = (old >= HOLD) & (old < 6) & (old_hop == 2)
        held_sent, held_came = slot - 15, slot - 17
        send_held, take_held = (held_sent >= HOLD) & (held_sent < 6), (held_came >= HOLD) & (held_came < 6)

        @pl.when(live & (z >= 1) & (z - 1 <= old_hop) & ~(old_held & (z == 3)))
        def _():
            rs_add(0, old, old_hop, z + 2 - old_hop)

        @pl.when(live & (z <= 2) & (2 - z <= old_hop) & ~(old_held & (z == 0)))
        def _():
            rs_add(1, old, old_hop, z - 2 + old_hop)

        @pl.when(take_held & (z == 3))
        def _():
            held_add(0, held_came)

        @pl.when(take_held & (z == 0))
        def _():
            held_add(1, held_came)

        piece, hop = parts(jnp.clip(slot, 0, SLOTS - 1))
        sending = (slot >= 0) & (slot < SLOTS)
        held = (piece >= HOLD) & (piece < 6) & (hop == 2)

        @pl.when(send_held & (z == 2))
        def _():
            held_copy(0, held_sent).start()

        @pl.when(send_held & (z == 1))
        def _():
            held_copy(1, held_sent).start()

        @pl.when(sending & (z <= 2) & (z <= hop) & ~(held & (z == 2)))
        def _():
            rs_copy(0, piece, hop, z + 3 - hop).start()

        @pl.when(sending & (z >= 1) & (3 - z <= hop) & ~(held & (z == 1)))
        def _():
            rs_copy(1, piece, hop, z - 3 + hop).start()

        @pl.when(live & (z <= 2) & (z <= old_hop) & ~(old_held & (z == 2)))
        def _():
            rs_copy(0, old, old_hop, z + 3 - old_hop).wait_send()

        @pl.when(live & (z >= 1) & (3 - z <= old_hop) & ~(old_held & (z == 1)))
        def _():
            rs_copy(1, old, old_hop, z - 3 + old_hop).wait_send()

        @pl.when(take_held & (z == 2))
        def _():
            held_copy(0, held_came).wait_send()

        @pl.when(take_held & (z == 1))
        def _():
            held_copy(1, held_came).wait_send()

        ready = jnp.where(take_held, held_came, old)

        @pl.when((live & (old_hop == 2) & ~(old_held & ends)) | (take_held & ends))
        def _():
            red_copy(ready).start()
            red_copy(ready).wait()
            red_gather(ready)[0]()

        for step, delay in ((1, 1), (2, 2), (3, 3), (4, 5)):
            begun = slot - delay
            shifted = (begun >= 17 + HOLD) & (begun < 23)
            usual = (begun >= 6) & (begun < SLOTS + 6) & (begun % 6 < 2) & ~(ends & (begun // 2 == 9))
            n = jnp.where(shifted, begun - 17, jnp.clip((begun // 6) * 2 - 2 + begun % 6, 0, PIECES - 1))

            @pl.when(usual | (shifted & ends))
            def _(step=step, n=n):
                red_gather(n)[step]()

    def service(slot):
        if isinstance(slot, int):
            if slot < SLOTS + 2:
                ag_service(jnp.int32(slot))
            if slot >= RS_START:
                rs_service(jnp.int32(slot - RS_START))
        else:
            ag_service(slot)
            rs_service(slot - RS_START)

    def services(first, last, early=False):
        def step(slot, carry):
            ag_service(slot)
            if not early:
                rs_service(slot - RS_START)
            return carry

        lax.fori_loop(first, last, step, 0)

    def loop(count, body, first=None, ag=True, rs=True):
        def step(i, carry):
            if first is not None:
                if ag:
                    ag_service(first + i)
                if rs:
                    rs_service(first + i - RS_START)
            body(i)
            return carry

        lax.fori_loop(0, count, step, 0)

    services(0, 2, True)
    for load in loads[1:]:
        load.wait()
    for d in range(3):
        here = vecs.at[lax.rem(z + 3 - d, 4)]
        remote(here, here, vec_send.at[d], vec_recv.at[d], above[d]).wait_recv()
    other = places.at[1 - y]
    remote(other, other, vec_send.at[3], vec_recv.at[3], dev_y).wait_recv()
    for shard in range(4):
        here = pl.ds(shard * ROWS, ROWS)
        for k in range(4):
            rows[k : k + 1, here] = vecs[shard, 9 + k : 10 + k, :]
        rows[4:5, here] = vecs[shard, 3:4, :] + vecs[shard, 8:9, :]
        rows[5:8, here] = jnp.zeros((3, ROWS), WIDE)
    for kind in range(3):
        flat = kind * WIDTH + place * COLS
        bias[kind : kind + 1, :] = vecs[flat // 1536, pl.ds((flat % 1536) // 512, 1), at((flat % 512) // 256, COLS)]
    for part in range(4):
        flat = place * 1024 + part * COLS
        bias[3 + part : 4 + part, :] = vecs[flat // 2048, pl.ds(4 + (flat % 2048) // 512, 1), at((flat % 512) // 256, COLS)]

    def set_place(i, carry):
        seq, block = i // 8, i % 8
        value = jnp.sum(jnp.where(lane == block, places[seq, 5:6, 0:128], 0.0), 1, keepdims=True)
        made = jnp.zeros((BLK, 128), WIDE)
        for b in range(8):
            made = jnp.where(value == float(b), small[pl.ds(b * BLK, BLK), :], made)
        tab[at(i, BLK), :] = made
        pos[seq, :, at(block, BLK)] = jnp.broadcast_to(value * float(BLK) + lane.astype(WIDE), (8, BLK))
        return carry

    services(2, 3, True)
    lax.fori_loop(0, 16, set_place, 0)
    for shard in range(4):
        tall = jnp.concatenate([rows[:, pl.ds(shard * ROWS, ROWS)], jnp.zeros((120, ROWS), WIDE)], 0)
        small[pl.ds(shard * ROWS, ROWS), :] = jnp.transpose(tall)
    x_gather[1]()
    services(3, 5, True)
    x_gather[2]()
    dy_gather[0]()
    services(5, 7, True)
    x_gather[3]()
    services(7, 8, True)
    x_gather[4]()
    def norm_tile(which):
        def run(i):
            def part(n, carry):
                block = at(i * 4 + n, 64)
                centred, scale = standardise_rows(x_buf[block, :].astype(WIDE))
                x_buf[block, :] = (centred * scale * rows[2 * which : 2 * which + 1, :] + rows[2 * which + 1 : 2 * which + 2, :]).astype(LOW)
                return carry

            lax.fori_loop(0, 4, part, 0)
        return run

    def load_x():
        copies = [pltpu.make_async_copy(tokens.at[0], x_buf.at[at(place, OWN)], own_sem.at[0])]
        for d in range(1, 8):
            other = lax.rem(place + d, 8)
            copies.append(pltpu.make_async_copy(x_land.at[other], x_buf.at[at(other, OWN)], own_sem.at[d]))
        for copy in copies:
            copy.start()
        for copy in copies:
            copy.wait()

    def norm(which, first, rs):
        load_x()

        def body(i):
            for n in range(4):
                norm_tile(which)(4 * i + n)

        loop(2, body, first, rs=rs)

    norm(0, 8, False)
    dy_gather[1]()

    def turned(values, block, sign):
        entry = tab[block, :]
        cosine = jnp.where(lane < 32, entry, jnp.where(lane < 64, pltpu.roll(entry, 32, 1), 1.0))
        sine = jnp.where(lane < 32, -pltpu.roll(entry, 96, 1), jnp.where(lane < 64, entry, 0.0))
        low = values[:, :128]
        partner = jnp.where(lane < 32, pltpu.roll(low, 96, 1), pltpu.roll(low, 32, 1))
        return jnp.concatenate([low * cosine + partner * (sine * sign), values[:, 128:]], 1)

    def project(kind):
        def run(i):
            block = at(i, 512)
            made = dot_nn(x_buf[block, :], w_all[kind]) + bias[kind : kind + 1, :]
            if kind < 2:
                made = turned(made, block, 1.0)
            if kind == 0:
                made = made * SCALING
            act[9 + kind, block, :] = made.astype(LOW)
        return run

    services(10, 11, True)
    loop(4, project(0))
    dy_gather[2]()
    services(11, 12, True)
    loop(4, project(1))
    services(12, 13, True)
    loop(4, project(2))
    dy_gather[3]()
    dy_gather[4]()
    loads[0].wait()

    def attend(i):
        seq = i // 4
        block, keys = at(i, 256), at(seq, LENGTH)

        q, k, v = act[9, block, :], act[10, keys, :], act[11, keys, :]
        kept = tab[block, 64:65] >= pos[seq, 0:1, :]
        scores = jnp.where(kept, dot_nt(q, k), -1e30)
        expo = jnp.exp(scores - jnp.max(scores, -1, keepdims=True))
        p = expo * (1.0 / jnp.sum(expo, -1, keepdims=True))
        p_low = p.astype(LOW)
        act[3, block, :] = dot_nn(p_low, v).astype(LOW)
        d_attn = dot_nn(dy_buf[block, :], w_all[3]).astype(LOW)
        dp = dot_nt(d_attn, v)
        ds = jnp.where(kept, p * (dp - jnp.sum(p * dp, -1, keepdims=True)), 0.0).astype(LOW)
        act[0, block, :] = turned(dot_nn(ds, k) * SCALING, block, -1.0).astype(LOW)
        act[8, block, :] = d_attn
        for n in range(4):
            g_ring[n, at(i % 4, 256), :] = ds[:, n * COLS : (n + 1) * COLS]
            g_ring[n, at(4 + i % 4, 256), :] = p_low[:, n * COLS : (n + 1) * COLS]

        @pl.when(i % 4 == 3)
        def _():
            def keyed(n, carry):
                mine = at(seq * 4 + n, COLS)
                d_keys = dot_tn(g_ring[n, 0:LENGTH, :], act[9, keys, :])
                act[1, mine, :] = turned(d_keys, mine, -1.0).astype(LOW)
                act[2, mine, :] = dot_tn(g_ring[n, LENGTH:, :], act[8, keys, :]).astype(LOW)
                return carry

            lax.fori_loop(0, 4, keyed, 0)

    def attend_two(i):
        def inner(n, carry):
            attend(2 * i + n)
            return carry

        lax.fori_loop(0, 2, inner, 0)

    loop(4, attend_two, 13, rs=False)

    def gradient(piece, n, source):
        summed = piece < 3 or (piece != 3 and piece % 2 == 0)
        if summed:
            gb[piece : piece + 1, :] = jnp.zeros((1, COLS), WIDE)

            def count(i, carry):
                gb[piece : piece + 1, :] += jnp.sum(act[piece, at(i, 256), :].astype(WIDE), 0, keepdims=True)
                return carry

            lax.fori_loop(0, 8, count, 0)

        def part(s, carry):
            block = at(s, ROWS)
            made = dot_tn(source[:, block], act[piece])
            g_ring[n % RING, block, :] = made.astype(LOW)
            if summed:
                mine = 0 if piece < 3 else 1
                weight = w_all[piece, block, :].astype(WIDE)
                sums = gb[piece : piece + 1, :]
                gain = jnp.sum(weight * (made - small[block, 2 * mine + 1 : 2 * mine + 2] * sums), 1, keepdims=True)
                shift = jnp.sum(weight * sums, 1, keepdims=True)
                here = 8 + 2 * mine
                old = small[block, :]
                small[block, :] = old + jnp.where(lane == here, gain, 0.0) + jnp.where(lane == here + 1, shift, 0.0)
            return carry

        lax.fori_loop(0, 4, part, 0)

    rows[5:6, :] = jnp.sum(dy_buf[at(place, OWN), :].astype(WIDE), 0, keepdims=True)
    gradient(3, 0, dy_buf)
    service(17)
    gradient(2, 1, x_buf)
    service(18)
    gradient(1, 2, x_buf)
    service(19)
    gradient(0, 3, x_buf)
    service(20)
    norm(1, 21, True)

    def feed(part):
        up, down = 4 + 2 * part, 5 + 2 * part

        def run(i):
            for n in range(2):
                block = at(2 * i + n, 512)
                hidden = dot_nn(x_buf[block, :], w_all[up]) + bias[3 + part : 4 + part, :]
                d_gelu = dot_nn(dy_buf[block, :], w_all[down])
                made, slope = gelu_pair(hidden)
                act[down, block, :] = made.astype(LOW)
                act[up, block, :] = (d_gelu * slope).astype(LOW)
        return run

    slot = 23
    for part in range(3):
        loop(2, feed(part), slot)
        slot += 2
        gradient(4 + 2 * part, 4 + 2 * part, x_buf)
        service(slot)
        gradient(5 + 2 * part, 5 + 2 * part, dy_buf)
        service(slot + 1)
        slot += 2
    services(35, 38)
    service(38)
    loop(2, feed(3))
    gradient(10, 10, x_buf)
    service(39)

    def make_pack():
        for shard in range(4):
            here = pl.ds(shard * ROWS, ROWS)
            flat = jnp.transpose(small[here, :])
            pack[shard, 0:1, :] = flat[8:9] / rows[0:1, here]
            pack[shard, 1:2, :] = flat[9:10]
            pack[shard, 2:3, :] = flat[10:11] / rows[2:3, here]
            pack[shard, 3:4, :] = flat[11:12]
            pack[shard, 4:5, :] = rows[5:6, here]
            pack[shard, 5:8, :] = jnp.zeros((3, ROWS), WIDE)
            pack[shard, 8:16, :] = jnp.zeros((8, ROWS), WIDE)
            for kind in range(3):
                pack[shard, 8 + kind : 9 + kind, :COLS] = gb[kind : kind + 1, :]
            for part in range(4):
                pack[shard, 11 + part : 12 + part, :COLS] = gb[4 + 2 * part : 5 + 2 * part, :]
        pack_z[z] = pack[z]

    def pack_copy(d):
        return remote(pack.at[lax.rem(z + d + 1, 4)], pack_z.at[z], pk_send.at[d], pk_recv.at[d], above[d])

    def peer_copy(d):
        return remote(pack_p.at[place], pack_p.at[place], pp_send.at[d], pp_recv.at[d], beside[d])

    def sum_start():
        for d in range(3):
            pack_copy(d).start()

    def sum_z():
        for d in range(3):
            here = pack_z.at[lax.rem(z + 3 - d, 4)]
            remote(here, here, pk_send.at[d], pk_recv.at[d], above[d]).wait_recv()
        pack_p[place] = pack_z[0] + pack_z[1] + pack_z[2] + pack_z[3]
        for d in range(7):
            peer_copy(d).start()

    def sum_plane():
        for d in range(7):
            here = pack_p.at[lax.rem(place + 7 - d, 8)]
            remote(here, here, pp_send.at[d], pp_recv.at[d], beside[d]).wait_recv()
        total = pack_p[0, 0:8, :]
        for p in range(1, 8):
            total = total + pack_p[p, 0:8, :]
        final[:, 0:ROWS] = total
        final[:, ROWS:] = jnp.zeros((8, 2 * COLS), WIDE)
        for r in range(6):
            flat = 6 * z + r
            final[r : r + 1, ROWS : ROWS + COLS] = pack_p[flat % 8, pl.ds(8 + flat // 8, 1), 0:COLS]
        for r in range(8):
            final[r : r + 1, ROWS + COLS :] = pack_p[2 * z + r // 4, 11 + r % 4 : 12 + r % 4, 0:COLS]

    tiles = {"d": (1 - y) * 2 + 1 - chip, "x": y * 2 + 1 - chip, "y": (1 - y) * 2 + chip, "own": y * 2 + chip}
    order = ("d", "x", "y", "own")
    both = (x_buf, dy_buf)

    def finish(name, whose, a):
        block = block_of(name, whose)

        def run(i, carry):
            columns = at(i, 512)

            def total(pieces):
                return sum(dot_nt(act[piece, block, :], w_all[piece, columns, :]) for piece in pieces)

            if a == 0:
                x_buf[block, columns] = total((3, 5, 7, 9, 11)).astype(LOW)
            else:
                first = total((0, 1, 2)) * rows[0:1, columns]
                dy_buf[block, columns] = (first + total((4, 6, 8, 10)) * rows[2:3, columns]).astype(LOW)
            return carry

        lax.fori_loop(0, 4, run, 0)

    def block_of(name, whose):
        return at(tiles[name] * 2 + whose, OWN)

    def half_rows(name, half):
        return at(tiles[name] * 4 + core * 2 + half, 128)

    def core_copy(name, a):
        i = order.index(name)
        return remote(both[a].at[block_of(name, 1 - core)], core_land.at[i, a], core_send.at[i, a], core_recv.at[i, a], dev_c)

    def first_copy(i, a):
        name, half, device = (("d", 0, dev_x), ("d", 1, dev_y), ("x", 0, dev_x), ("y", 1, dev_y))[i]
        return remote(both[a].at[half_rows(name, half)], first_land.at[i, a], one_send.at[i, a], one_recv.at[i, a], device)

    def second_copy(i, a):
        name, half, device = (("y", 0, dev_y), ("x", 1, dev_x))[i]
        return remote(both[a].at[half_rows(name, half)], second_land.at[i, a], two_send.at[i, a], two_recv.at[i, a], device)

    def fetch(source, a):
        return pltpu.make_async_copy(source, stage.at[a], load_sem.at[a])

    def add_in(copy, source, spots, a):
        copy.wait_recv()
        for half, spot in enumerate(spots):
            fetch(source.at[pl.ds(half * 128, 128)], a).start()
            fetch(source.at[pl.ds(half * 128, 128)], a).wait()
            both[a][spot, :] = (both[a][spot, :].astype(WIDE) + stage[a].astype(WIDE)).astype(LOW)

    def core_add(name, a):
        i = order.index(name)
        add_in(core_copy(name, a), core_land.at[i, a], [half_rows(name, 0), half_rows(name, 1)], a)

    def first_add(i, a):
        name, half = (("y", 0), ("x", 1), ("own", 0), ("own", 1))[i]
        add_in(first_copy(i, a), first_land.at[i, a], [half_rows(name, half)], a)

    def second_add(i, a):
        add_in(second_copy(i, a), second_land.at[i, a], [half_rows("own", i)], a)

    def pass_on(a):
        for i in range(2):
            first_add(i, a)
            second_copy(i, a).start()

    def spread(a, slots):
        for i, name in enumerate(order):
            finish(name, 1 - core, a)
            core_copy(name, a).start()
            if i == 1:
                core_add("d", a)
                first_copy(0, a).start()
                first_copy(1, a).start()
            elif i > 1:
                core_add(order[i - 1], a)
                first_copy(i, a).start()
            finish(name, core, a)
            if slots[i] is not None:
                service(slots[i])

    spread(0, (40, None, 41, None))
    gradient(11, 11, dy_buf)
    service(42)
    make_pack()
    sum_start()
    core_add("own", 0)
    spread(1, (43, None, 44, 45))
    core_add("own", 1)
    pass_on(0)
    sum_z()
    services(46, 48)
    first_add(2, 0)
    first_add(3, 0)
    services(48, 50)
    pass_on(1)
    services(50, 53)
    sum_plane()
    second_add(0, 0)
    second_add(1, 0)
    first_add(2, 1)
    first_add(3, 1)
    services(53, 56)
    second_add(0, 1)
    second_add(1, 1)

    for half in range(2):
        given = [tokens.at[0, pl.ds(half * 128, 128)], cotangent.at[0, pl.ds(half * 128, 128)]]
        for a in range(2):
            fetch(given[a], a).start()
        for a in range(2):
            fetch(given[a], a).wait()

        def emit(i, carry, half=half):
            here, mine = at(i, 64), at(place * 4 + half * 2 + i, 64)
            inputs = stage[0, here, :].astype(WIDE)
            x_buf[mine, :] = (inputs + x_buf[mine, :].astype(WIDE) + rows[4:5, :]).astype(LOW)
            centred, scale = standardise_rows(inputs)
            hat = centred * scale
            u = dy_buf[mine, :].astype(WIDE)
            inner = jnp.mean(u * hat, -1, keepdims=True)
            d_x = scale * (u - jnp.mean(u, -1, keepdims=True) - hat * inner)
            dy_buf[mine, :] = (stage[1, here, :].astype(WIDE) + d_x).astype(LOW)
            return carry

        lax.fori_loop(0, 2, emit, 0)
    ends = [
        pltpu.make_async_copy(x_buf.at[at(place, OWN)], out, load_sem.at[0]),
        pltpu.make_async_copy(dy_buf.at[at(place, OWN)], input_grad, load_sem.at[1]),
        pltpu.make_async_copy(final, small_out, load_sem.at[2]),
    ]
    for end in ends:
        end.start()
    services(56, LAST)
    for end in ends:
        end.wait()
    for d in range(3):
        vec_copy(d).wait_send()
        pack_copy(d).wait_send()
    place_copy().wait_send()
    for d in range(7):
        peer_copy(d).wait_send()
    for a in range(2):
        for name in order:
            core_copy(name, a).wait_send()
        for i in range(4):
            first_copy(i, a).wait_send()
        for i in range(2):
            second_copy(i, a).wait_send()


def standardise_rows(values):
    middle = jnp.mean(values, -1, keepdims=True)
    centred = values - middle
    spread = jnp.mean(centred * centred, -1, keepdims=True)
    return centred, lax.rsqrt(spread + EPS)


def layer_call(*operands):
    anywhere = pl.BlockSpec(memory_space=pltpu.HBM)
    shape = jax.ShapeDtypeStruct
    dma = pltpu.SemaphoreType.DMA
    out_shape = (
        shape((OWN, WIDTH), LOW),
        shape((OWN, WIDTH), LOW),
        shape((8, 1024), WIDE),
        shape((PIECES, 8, ROWS, COLS), LOW),
        shape((8, OWN, WIDTH), LOW),
        shape((4, 2, OWN, WIDTH), LOW),
        shape((4, 2, 128, WIDTH), LOW),
        shape((2, 2, 128, WIDTH), LOW),
    )
    return pl.pallas_call(
        layer_kernel,
        out_shape=out_shape,
        in_specs=[anywhere] * len(operands),
        out_specs=[anywhere] * len(out_shape),
        scratch_shapes=[
            pltpu.VMEM((PIECES, WIDTH, COLS), LOW),
            pltpu.VMEM((PIECES, TOK, COLS), LOW),
            pltpu.VMEM((TOK, WIDTH), LOW),
            pltpu.VMEM((TOK, WIDTH), LOW),
            pltpu.VMEM((RING, WIDTH, COLS), LOW),
            pltpu.VMEM((2, 8, ROWS, COLS), LOW),
            pltpu.VMEM((WIDTH, 128), WIDE),
            pltpu.VMEM((16, COLS), WIDE),
            pltpu.VMEM((TOK, 128), WIDE),
            pltpu.VMEM((2, 8, LENGTH), WIDE),
            pltpu.VMEM((8, WIDTH), WIDE),
            pltpu.VMEM((8, COLS), WIDE),
            pltpu.VMEM((2, 128, WIDTH), LOW),
            pltpu.VMEM((4, 16, ROWS), WIDE),
            pltpu.VMEM((2, 8, ROWS), WIDE),
            pltpu.VMEM((4, 16, ROWS), WIDE),
            pltpu.VMEM((4, 16, ROWS), WIDE),
            pltpu.VMEM((8, 16, ROWS), WIDE),
            pltpu.VMEM((8, 1024), WIDE),
            dma((5,)),
            dma((PIECES,)),
            dma((2, PIECES, HOPS)),
            dma((2, PIECES, HOPS)),
            dma((2, PIECES, HOPS)),
            dma((2, PIECES, HOPS)),
            dma((PIECES,)),
            dma((2 + PIECES, 10)),
            dma((2 + PIECES, 10)),
            dma((4,)),
            dma((4,)),
            dma((3,)),
            dma((3,)),
            dma((7,)),
            dma((7,)),
            dma((4, 2)),
            dma((4, 2)),
            dma((4, 2)),
            dma((4, 2)),
            dma((2, 2)),
            dma((2, 2)),
        ],
        compiler_params=pltpu.CompilerParams(collective_id=0, has_side_effects=True, vmem_limit_bytes=61 * 1024 * 1024),
    )(*operands)


DEPTH = 8


def widen_kernel(gathered, made, made_grad, g_qkv, g_o, g_up, g_down, output, input_grad, low, wide, held, low_sem, wide_sem, pass_sem):
    brought = [pltpu.make_async_copy(made, held.at[0], pass_sem.at[0]), pltpu.make_async_copy(made_grad, held.at[1], pass_sem.at[1])]
    passing = [pltpu.make_async_copy(held.at[0], output, pass_sem.at[0]), pltpu.make_async_copy(held.at[1], input_grad, pass_sem.at[1])]
    for copy in brought:
        copy.start()

    def load(i):
        return pltpu.make_async_copy(gathered.at[i // 8, i % 8], low.at[i % DEPTH], low_sem.at[i % DEPTH])

    def store(i, act):
        piece, p = i // 8, i % 8

        def copy(target):
            act(pltpu.make_async_copy(wide.at[i % DEPTH], target, wide_sem.at[i % DEPTH]))

        @pl.when(piece < 3)
        def _():
            copy(g_qkv.at[:, at(jnp.minimum(i, 23), COLS)])

        @pl.when(piece == 3)
        def _():
            copy(g_o.at[:, at(p, COLS)])

        @pl.when((piece >= 4) & (piece < 8))
        def _():
            copy(g_up.at[:, at(p * 4 + jnp.clip(piece - 4, 0, 3), COLS)])

        @pl.when(piece >= 8)
        def _():
            copy(g_down.at[:, at(p * 4 + jnp.clip(piece - 8, 0, 3), COLS)])

    def first(i, carry):
        load(i).start()
        return carry

    def step(i, carry):
        load(i).wait()

        @pl.when(i >= DEPTH)
        def _():
            store(i - DEPTH, lambda copy: copy.wait())

        wide[i % DEPTH] = low[i % DEPTH].astype(WIDE)
        store(i, lambda copy: copy.start())

        @pl.when(i + DEPTH < 96)
        def _():
            load(i + DEPTH).start()

        return carry

    def last(i, carry):
        store(i, lambda copy: copy.wait())
        return carry

    lax.fori_loop(0, DEPTH, first, 0)
    lax.fori_loop(0, 16, step, 0)
    for copy in brought:
        copy.wait()
    for copy in passing:
        copy.start()
    lax.fori_loop(16, 96, step, 0)
    lax.fori_loop(96 - DEPTH, 96, last, 0)
    for copy in passing:
        copy.wait()


def widen(gathered, made, made_grad):
    shape = jax.ShapeDtypeStruct
    anywhere = pl.BlockSpec(memory_space=pltpu.HBM)
    return pl.pallas_call(
        widen_kernel,
        in_specs=[anywhere] * 3,
        out_specs=[anywhere] * 6,
        out_shape=(shape((ROWS, 3 * WIDTH), WIDE), shape((ROWS, WIDTH), WIDE), shape((ROWS, 4 * WIDTH), WIDE), shape((ROWS, 4 * WIDTH), WIDE), shape(made.shape, LOW), shape(made.shape, LOW)),
        scratch_shapes=[
            pltpu.VMEM((DEPTH, ROWS, COLS), LOW),
            pltpu.VMEM((DEPTH, ROWS, COLS), WIDE),
            pltpu.VMEM((2, OWN, WIDTH), LOW),
            pltpu.SemaphoreType.DMA((DEPTH,)),
            pltpu.SemaphoreType.DMA((DEPTH,)),
            pltpu.SemaphoreType.DMA((2,)),
        ],
        compiler_params=pltpu.CompilerParams(vmem_limit_bytes=56 * 1024 * 1024),
    )(gathered, made, made_grad)


def turn_table():
    where = np.arange(LENGTH, dtype=np.float32)[:, None]
    freqs = np.float32(10000.0) ** (-(np.arange(ROT // 2, dtype=np.float32) * np.float32(2.0 / ROT)))
    turned = (where * freqs[None, :]).astype(np.float32)
    return np.concatenate([np.cos(turned), np.sin(turned), np.broadcast_to(where, (LENGTH, 64))], 1).astype(np.float32)


def fused_body(tokens, block_place, w_qkv, b_qkv, w_o_t, b_o, w_up, b_up, w_down_t, b_down,
               norm1_gain, norm1_shift, norm2_gain, norm2_shift, cotangent):
    given = (b_qkv, b_o, b_up, b_down, norm1_gain, norm1_shift, norm2_gain, norm2_shift)
    spots = block_place.astype(WIDE).reshape(-1)
    vec, start = jnp.zeros((16 * ROWS,), WIDE), 0
    for part in given + (spots,):
        vec = vec + jnp.pad(part.astype(WIDE), (start, 16 * ROWS - start - part.shape[0]))
        start += part.shape[0]
    vec = vec.reshape(16, ROWS)
    turns = jnp.asarray(turn_table())
    results = layer_call(tokens, cotangent, w_qkv, w_o_t, w_up, w_down_t, vec, turns)
    made, made_grad, sums, gathered = results[:4]
    g_qkv, g_o, g_up, g_down, output, input_grad = widen(gathered, made, made_grad)
    grad_bias = sums[4, :ROWS]
    return (
        output[None],
        input_grad[None],
        g_qkv,
        sums[:6, ROWS : ROWS + COLS].reshape(-1),
        g_o,
        grad_bias,
        g_up,
        sums[:, ROWS + COLS :].reshape(-1),
        g_down,
        grad_bias,
        sums[0, :ROWS],
        sums[1, :ROWS],
        sums[2, :ROWS],
        sums[3, :ROWS],
    )


def solution(mesh):
    tok = P(("seq", "fsdp"), "ctx", None)
    mat, vec = P("fsdp", None), P("fsdp")
    params = (mat, vec, mat, vec, mat, vec, mat, vec, vec, vec, vec, vec)
    in_specs = (tok, P(("seq", "fsdp"), None)) + params + (tok,)
    return jax.shard_map(fused_body if fits(mesh) else body, mesh=mesh, in_specs=in_specs, out_specs=(tok, tok) + params, check_vma=False)
```

```python
import math

import jax
import jax.numpy as jnp
import numpy as np
from jax import lax
from jax.experimental import pallas as pl
from jax.experimental.pallas import tpu as pltpu
from jax.sharding import PartitionSpec as P

HEADS = 8
HEAD = 256
ROT = 64
BLK = 128
EPS = 1e-05
PLANE = ("seq", "ctx")
LOW = jnp.bfloat16
WIDE = jnp.float32


def dot_nn(left, right):
    return lax.dot_general(left, right, (((1,), (0,)), ((), ())), preferred_element_type=WIDE)


def dot_nt(left, right):
    return lax.dot_general(left, right, (((1,), (1,)), ((), ())), preferred_element_type=WIDE)


def dot_tn(left, right):
    return lax.dot_general(left, right, (((0,), (0,)), ((), ())), preferred_element_type=WIDE)


def batch_nn(left, right):
    return lax.dot_general(left, right, (((2,), (1,)), ((0,), (0,))), preferred_element_type=WIDE)


def batch_nt(left, right):
    return lax.dot_general(left, right, (((2,), (2,)), ((0,), (0,))), preferred_element_type=WIDE)


def batch_tn(left, right):
    return lax.dot_general(left, right, (((1,), (1,)), ((0,), (0,))), preferred_element_type=WIDE)


def standardise(values):
    middle = jnp.mean(values, -1, keepdims=True)
    centred = values - middle
    spread = jnp.mean(centred * centred, -1, keepdims=True)
    scale = lax.rsqrt(spread + EPS)
    return centred * scale, scale


def angles(positions):
    freqs = 10000.0 ** (-(jnp.arange(ROT // 2, dtype=WIDE) * 2.0 / ROT))
    turned = positions.astype(WIDE)[:, None] * freqs[None, :]
    return jnp.cos(turned), jnp.sin(turned)


def turn(values, cosine, sine):
    half = ROT // 2
    one, two, rest = values[..., :half], values[..., half:ROT], values[..., ROT:]
    return jnp.concatenate([one * cosine - two * sine, two * cosine + one * sine, rest], -1)


def gelu_pair(hidden):
    bell = 0.5 * (1.0 + lax.erf(hidden * (1.0 / math.sqrt(2.0))))
    slope = bell + hidden * jnp.exp(-0.5 * hidden * hidden) * (1.0 / math.sqrt(2.0 * math.pi))
    return hidden * bell, slope


def body(tokens, block_place, w_qkv, b_qkv, w_o_t, b_o, w_up, b_up, w_down_t, b_down,
         norm1_gain, norm1_shift, norm2_gain, norm2_shift, cotangent):
    seqs, ctxs, shards = lax.axis_size("seq"), lax.axis_size("ctx"), lax.axis_size("fsdp")
    peers = seqs * ctxs
    place = lax.axis_index("seq") * ctxs + lax.axis_index("ctx")
    own, width = tokens.shape[1:]
    hidden_all = w_up.shape[1]
    length = own * ctxs
    share = max(1, peers // HEADS)
    heads = max(1, HEADS // peers)
    own_seqs = seqs // share
    group = place // share
    first_seq = (place % share) * own_seqs
    cols = heads * HEAD
    hid = hidden_all // peers

    x_own = tokens[0].astype(WIDE)
    dy_own = cotangent[0]
    both = lax.all_gather(jnp.stack([tokens[0], dy_own]), PLANE, axis=0, tiled=False)
    x_all = both[:, 0].reshape(seqs * length, width)
    dy_all = both[:, 1].reshape(seqs * length, width)
    places = lax.all_gather(block_place[0], "seq", axis=0, tiled=False)

    small = (b_qkv, b_o, b_up, b_down, norm1_gain, norm1_shift, norm2_gain, norm2_shift)
    packed = lax.all_gather(jnp.concatenate(small), "fsdp", axis=0, tiled=False)
    unpacked, start = [], 0
    for part in small:
        size = part.shape[0]
        unpacked.append(packed[:, start : start + size].reshape(-1).astype(WIDE))
        start += size
    bias_qkv, bias_o, bias_up, bias_down, gain1, shift1, gain2, shift2 = unpacked

    def head_cols(values, kinds):
        rows = values.shape[0]
        split = values.reshape(rows, kinds, HEADS * HEAD)
        return lax.dynamic_slice_in_dim(split, group * cols, cols, 2).reshape(rows, kinds * cols)

    def hid_cols(values):
        return lax.dynamic_slice_in_dim(values, place * hid, hid, 1)

    own_cols = jnp.concatenate([head_cols(w_qkv, 3), head_cols(w_o_t, 1), hid_cols(w_up), hid_cols(w_down_t)], 1)
    weights = lax.all_gather(own_cols, "fsdp", axis=0, tiled=True)
    cut = 4 * cols
    m_qkv, m_o, m_up, m_down = weights[:, : 3 * cols], weights[:, 3 * cols : cut], weights[:, cut : cut + hid], weights[:, cut + hid :]
    own_bias_qkv = head_cols(bias_qkv[None], 3)
    own_bias_up = hid_cols(bias_up[None])

    x_hat, _ = standardise(x_all.astype(WIDE))
    a1 = (x_hat * gain1 + shift1).astype(LOW)
    a2 = (x_hat * gain2 + shift2).astype(LOW)

    rows = own_seqs * length
    a1_seq = lax.dynamic_slice_in_dim(a1, first_seq * length, rows, 0)
    dy_seq = lax.dynamic_slice_in_dim(dy_all, first_seq * length, rows, 0)
    positions = (places[:, :, None] * BLK + jnp.arange(BLK, dtype=jnp.int32)).reshape(seqs, length)
    positions = lax.dynamic_slice_in_dim(positions, first_seq, own_seqs, 0)
    cosine, sine = angles(positions.reshape(-1))
    cosine, sine = cosine[:, None], sine[:, None]
    qkv = dot_nn(a1_seq, m_qkv) + own_bias_qkv

    def to_heads(values):
        return values.reshape(own_seqs, length, heads, HEAD).transpose(0, 2, 1, 3).reshape(own_seqs * heads, length, HEAD)

    def from_heads(values):
        return values.reshape(own_seqs, heads, length, HEAD).transpose(0, 2, 1, 3).reshape(rows, cols)

    def turned(values):
        return turn(values.reshape(rows, heads, HEAD), cosine, sine).reshape(rows, cols)

    def turned_back(values):
        return turn(values.reshape(rows, heads, HEAD), cosine, -sine).reshape(rows, cols)

    q = to_heads(turned(qkv[:, :cols]).astype(LOW))
    k = to_heads(turned(qkv[:, cols : 2 * cols]).astype(LOW))
    v = to_heads(qkv[:, 2 * cols :].astype(LOW))
    scaling = 1.0 / math.sqrt(HEAD)
    kept = (positions[:, :, None] >= positions[:, None, :])[:, None]
    kept = jnp.broadcast_to(kept, (own_seqs, heads, length, length)).reshape(own_seqs * heads, length, length)
    scores = jnp.where(kept, batch_nt(q, k) * scaling, -1e30)
    expo = jnp.exp(scores - jnp.max(scores, -1, keepdims=True))
    p = expo / jnp.sum(expo, -1, keepdims=True)
    p_low = p.astype(LOW)
    attn = from_heads(batch_nn(p_low, v).astype(LOW))
    d_attn = to_heads(dot_nn(dy_seq, m_o).astype(LOW))
    dp = batch_nt(d_attn, v)
    ds = jnp.where(kept, p * (dp - jnp.sum(p * dp, -1, keepdims=True)), 0.0).astype(LOW)
    dq = from_heads(batch_nn(ds, k) * scaling)
    dk = from_heads(batch_tn(ds, q) * scaling)
    dv = from_heads(batch_tn(p_low, d_attn))
    d_qkv = jnp.concatenate([turned_back(dq), turned_back(dk), dv], 1).astype(LOW)

    g, slope = gelu_pair(dot_nn(a2, m_up) + own_bias_up)
    g = g.astype(LOW)
    d_h = (dot_nn(dy_all, m_down) * slope).astype(LOW)

    def onto(values, part):
        return lax.dynamic_update_slice_in_dim(values, lax.dynamic_slice_in_dim(values, first_seq * length, rows, 0) + part, first_seq * length, 0)

    out_part = onto(dot_nt(g, m_down), dot_nt(attn, m_o))
    u_part = onto(dot_nt(d_h, m_up) * gain2, dot_nt(d_qkv, m_qkv) * gain1)
    out_sum = lax.psum_scatter(out_part.astype(LOW), PLANE, scatter_dimension=0, tiled=True).astype(WIDE)
    u_sum = lax.psum_scatter(u_part.astype(LOW), PLANE, scatter_dimension=0, tiled=True).astype(WIDE)
    output = (x_own + out_sum + bias_o + bias_down).astype(LOW)[None]
    hat_own, scale_own = standardise(x_own)
    d_x = scale_own * (u_sum - jnp.mean(u_sum, -1, keepdims=True) - hat_own * jnp.mean(u_sum * hat_own, -1, keepdims=True))
    input_grad = (dy_own.astype(WIDE) + d_x).astype(LOW)[None]

    g_qkv = dot_tn(a1_seq, d_qkv)
    g_o = dot_tn(dy_seq, attn)
    g_up = dot_tn(a2, d_h)
    g_down = dot_tn(dy_all, g)
    gb_qkv = jnp.sum(d_qkv, 0, dtype=WIDE)
    gb_up = jnp.sum(d_h, 0, dtype=WIDE)
    wide_qkv, wide_up = m_qkv.astype(WIDE), m_up.astype(WIDE)
    d_gain1 = jnp.sum(wide_qkv * (g_qkv - shift1[:, None] * gb_qkv), 1) / gain1
    d_gain2 = jnp.sum(wide_up * (g_up - shift2[:, None] * gb_up), 1) / gain2
    d_shift1 = jnp.sum(wide_qkv * gb_qkv, 1)
    d_shift2 = jnp.sum(wide_up * gb_up, 1)
    full_qkv = lax.dynamic_update_slice(jnp.zeros((3, HEADS * HEAD), WIDE), gb_qkv.reshape(3, cols), (0, group * cols)).reshape(-1)
    full_up = lax.dynamic_update_slice(jnp.zeros((hidden_all,), WIDE), gb_up, (place * hid,))
    sums = lax.psum((full_qkv, jnp.sum(dy_own, 0, dtype=WIDE), full_up, d_gain1, d_shift1, d_gain2, d_shift2), PLANE + ("fsdp",))
    mine = lax.axis_index("fsdp")

    def own_share(values):
        size = values.shape[0] // shards
        return lax.dynamic_slice_in_dim(values, mine * size, size, 0)

    sums = [own_share(s) for s in sums]
    grads = jnp.concatenate([g_qkv, g_o, g_up, g_down], 1).astype(LOW)
    reduced = lax.psum_scatter(grads, "fsdp", scatter_dimension=0, tiled=True)
    gathered = lax.all_gather(reduced, PLANE, axis=0, tiled=False)
    rows_own = reduced.shape[0]

    def spread_heads(values, kinds):
        values = values.astype(WIDE).reshape(peers // share, share, rows_own, kinds, cols).sum(1)
        return values.transpose(1, 2, 0, 3).reshape(rows_own, kinds * HEADS * HEAD)

    def spread_hid(values):
        return values.transpose(1, 0, 2).reshape(rows_own, hidden_all).astype(WIDE)

    return (
        output,
        input_grad,
        spread_heads(gathered[:, :, : 3 * cols], 3),
        sums[0],
        spread_heads(gathered[:, :, 3 * cols : cut], 1),
        sums[1],
        spread_hid(gathered[:, :, cut : cut + hid]),
        sums[2],
        spread_hid(gathered[:, :, cut + hid :]),
        sums[1],
        sums[3],
        sums[4],
        sums[5],
        sums[6],
    )


MESH = pl.DeviceIdType.MESH
PIECES = 12
ROWS = 512
COLS = 256
WIDTH = 2048
TOK = 2048
OWN = 256
LENGTH = 1024
HOPS = 3
SLOTS = 36
RS_START = 17
RING = 6
HOLD = 4
LAST = RS_START + SLOTS + 7
SCALING = 1.0 / math.sqrt(HEAD)


def fits(mesh):
    return dict(mesh.shape) == {"seq": 2, "ctx": 4, "fsdp": 4}


def at(index, size):
    return pl.ds(pl.multiple_of(index * size, size), size)


def remote(source, target, sent, came, device):
    return pltpu.make_async_remote_copy(
        src_ref=source, dst_ref=target, send_sem=sent, recv_sem=came, device_id=device, device_id_type=MESH)


def layer_kernel(tokens, cotangent, w_qkv, w_o, w_up, w_down, vec_own, turns,
                 out, input_grad, small_out, gout, x_land, core_land, first_land, second_land,
                 w_all, act, x_buf, dy_buf, g_ring, landing, small, gb, tab, pos, rows, bias,
                 stage, vecs, places, pack, pack_z, pack_p, final,
                 load_sem, own_sem, ag_send, ag_recv, rs_send, rs_recv, red_sem, ga_send, ga_recv,
                 vec_send, vec_recv, pk_send, pk_recv, pp_send, pp_recv, core_send, core_recv, one_send, one_recv,
                 two_send, two_recv):
    y, c, z = lax.axis_index("seq"), lax.axis_index("ctx"), lax.axis_index("fsdp")
    core = lax.rem(c, 2)
    chip = c // 2
    place = y * 4 + c
    right, left = (y, c, jnp.minimum(z + 1, 3)), (y, c, jnp.maximum(z - 1, 0))
    c_x, c_core = lax.rem(c + 2, 4), c + 1 - 2 * core
    dev_x, dev_y, dev_c = (y, c_x, z), (1 - y, c, z), (y, c_core, z)
    place_x, place_y, place_d = y * 4 + c_x, (1 - y) * 4 + c, (1 - y) * 4 + c_x
    c_core_x = lax.rem(c_core + 2, 4)
    place_c, place_cx, place_cy, place_cd = y * 4 + c_core, y * 4 + c_core_x, (1 - y) * 4 + c_core, (1 - y) * 4 + c_core_x
    above = [(y, c, lax.rem(z + d, 4)) for d in (1, 2, 3)]
    beside = []
    for d in range(1, 8):
        other = lax.rem(place + d, 8)
        beside.append((other // 4, lax.rem(other, 4), z))
    lane = lax.broadcasted_iota(jnp.int32, (1, 128), 1)

    barrier = pltpu.get_barrier_semaphore()
    for device in above + beside:
        pl.semaphore_signal(barrier, inc=1, device_id=device, device_id_type=MESH)

    def own_piece(i):
        if i < 3:
            source = w_qkv.at[:, at(i * 8 + place, COLS)]
        elif i == 3:
            source = w_o.at[:, at(place, COLS)]
        else:
            source = (w_up if i % 2 == 0 else w_down).at[:, at(place * 4 + (i - 4) // 2, COLS)]
        return pltpu.make_async_copy(source, w_all.at[i, at(z, ROWS)], own_sem.at[i])

    loads = [
        pltpu.make_async_copy(cotangent.at[0], dy_buf.at[at(place, OWN)], load_sem.at[1]),
        pltpu.make_async_copy(vec_own, vecs.at[z], load_sem.at[2]),
        pltpu.make_async_copy(vec_own.at[pl.ds(8, 8)], places.at[y], load_sem.at[3]),
        pltpu.make_async_copy(turns, small.at[pl.ds(0, LENGTH)], load_sem.at[4]),
    ]
    for i in range(PIECES):
        own_piece(i).start()
    for load in loads:
        load.start()
    pl.semaphore_wait(barrier, 10)

    def gather(tag, source, target):
        def copy(k):
            sent, came = ga_send.at[tag, k], ga_recv.at[tag, k]
            if k == 0:
                return remote(source(0), target(place, 0), sent, came, dev_x)
            if k == 1:
                return remote(source(1), target(place, 1), sent, came, dev_x)
            if k == 2:
                return remote(source(1), target(place, 1), sent, came, dev_y)
            if k == 3:
                return remote(source(0), target(place, 0), sent, came, dev_y)
            if k == 4:
                return remote(source(None), target(place, None), sent, came, dev_c)
            if k == 5:
                return remote(target(place_x, 0), target(place_x, 0), sent, came, dev_y)
            if k == 6:
                return remote(target(place_y, 1), target(place_y, 1), sent, came, dev_x)
            which = (place_x, place_y, place_d)[k - 7]
            return remote(target(which, None), target(which, None), sent, came, dev_c)

        def arrived(k):
            spot = (
                (place_x, 0), (place_x, 1), (place_y, 1), (place_y, 0), (place_c, None),
                (place_d, 0), (place_d, 1), (place_cx, None), (place_cy, None), (place_cd, None),
            )[k]
            here = target(*spot)
            remote(here, here, ga_send.at[tag, k], ga_recv.at[tag, k], dev_c).wait_recv()

        def start():
            for k in (0, 2, 1, 3, 4):
                copy(k).start()

        def middle():
            arrived(0)
            copy(5).start()
            arrived(2)
            copy(6).start()

        def forward():
            arrived(1)
            copy(7).start()
            arrived(3)
            copy(8).start()

        def far():
            arrived(5)
            arrived(6)
            copy(9).start()

        def end():
            for k in (4, 7, 8, 9):
                arrived(k)
            for k in range(10):
                copy(k).wait_send()

        return start, middle, forward, far, end

    def half_of(ref, half, size):
        return ref if half is None else ref.at[pl.ds(half * size, size)]

    x_gather = gather(0, lambda half: half_of(tokens.at[0], half, 128), lambda who, half: half_of(x_land.at[who], half, 128))
    dy_gather = gather(
        1, lambda half: half_of(cotangent.at[0], half, 128),
        lambda who, half: dy_buf.at[at(who, OWN)] if half is None else dy_buf.at[at(who * 2 + half, 128)])
    x_gather[0]()

    def vec_copy(d):
        return remote(vec_own, vecs.at[z], vec_send.at[d], vec_recv.at[d], above[d])

    def place_copy():
        return remote(vec_own.at[pl.ds(8, 8)], places.at[y], vec_send.at[3], vec_recv.at[3], dev_y)

    for d in range(3):
        vec_copy(d).start()
    place_copy().start()
    for i in range(PIECES):
        own_piece(i).wait()

    def parts(s):
        return (s // 6) * 2 + s % 2, (s // 2) % 3

    def ag_copy(way, piece, hop, shard):
        block = w_all.at[piece, at(shard, ROWS)]
        return remote(block, block, ag_send.at[way, piece, hop], ag_recv.at[way, piece, hop], right if way == 0 else left)

    def ag_service(slot):
        before = slot - 2
        old, old_hop = parts(jnp.maximum(before, 0))
        live = (before >= 0) & (before < SLOTS)

        @pl.when(live & (z >= 1) & (z - 1 - old_hop >= 0))
        def _():
            ag_copy(0, old, old_hop, z - 1 - old_hop).wait_recv()

        @pl.when(live & (z <= 2) & (z + 1 + old_hop <= 3))
        def _():
            ag_copy(1, old, old_hop, z + 1 + old_hop).wait_recv()

        piece, hop = parts(jnp.minimum(slot, SLOTS - 1))
        later = (hop == 0) & (piece >= PIECES // 2)
        ahead = (slot < SLOTS // 2) & (hop == 2)

        @pl.when((slot < SLOTS) & (z <= 2) & (z - hop >= 0) & ~(later & (z <= 1)))
        def _():
            ag_copy(0, piece, hop, z - hop).start()

        @pl.when((slot < SLOTS) & (z >= 1) & (z + hop <= 3) & ~(later & (z >= 2)))
        def _():
            ag_copy(1, piece, hop, z + hop).start()

        @pl.when(ahead & (z <= 1))
        def _():
            ag_copy(0, piece + PIECES // 2, 0, z).start()

        @pl.when(ahead & (z >= 2))
        def _():
            ag_copy(1, piece + PIECES // 2, 0, z).start()

        @pl.when(live & (z <= 2) & (z - old_hop >= 0))
        def _():
            ag_copy(0, old, old_hop, z - old_hop).wait_send()

        @pl.when(live & (z >= 1) & (z + old_hop <= 3))
        def _():
            ag_copy(1, old, old_hop, z + old_hop).wait_send()

    def rs_piece(n):
        return jnp.where(n < 4, 3 - n, 4 + (n - 4) // 2 + 4 * (n % 2))

    def landing_slot(n, hop):
        return jnp.where(hop < 2, (n % 2) * 2 + hop, 4 + n % 4)

    def rs_copy(way, n, hop, shard):
        return remote(
            g_ring.at[n % RING, at(shard, ROWS)], landing.at[way, landing_slot(n, hop)],
            rs_send.at[way, n, hop], rs_recv.at[way, n, hop], right if way == 0 else left)

    def rs_add(way, n, hop, shard):
        rs_copy(way, n, hop, shard).wait_recv()
        block = g_ring.at[n % RING, at(shard, ROWS)]
        block[...] = (block[...].astype(WIDE) + landing[way, landing_slot(n, hop)].astype(WIDE)).astype(LOW)

    def held_copy(way, n):
        return remote(
            g_ring.at[n % RING, pl.ds((1 - way) * 3 * ROWS, ROWS)], landing.at[1 - way, n],
            rs_send.at[way, n, 2], rs_recv.at[way, n, 2], right if way == 0 else left)

    def held_add(way, n):
        held_copy(way, n).wait_recv()
        block = g_ring.at[n % RING, pl.ds((1 - way) * 3 * ROWS, ROWS)]
        block[...] = (block[...].astype(WIDE) + landing[1 - way, n].astype(WIDE)).astype(LOW)

    def red_copy(n):
        return pltpu.make_async_copy(g_ring.at[n % RING, at(z, ROWS)], gout.at[rs_piece(n), place], red_sem.at[n])

    def red_gather(n):
        piece = rs_piece(n)
        return gather(
            2 + n, lambda half: half_of(gout.at[piece, place], half, 256),
            lambda who, half: half_of(gout.at[piece, who], half, 256))

    def rs_service(slot):
        before = slot - 2
        old, old_hop = parts(jnp.clip(before, 0, SLOTS - 1))
        live = (before >= 0) & (before < SLOTS)
        ends = (z == 0) | (z == 3)
        old_held = (old >= HOLD) & (old < 6) & (old_hop == 2)
        held_sent, held_came = slot - 15, slot - 17
        send_held, take_held = (held_sent >= HOLD) & (held_sent < 6), (held_came >= HOLD) & (held_came < 6)

        @pl.when(live & (z >= 1) & (z - 1 <= old_hop) & ~(old_held & (z == 3)))
        def _():
            rs_add(0, old, old_hop, z + 2 - old_hop)

        @pl.when(live & (z <= 2) & (2 - z <= old_hop) & ~(old_held & (z == 0)))
        def _():
            rs_add(1, old, old_hop, z - 2 + old_hop)

        @pl.when(take_held & (z == 3))
        def _():
            held_add(0, held_came)

        @pl.when(take_held & (z == 0))
        def _():
            held_add(1, held_came)

        piece, hop = parts(jnp.clip(slot, 0, SLOTS - 1))
        sending = (slot >= 0) & (slot < SLOTS)
        held = (piece >= HOLD) & (piece < 6) & (hop == 2)

        @pl.when(send_held & (z == 2))
        def _():
            held_copy(0, held_sent).start()

        @pl.when(send_held & (z == 1))
        def _():
            held_copy(1, held_sent).start()

        @pl.when(sending & (z <= 2) & (z <= hop) & ~(held & (z == 2)))
        def _():
            rs_copy(0, piece, hop, z + 3 - hop).start()

        @pl.when(sending & (z >= 1) & (3 - z <= hop) & ~(held & (z == 1)))
        def _():
            rs_copy(1, piece, hop, z - 3 + hop).start()

        @pl.when(live & (z <= 2) & (z <= old_hop) & ~(old_held & (z == 2)))
        def _():
            rs_copy(0, old, old_hop, z + 3 - old_hop).wait_send()

        @pl.when(live & (z >= 1) & (3 - z <= old_hop) & ~(old_held & (z == 1)))
        def _():
            rs_copy(1, old, old_hop, z - 3 + old_hop).wait_send()

        @pl.when(take_held & (z == 2))
        def _():
            held_copy(0, held_came).wait_send()

        @pl.when(take_held & (z == 1))
        def _():
            held_copy(1, held_came).wait_send()

        ready = jnp.where(take_held, held_came, old)

        @pl.when((live & (old_hop == 2) & ~(old_held & ends)) | (take_held & ends))
        def _():
            red_copy(ready).start()
            red_copy(ready).wait()
            red_gather(ready)[0]()

        for step, delay in ((1, 1), (2, 2), (3, 3), (4, 5)):
            begun = slot - delay
            shifted = (begun >= 17 + HOLD) & (begun < 23)
            usual = (begun >= 6) & (begun < SLOTS + 6) & (begun % 6 < 2) & ~(ends & (begun // 2 == 9))
            n = jnp.where(shifted, begun - 17, jnp.clip((begun // 6) * 2 - 2 + begun % 6, 0, PIECES - 1))

            @pl.when(usual | (shifted & ends))
            def _(step=step, n=n):
                red_gather(n)[step]()

    def service(slot):
        if isinstance(slot, int):
            if slot < SLOTS + 2:
                ag_service(jnp.int32(slot))
            if slot >= RS_START:
                rs_service(jnp.int32(slot - RS_START))
        else:
            ag_service(slot)
            rs_service(slot - RS_START)

    def services(first, last, early=False):
        def step(slot, carry):
            ag_service(slot)
            if not early:
                rs_service(slot - RS_START)
            return carry

        lax.fori_loop(first, last, step, 0)

    def loop(count, body, first=None, ag=True, rs=True):
        def step(i, carry):
            if first is not None:
                if ag:
                    ag_service(first + i)
                if rs:
                    rs_service(first + i - RS_START)
            body(i)
            return carry

        lax.fori_loop(0, count, step, 0)

    services(0, 2, True)
    for load in loads[1:]:
        load.wait()
    for d in range(3):
        here = vecs.at[lax.rem(z + 3 - d, 4)]
        remote(here, here, vec_send.at[d], vec_recv.at[d], above[d]).wait_recv()
    other = places.at[1 - y]
    remote(other, other, vec_send.at[3], vec_recv.at[3], dev_y).wait_recv()
    for shard in range(4):
        here = pl.ds(shard * ROWS, ROWS)
        for k in range(4):
            rows[k : k + 1, here] = vecs[shard, 9 + k : 10 + k, :]
        rows[4:5, here] = vecs[shard, 3:4, :] + vecs[shard, 8:9, :]
        rows[5:8, here] = jnp.zeros((3, ROWS), WIDE)
    for kind in range(3):
        flat = kind * WIDTH + place * COLS
        bias[kind : kind + 1, :] = vecs[flat // 1536, pl.ds((flat % 1536) // 512, 1), at((flat % 512) // 256, COLS)]
    for part in range(4):
        flat = place * 1024 + part * COLS
        bias[3 + part : 4 + part, :] = vecs[flat // 2048, pl.ds(4 + (flat % 2048) // 512, 1), at((flat % 512) // 256, COLS)]

    def set_place(i, carry):
        seq, block = i // 8, i % 8
        value = jnp.sum(jnp.where(lane == block, places[seq, 5:6, 0:128], 0.0), 1, keepdims=True)
        made = jnp.zeros((BLK, 128), WIDE)
        for b in range(8):
            made = jnp.where(value == float(b), small[pl.ds(b * BLK, BLK), :], made)
        tab[at(i, BLK), :] = made
        pos[seq, :, at(block, BLK)] = jnp.broadcast_to(value * float(BLK) + lane.astype(WIDE), (8, BLK))
        return carry

    services(2, 3, True)
    lax.fori_loop(0, 16, set_place, 0)
    for shard in range(4):
        tall = jnp.concatenate([rows[:, pl.ds(shard * ROWS, ROWS)], jnp.zeros((120, ROWS), WIDE)], 0)
        small[pl.ds(shard * ROWS, ROWS), :] = jnp.transpose(tall)
    x_gather[1]()
    services(3, 5, True)
    x_gather[2]()
    dy_gather[0]()
    services(5, 7, True)
    x_gather[3]()
    services(7, 8, True)
    x_gather[4]()
    def norm_tile(which):
        def run(i):
            def part(n, carry):
                block = at(i * 4 + n, 64)
                centred, scale = standardise_rows(x_buf[block, :].astype(WIDE))
                x_buf[block, :] = (centred * scale * rows[2 * which : 2 * which + 1, :] + rows[2 * which + 1 : 2 * which + 2, :]).astype(LOW)
                return carry

            lax.fori_loop(0, 4, part, 0)
        return run

    def load_x():
        copies = [pltpu.make_async_copy(tokens.at[0], x_buf.at[at(place, OWN)], own_sem.at[0])]
        for d in range(1, 8):
            other = lax.rem(place + d, 8)
            copies.append(pltpu.make_async_copy(x_land.at[other], x_buf.at[at(other, OWN)], own_sem.at[d]))
        for copy in copies:
            copy.start()
        for copy in copies:
            copy.wait()

    def norm(which, first, rs):
        load_x()

        def body(i):
            for n in range(4):
                norm_tile(which)(4 * i + n)

        loop(2, body, first, rs=rs)

    norm(0, 8, False)
    dy_gather[1]()

    def turned(values, block, sign):
        entry = tab[block, :]
        cosine = jnp.where(lane < 32, entry, jnp.where(lane < 64, pltpu.roll(entry, 32, 1), 1.0))
        sine = jnp.where(lane < 32, -pltpu.roll(entry, 96, 1), jnp.where(lane < 64, entry, 0.0))
        low = values[:, :128]
        partner = jnp.where(lane < 32, pltpu.roll(low, 96, 1), pltpu.roll(low, 32, 1))
        return jnp.concatenate([low * cosine + partner * (sine * sign), values[:, 128:]], 1)

    def project(kind):
        def run(i):
            block = at(i, 512)
            made = dot_nn(x_buf[block, :], w_all[kind]) + bias[kind : kind + 1, :]
            if kind < 2:
                made = turned(made, block, 1.0)
            if kind == 0:
                made = made * SCALING
            act[9 + kind, block, :] = made.astype(LOW)
        return run

    services(10, 11, True)
    loop(4, project(0))
    dy_gather[2]()
    services(11, 12, True)
    loop(4, project(1))
    services(12, 13, True)
    loop(4, project(2))
    dy_gather[3]()
    dy_gather[4]()
    loads[0].wait()

    def attend(i):
        seq = i // 4
        block, keys = at(i, 256), at(seq, LENGTH)

        q, k, v = act[9, block, :], act[10, keys, :], act[11, keys, :]
        kept = tab[block, 64:65] >= pos[seq, 0:1, :]
        scores = jnp.where(kept, dot_nt(q, k), -1e30)
        expo = jnp.exp(scores - jnp.max(scores, -1, keepdims=True))
        p = expo * (1.0 / jnp.sum(expo, -1, keepdims=True))
        p_low = p.astype(LOW)
        act[3, block, :] = dot_nn(p_low, v).astype(LOW)
        d_attn = dot_nn(dy_buf[block, :], w_all[3]).astype(LOW)
        dp = dot_nt(d_attn, v)
        ds = jnp.where(kept, p * (dp - jnp.sum(p * dp, -1, keepdims=True)), 0.0).astype(LOW)
        act[0, block, :] = turned(dot_nn(ds, k) * SCALING, block, -1.0).astype(LOW)
        act[8, block, :] = d_attn
        for n in range(4):
            g_ring[n, at(i % 4, 256), :] = ds[:, n * COLS : (n + 1) * COLS]
            g_ring[n, at(4 + i % 4, 256), :] = p_low[:, n * COLS : (n + 1) * COLS]

        @pl.when(i % 4 == 3)
        def _():
            def keyed(n, carry):
                mine = at(seq * 4 + n, COLS)
                d_keys = dot_tn(g_ring[n, 0:LENGTH, :], act[9, keys, :])
                act[1, mine, :] = turned(d_keys, mine, -1.0).astype(LOW)
                act[2, mine, :] = dot_tn(g_ring[n, LENGTH:, :], act[8, keys, :]).astype(LOW)
                return carry

            lax.fori_loop(0, 4, keyed, 0)

    def attend_two(i):
        def inner(n, carry):
            attend(2 * i + n)
            return carry

        lax.fori_loop(0, 2, inner, 0, unroll=True)

    loop(4, attend_two, 13, rs=False)

    def gradient(piece, n, source):
        summed = piece < 3 or (piece != 3 and piece % 2 == 0)
        if summed:
            gb[piece : piece + 1, :] = jnp.zeros((1, COLS), WIDE)

            def count(i, carry):
                gb[piece : piece + 1, :] += jnp.sum(act[piece, at(i, 256), :].astype(WIDE), 0, keepdims=True)
                return carry

            lax.fori_loop(0, 8, count, 0)

        def part(s, carry):
            block = at(s, ROWS)
            made = dot_tn(source[:, block], act[piece])
            g_ring[n % RING, block, :] = made.astype(LOW)
            if summed:
                mine = 0 if piece < 3 else 1
                weight = w_all[piece, block, :].astype(WIDE)
                sums = gb[piece : piece + 1, :]
                gain = jnp.sum(weight * (made - small[block, 2 * mine + 1 : 2 * mine + 2] * sums), 1, keepdims=True)
                shift = jnp.sum(weight * sums, 1, keepdims=True)
                here = 8 + 2 * mine
                old = small[block, :]
                small[block, :] = old + jnp.where(lane == here, gain, 0.0) + jnp.where(lane == here + 1, shift, 0.0)
            return carry

        lax.fori_loop(0, 4, part, 0)

    rows[5:6, :] = jnp.sum(dy_buf[at(place, OWN), :].astype(WIDE), 0, keepdims=True)
    gradient(3, 0, dy_buf)
    service(17)
    gradient(2, 1, x_buf)
    service(18)
    gradient(1, 2, x_buf)
    service(19)
    gradient(0, 3, x_buf)
    service(20)
    norm(1, 21, True)

    def feed(part):
        up, down = 4 + 2 * part, 5 + 2 * part

        def run(i):
            for n in range(2):
                block = at(2 * i + n, 512)
                hidden = dot_nn(x_buf[block, :], w_all[up]) + bias[3 + part : 4 + part, :]
                d_gelu = dot_nn(dy_buf[block, :], w_all[down])
                made, slope = gelu_pair(hidden)
                act[down, block, :] = made.astype(LOW)
                act[up, block, :] = (d_gelu * slope).astype(LOW)
        return run

    slot = 23
    for part in range(3):
        loop(2, feed(part), slot)
        slot += 2
        gradient(4 + 2 * part, 4 + 2 * part, x_buf)
        service(slot)
        gradient(5 + 2 * part, 5 + 2 * part, dy_buf)
        service(slot + 1)
        slot += 2
    services(35, 38)
    service(38)
    loop(2, feed(3))
    gradient(10, 10, x_buf)
    service(39)

    def make_pack():
        for shard in range(4):
            here = pl.ds(shard * ROWS, ROWS)
            flat = jnp.transpose(small[here, :])
            pack[shard, 0:1, :] = flat[8:9] / rows[0:1, here]
            pack[shard, 1:2, :] = flat[9:10]
            pack[shard, 2:3, :] = flat[10:11] / rows[2:3, here]
            pack[shard, 3:4, :] = flat[11:12]
            pack[shard, 4:5, :] = rows[5:6, here]
            pack[shard, 5:8, :] = jnp.zeros((3, ROWS), WIDE)
            pack[shard, 8:16, :] = jnp.zeros((8, ROWS), WIDE)
            for kind in range(3):
                pack[shard, 8 + kind : 9 + kind, :COLS] = gb[kind : kind + 1, :]
            for part in range(4):
                pack[shard, 11 + part : 12 + part, :COLS] = gb[4 + 2 * part : 5 + 2 * part, :]
        pack_z[z] = pack[z]

    def pack_copy(d):
        return remote(pack.at[lax.rem(z + d + 1, 4)], pack_z.at[z], pk_send.at[d], pk_recv.at[d], above[d])

    def peer_copy(d):
        return remote(pack_p.at[place], pack_p.at[place], pp_send.at[d], pp_recv.at[d], beside[d])

    def sum_start():
        for d in range(3):
            pack_copy(d).start()

    def sum_z():
        for d in range(3):
            here = pack_z.at[lax.rem(z + 3 - d, 4)]
            remote(here, here, pk_send.at[d], pk_recv.at[d], above[d]).wait_recv()
        pack_p[place] = pack_z[0] + pack_z[1] + pack_z[2] + pack_z[3]
        for d in range(7):
            peer_copy(d).start()

    def sum_plane():
        for d in range(7):
            here = pack_p.at[lax.rem(place + 7 - d, 8)]
            remote(here, here, pp_send.at[d], pp_recv.at[d], beside[d]).wait_recv()
        total = pack_p[0, 0:8, :]
        for p in range(1, 8):
            total = total + pack_p[p, 0:8, :]
        final[:, 0:ROWS] = total
        final[:, ROWS:] = jnp.zeros((8, 2 * COLS), WIDE)
        for r in range(6):
            flat = 6 * z + r
            final[r : r + 1, ROWS : ROWS + COLS] = pack_p[flat % 8, pl.ds(8 + flat // 8, 1), 0:COLS]
        for r in range(8):
            final[r : r + 1, ROWS + COLS :] = pack_p[2 * z + r // 4, 11 + r % 4 : 12 + r % 4, 0:COLS]

    tiles = {"d": (1 - y) * 2 + 1 - chip, "x": y * 2 + 1 - chip, "y": (1 - y) * 2 + chip, "own": y * 2 + chip}
    order = ("d", "x", "y", "own")
    both = (x_buf, dy_buf)

    def finish(name, whose, a):
        block = block_of(name, whose)

        def run(i, carry):
            columns = at(i, 512)

            def total(pieces):
                return sum(dot_nt(act[piece, block, :], w_all[piece, columns, :]) for piece in pieces)

            if a == 0:
                x_buf[block, columns] = total((3, 5, 7, 9, 11)).astype(LOW)
            else:
                first = total((0, 1, 2)) * rows[0:1, columns]
                dy_buf[block, columns] = (first + total((4, 6, 8, 10)) * rows[2:3, columns]).astype(LOW)
            return carry

        lax.fori_loop(0, 4, run, 0)

    def block_of(name, whose):
        return at(tiles[name] * 2 + whose, OWN)

    def half_rows(name, half):
        return at(tiles[name] * 4 + core * 2 + half, 128)

    def core_copy(name, a):
        i = order.index(name)
        return remote(both[a].at[block_of(name, 1 - core)], core_land.at[i, a], core_send.at[i, a], core_recv.at[i, a], dev_c)

    def first_copy(i, a):
        name, half, device = (("d", 0, dev_x), ("d", 1, dev_y), ("x", 0, dev_x), ("y", 1, dev_y))[i]
        return remote(both[a].at[half_rows(name, half)], first_land.at[i, a], one_send.at[i, a], one_recv.at[i, a], device)

    def second_copy(i, a):
        name, half, device = (("y", 0, dev_y), ("x", 1, dev_x))[i]
        return remote(both[a].at[half_rows(name, half)], second_land.at[i, a], two_send.at[i, a], two_recv.at[i, a], device)

    def fetch(source, a):
        return pltpu.make_async_copy(source, stage.at[a], load_sem.at[a])

    def add_in(copy, source, spots, a):
        copy.wait_recv()
        for half, spot in enumerate(spots):
            fetch(source.at[pl.ds(half * 128, 128)], a).start()
            fetch(source.at[pl.ds(half * 128, 128)], a).wait()
            both[a][spot, :] = (both[a][spot, :].astype(WIDE) + stage[a].astype(WIDE)).astype(LOW)

    def core_add(name, a):
        i = order.index(name)
        add_in(core_copy(name, a), core_land.at[i, a], [half_rows(name, 0), half_rows(name, 1)], a)

    def first_add(i, a):
        name, half = (("y", 0), ("x", 1), ("own", 0), ("own", 1))[i]
        add_in(first_copy(i, a), first_land.at[i, a], [half_rows(name, half)], a)

    def second_add(i, a):
        add_in(second_copy(i, a), second_land.at[i, a], [half_rows("own", i)], a)

    def pass_on(a):
        for i in range(2):
            first_add(i, a)
            second_copy(i, a).start()

    def spread(a, slots):
        for i, name in enumerate(order):
            finish(name, 1 - core, a)
            core_copy(name, a).start()
            if i == 1:
                core_add("d", a)
                first_copy(0, a).start()
                first_copy(1, a).start()
            elif i > 1:
                core_add(order[i - 1], a)
                first_copy(i, a).start()
            finish(name, core, a)
            if slots[i] is not None:
                service(slots[i])

    spread(0, (40, None, 41, None))
    gradient(11, 11, dy_buf)
    service(42)
    make_pack()
    sum_start()
    core_add("own", 0)
    spread(1, (43, None, 44, 45))
    core_add("own", 1)
    pass_on(0)
    sum_z()
    services(46, 48)
    first_add(2, 0)
    first_add(3, 0)
    services(48, 50)
    pass_on(1)
    services(50, 53)
    sum_plane()
    second_add(0, 0)
    second_add(1, 0)
    first_add(2, 1)
    first_add(3, 1)
    services(53, 56)
    second_add(0, 1)
    second_add(1, 1)

    for half in range(2):
        given = [tokens.at[0, pl.ds(half * 128, 128)], cotangent.at[0, pl.ds(half * 128, 128)]]
        for a in range(2):
            fetch(given[a], a).start()
        for a in range(2):
            fetch(given[a], a).wait()

        def emit(i, carry, half=half):
            here, mine = at(i, 64), at(place * 4 + half * 2 + i, 64)
            inputs = stage[0, here, :].astype(WIDE)
            x_buf[mine, :] = (inputs + x_buf[mine, :].astype(WIDE) + rows[4:5, :]).astype(LOW)
            centred, scale = standardise_rows(inputs)
            hat = centred * scale
            u = dy_buf[mine, :].astype(WIDE)
            inner = jnp.mean(u * hat, -1, keepdims=True)
            d_x = scale * (u - jnp.mean(u, -1, keepdims=True) - hat * inner)
            dy_buf[mine, :] = (stage[1, here, :].astype(WIDE) + d_x).astype(LOW)
            return carry

        lax.fori_loop(0, 2, emit, 0)
    ends = [
        pltpu.make_async_copy(x_buf.at[at(place, OWN)], out, load_sem.at[0]),
        pltpu.make_async_copy(dy_buf.at[at(place, OWN)], input_grad, load_sem.at[1]),
        pltpu.make_async_copy(final, small_out, load_sem.at[2]),
    ]
    for end in ends:
        end.start()
    services(56, LAST)
    for end in ends:
        end.wait()
    for d in range(3):
        vec_copy(d).wait_send()
        pack_copy(d).wait_send()
    place_copy().wait_send()
    for d in range(7):
        peer_copy(d).wait_send()
    for a in range(2):
        for name in order:
            core_copy(name, a).wait_send()
        for i in range(4):
            first_copy(i, a).wait_send()
        for i in range(2):
            second_copy(i, a).wait_send()


def standardise_rows(values):
    middle = jnp.mean(values, -1, keepdims=True)
    centred = values - middle
    spread = jnp.mean(centred * centred, -1, keepdims=True)
    return centred, lax.rsqrt(spread + EPS)


def layer_call(*operands):
    anywhere = pl.BlockSpec(memory_space=pltpu.HBM)
    shape = jax.ShapeDtypeStruct
    dma = pltpu.SemaphoreType.DMA
    out_shape = (
        shape((OWN, WIDTH), LOW),
        shape((OWN, WIDTH), LOW),
        shape((8, 1024), WIDE),
        shape((PIECES, 8, ROWS, COLS), LOW),
        shape((8, OWN, WIDTH), LOW),
        shape((4, 2, OWN, WIDTH), LOW),
        shape((4, 2, 128, WIDTH), LOW),
        shape((2, 2, 128, WIDTH), LOW),
    )
    return pl.pallas_call(
        layer_kernel,
        out_shape=out_shape,
        in_specs=[anywhere] * len(operands),
        out_specs=[anywhere] * len(out_shape),
        scratch_shapes=[
            pltpu.VMEM((PIECES, WIDTH, COLS), LOW),
            pltpu.VMEM((PIECES, TOK, COLS), LOW),
            pltpu.VMEM((TOK, WIDTH), LOW),
            pltpu.VMEM((TOK, WIDTH), LOW),
            pltpu.VMEM((RING, WIDTH, COLS), LOW),
            pltpu.VMEM((2, 8, ROWS, COLS), LOW),
            pltpu.VMEM((WIDTH, 128), WIDE),
            pltpu.VMEM((16, COLS), WIDE),
            pltpu.VMEM((TOK, 128), WIDE),
            pltpu.VMEM((2, 8, LENGTH), WIDE),
            pltpu.VMEM((8, WIDTH), WIDE),
            pltpu.VMEM((8, COLS), WIDE),
            pltpu.VMEM((2, 128, WIDTH), LOW),
            pltpu.VMEM((4, 16, ROWS), WIDE),
            pltpu.VMEM((2, 8, ROWS), WIDE),
            pltpu.VMEM((4, 16, ROWS), WIDE),
            pltpu.VMEM((4, 16, ROWS), WIDE),
            pltpu.VMEM((8, 16, ROWS), WIDE),
            pltpu.VMEM((8, 1024), WIDE),
            dma((5,)),
            dma((PIECES,)),
            dma((2, PIECES, HOPS)),
            dma((2, PIECES, HOPS)),
            dma((2, PIECES, HOPS)),
            dma((2, PIECES, HOPS)),
            dma((PIECES,)),
            dma((2 + PIECES, 10)),
            dma((2 + PIECES, 10)),
            dma((4,)),
            dma((4,)),
            dma((3,)),
            dma((3,)),
            dma((7,)),
            dma((7,)),
            dma((4, 2)),
            dma((4, 2)),
            dma((4, 2)),
            dma((4, 2)),
            dma((2, 2)),
            dma((2, 2)),
        ],
        compiler_params=pltpu.CompilerParams(collective_id=0, has_side_effects=True, vmem_limit_bytes=61 * 1024 * 1024),
    )(*operands)


DEPTH = 8


def widen_kernel(gathered, made, made_grad, g_qkv, g_o, g_up, g_down, output, input_grad, low, wide, held, low_sem, wide_sem, pass_sem):
    brought = [pltpu.make_async_copy(made, held.at[0], pass_sem.at[0]), pltpu.make_async_copy(made_grad, held.at[1], pass_sem.at[1])]
    passing = [pltpu.make_async_copy(held.at[0], output, pass_sem.at[0]), pltpu.make_async_copy(held.at[1], input_grad, pass_sem.at[1])]
    for copy in brought:
        copy.start()

    def load(i):
        return pltpu.make_async_copy(gathered.at[i // 8, i % 8], low.at[i % DEPTH], low_sem.at[i % DEPTH])

    def store(i, act):
        piece, p = i // 8, i % 8

        def copy(target):
            act(pltpu.make_async_copy(wide.at[i % DEPTH], target, wide_sem.at[i % DEPTH]))

        @pl.when(piece < 3)
        def _():
            copy(g_qkv.at[:, at(jnp.minimum(i, 23), COLS)])

        @pl.when(piece == 3)
        def _():
            copy(g_o.at[:, at(p, COLS)])

        @pl.when((piece >= 4) & (piece < 8))
        def _():
            copy(g_up.at[:, at(p * 4 + jnp.clip(piece - 4, 0, 3), COLS)])

        @pl.when(piece >= 8)
        def _():
            copy(g_down.at[:, at(p * 4 + jnp.clip(piece - 8, 0, 3), COLS)])

    def first(i, carry):
        load(i).start()
        return carry

    def step(i, carry):
        load(i).wait()

        @pl.when(i >= DEPTH)
        def _():
            store(i - DEPTH, lambda copy: copy.wait())

        wide[i % DEPTH] = low[i % DEPTH].astype(WIDE)
        store(i, lambda copy: copy.start())

        @pl.when(i + DEPTH < 96)
        def _():
            load(i + DEPTH).start()

        return carry

    def last(i, carry):
        store(i, lambda copy: copy.wait())
        return carry

    lax.fori_loop(0, DEPTH, first, 0)
    lax.fori_loop(0, 16, step, 0)
    for copy in brought:
        copy.wait()
    for copy in passing:
        copy.start()
    lax.fori_loop(16, 96, step, 0)
    lax.fori_loop(96 - DEPTH, 96, last, 0)
    for copy in passing:
        copy.wait()


def widen(gathered, made, made_grad):
    shape = jax.ShapeDtypeStruct
    anywhere = pl.BlockSpec(memory_space=pltpu.HBM)
    return pl.pallas_call(
        widen_kernel,
        in_specs=[anywhere] * 3,
        out_specs=[anywhere] * 6,
        out_shape=(shape((ROWS, 3 * WIDTH), WIDE), shape((ROWS, WIDTH), WIDE), shape((ROWS, 4 * WIDTH), WIDE), shape((ROWS, 4 * WIDTH), WIDE), shape(made.shape, LOW), shape(made.shape, LOW)),
        scratch_shapes=[
            pltpu.VMEM((DEPTH, ROWS, COLS), LOW),
            pltpu.VMEM((DEPTH, ROWS, COLS), WIDE),
            pltpu.VMEM((2, OWN, WIDTH), LOW),
            pltpu.SemaphoreType.DMA((DEPTH,)),
            pltpu.SemaphoreType.DMA((DEPTH,)),
            pltpu.SemaphoreType.DMA((2,)),
        ],
        compiler_params=pltpu.CompilerParams(vmem_limit_bytes=56 * 1024 * 1024),
    )(gathered, made, made_grad)


def turn_table():
    where = np.arange(LENGTH, dtype=np.float32)[:, None]
    freqs = np.float32(10000.0) ** (-(np.arange(ROT // 2, dtype=np.float32) * np.float32(2.0 / ROT)))
    turned = (where * freqs[None, :]).astype(np.float32)
    return np.concatenate([np.cos(turned), np.sin(turned), np.broadcast_to(where, (LENGTH, 64))], 1).astype(np.float32)


def fused_body(tokens, block_place, w_qkv, b_qkv, w_o_t, b_o, w_up, b_up, w_down_t, b_down,
               norm1_gain, norm1_shift, norm2_gain, norm2_shift, cotangent):
    given = (b_qkv, b_o, b_up, b_down, norm1_gain, norm1_shift, norm2_gain, norm2_shift)
    spots = block_place.astype(WIDE).reshape(-1)
    vec, start = jnp.zeros((16 * ROWS,), WIDE), 0
    for part in given + (spots,):
        vec = vec + jnp.pad(part.astype(WIDE), (start, 16 * ROWS - start - part.shape[0]))
        start += part.shape[0]
    vec = vec.reshape(16, ROWS)
    turns = jnp.asarray(turn_table())
    results = layer_call(tokens, cotangent, w_qkv, w_o_t, w_up, w_down_t, vec, turns)
    made, made_grad, sums, gathered = results[:4]
    g_qkv, g_o, g_up, g_down, output, input_grad = widen(gathered, made, made_grad)
    grad_bias = sums[4, :ROWS]
    return (
        output[None],
        input_grad[None],
        g_qkv,
        sums[:6, ROWS : ROWS + COLS].reshape(-1),
        g_o,
        grad_bias,
        g_up,
        sums[:, ROWS + COLS :].reshape(-1),
        g_down,
        grad_bias,
        sums[0, :ROWS],
        sums[1, :ROWS],
        sums[2, :ROWS],
        sums[3, :ROWS],
    )


def solution(mesh):
    tok = P(("seq", "fsdp"), "ctx", None)
    mat, vec = P("fsdp", None), P("fsdp")
    params = (mat, vec, mat, vec, mat, vec, mat, vec, vec, vec, vec, vec)
    in_specs = (tok, P(("seq", "fsdp"), None)) + params + (tok,)
    return jax.shard_map(fused_body if fits(mesh) else body, mesh=mesh, in_specs=in_specs, out_specs=(tok, tok) + params, check_vma=False)
```
